512 devices in a mesh: outer: 8 (over z_hi, x), inner: 64 (over y, z_lo, core).
Axes of the slice: x: 4, y: 8, z: 8 (z_hi: 2, z_lo: 4; z = z_hi * 4 + z_lo), core: 2. Of those that a mesh axis runs over, the one named last changes fastest.
Arguments:
- positions: float32 [3, 262144], P(None, ('outer', 'inner')), may hold values from 0 to 3.4
- species: int32 [262144], P(('outer', 'inner')), may hold values from 0 to 6
- send_lists: int32 [8, 90112], P(None, ('outer', 'inner')), may hold values from 0 to 511, as said below
- centers: int32 [393216], P(('outer', 'inner')), may hold values from 0 to 511
- neighbours: int32 [393216], P(('outer', 'inner')), may hold values from 0 to 1919, as said below
- live_blocks: int32 [512], P(('outer', 'inner')), may hold values from 1 to 6
- w_rad: float32 [8, 128], replicated, may hold values from -2 to 2
- emb_center: bfloat16 [7, 128], replicated, may hold values from -5 to 5
- emb_neigh: bfloat16 [7, 128], replicated, may hold values from -5 to 5
- w_env: bfloat16 [128, 192], replicated, may hold values from -0.5 to 0.5
- w_lat: bfloat16 [320, 128], replicated, may hold values from -0.3125 to 0.3125
- w_out: bfloat16 [128], replicated, may hold values from -0.5 to 0.5
Outputs:
- forces: float32 [3, 262144], P(None, ('outer', 'inner'))
- atom_energy: float32 [262144], P(('outer', 'inner'))
The draws below stay inside these ranges and needn't reach their ends.
Inputs may be any that keep to these rules, and one draw needn't show every extreme that they name: `neighbours`: within the 768 pair slots of one domain no two share a neighbour index; values below 512 are local atoms, value 512 + k * 176 + s is entry s of ghost direction k. `send_lists`: each send list of one domain and one direction names 176 distinct local atoms.
All inputs are finite; a program needn't handle non-finite values.
Results may differ from the reference program's by a relative error of at most 0.013.
Values sent between devices are 32-bit elements; how exact they have to be, the bound alone decides.
No kernel may reach another device: no remote copies, remote signals or barrier semaphores. Data moves between devices by JAX's collectives and lax.ppermute only.
A program may use at most 64 MiB of HBM per device.

```python
import math
import jax
import jax.numpy as jnp
from jax import lax

FEAT = 64
LAT = 128
NBASIS = 8
NSPEC = 7
ATOM_DEV = 512
SEND = 176
NBLK = 6
PAIR_DEV = 768
ATOMS = 262144
PAIRS = 393216
SENDS = 90112
N_OUTER = 8
N_INNER = 64


def draw_neighbours(key, part):
    key = jax.random.fold_in(key, 7)
    domains = PAIRS // PAIR_DEV
    subkeys = jax.random.split(key, domains)

    def permuted(subkey):
        return jax.random.permutation(subkey, ATOM_DEV + 8 * SEND)[:PAIR_DEV]
    return jax.vmap(permuted)(subkeys).reshape(-1).astype(jnp.int32)


def draw_send_lists(key, part):
    key = jax.random.fold_in(key, 11)
    domains = SENDS // SEND
    subkeys = jax.random.split(key, 8 * domains)

    def chosen(subkey):
        return jax.random.permutation(subkey, ATOM_DEV)[:SEND]
    return jax.vmap(chosen)(subkeys).reshape(8, SENDS).astype(jnp.int32)


def place_ends(array, own_key, low, high):
    shape = array.shape
    place = [jax.random.randint(jax.random.fold_in(own_key, axis), (), 0, shape[axis]) for axis in range(len(shape))]
    array = array.at[tuple(place)].set(low)
    longest = shape.index(max(shape))
    place[longest] = (place[longest] + 1) % shape[longest]
    return array.at[tuple(place)].set(high)


def block_levels(stream_key, extent, shards, smallest, largest):
    def one(axis_at, shards_of):
        heights = jax.random.uniform(jax.random.fold_in(jax.random.fold_in(stream_key, 6), axis_at), (shards_of,), jnp.float32, smallest / len(shards), largest / len(shards))
        return jnp.repeat(jnp.exp(heights), extent[axis_at] // shards_of).reshape((-1,) + (1,) * (len(extent) - axis_at - 1))

    factor_of = one(*shards[0])
    for cut in shards[1:]:
        factor_of = factor_of * one(*cut)
    return factor_of


def scatter_about(own_key, dims, scale, bound, kind=jnp.bfloat16):
    return jnp.clip(scale * jax.random.normal(own_key, dims, jnp.float32), -bound, bound).astype(kind)


def setup_inputs(seed: int = 0) -> dict:
    splits = jax.random.split(jax.random.key(seed), 13)
    positions = jnp.clip(3.4 * jax.random.uniform(splits[0], (3, ATOMS), jnp.float32) ** block_levels(splits[0], (3, ATOMS), ((1, 512),), -0.2, 0.2), 0.0, 3.4)
    species = place_ends(jax.random.randint(splits[1], (ATOMS,), 0, NSPEC), jax.random.fold_in(splits[1], 1), 0, NSPEC - 1).astype(jnp.int32)
    send_lists = draw_send_lists(jax.random.fold_in(splits[12], 71), 0)
    centers = place_ends(jax.random.randint(splits[3], (PAIRS,), 0, ATOM_DEV), jax.random.fold_in(splits[3], 1), 0, ATOM_DEV - 1).astype(jnp.int32)
    neighbours = draw_neighbours(jax.random.fold_in(splits[12], 71), 0)
    live_blocks = place_ends(jax.random.randint(splits[5], (N_OUTER * N_INNER,), max(1, NBLK // 8), NBLK + 1), jax.random.fold_in(splits[5], 1), max(1, NBLK // 8), NBLK).astype(jnp.int32)
    w_rad = scatter_about(splits[6], (NBASIS, LAT), NBASIS ** -0.5, 2.0, jnp.float32)
    emb_center = scatter_about(splits[7], (NSPEC, LAT), 1.0, 5.0)
    emb_neigh = scatter_about(splits[8], (NSPEC, LAT), 1.0, 5.0)
    w_env = scatter_about(splits[9], (LAT, 3 * FEAT), LAT ** -0.5, 0.5)
    w_lat = scatter_about(splits[10], (LAT + 3 * FEAT, LAT), (LAT + 3 * FEAT) ** -0.5, 0.3125)
    w_out = scatter_about(splits[11], (LAT,), LAT ** -0.5, 0.5)
    return {"positions": positions, "species": species, "send_lists": send_lists, "centers": centers, "neighbours": neighbours, "live_blocks": live_blocks, "w_rad": w_rad, "emb_center": emb_center, "emb_neigh": emb_neigh, "w_env": w_env, "w_lat": w_lat, "w_out": w_out}


DIRS = ((-1, -1), (-1, 0), (-1, 1), (0, -1), (0, 1), (1, -1), (1, 0), (1, 1))
CUTOFF = 6.0
TP_SCALE = 2.0
ROOT3 = math.sqrt(3.0)
ROOT5 = math.sqrt(5.0)
ROOT15 = math.sqrt(15.0)

def harmonics(unit_vec):
    comp_x, comp_y, comp_z = (unit_vec[0], unit_vec[1], unit_vec[2])
    length_sq = comp_x * comp_x + comp_y * comp_y + comp_z * comp_z
    return jnp.stack([jnp.ones_like(comp_x), ROOT3 * comp_x, ROOT3 * comp_y, ROOT3 * comp_z, ROOT15 * comp_x * comp_y, ROOT15 * comp_y * comp_z, 0.5 * ROOT5 * (3.0 * comp_z * comp_z - length_sq), ROOT15 * comp_x * comp_z, 0.5 * ROOT15 * (comp_x * comp_x - comp_y * comp_y)], 0)

def pair_front(displace, onehot_center, onehot_neigh, live_mask, w_rad, emb_center, emb_neigh, w_env):
    squared = lax.optimization_barrier(jnp.sum(displace * displace, axis=0)) + 1.0
    distance = jnp.sqrt(squared)
    unit_vec = displace / distance
    envelope = (1.0 - squared / (CUTOFF * CUTOFF)) ** 2
    orders = jnp.arange(1, w_rad.shape[0] + 1).astype(jnp.float32)
    basis = jnp.sin(orders[:, None] * distance[None, :] * (math.pi / CUTOFF)) / distance * envelope
    preact = jnp.dot(basis.T, w_rad, precision=lax.Precision.HIGHEST)
    preact = preact + jnp.dot(onehot_center, emb_center, preferred_element_type=jnp.float32)
    preact = preact + jnp.dot(onehot_neigh, emb_neigh, preferred_element_type=jnp.float32)
    latent = jax.nn.silu(preact)
    latent_half = latent.astype(jnp.bfloat16)
    scaled = envelope * live_mask
    env_weight = jnp.dot(latent_half, w_env, preferred_element_type=jnp.float32) * scaled[:, None]
    return (latent, latent_half, env_weight, harmonics(unit_vec), scaled)

def spread(env_weight, harmonic):
    feat = env_weight.shape[1] // 3
    rows = harmonic.T
    pieces = [env_weight[:, 0:feat][:, None, :] * rows[:, 0:1, None], env_weight[:, feat:2 * feat][:, None, :] * rows[:, 1:4, None], env_weight[:, 2 * feat:][:, None, :] * rows[:, 4:9, None]]
    return jnp.concatenate(pieces, axis=1).reshape(rows.shape[0], 9 * feat)

def pair_energy(displace, gathered, onehot_center, onehot_neigh, live_mask, w_rad, emb_center, emb_neigh, w_env, w_lat, w_out):
    latent, latent_half, env_weight, harmonic, scaled = pair_front(displace, onehot_center, onehot_neigh, live_mask, w_rad, emb_center, emb_neigh, w_env)
    feat = env_weight.shape[1] // 3
    rows = harmonic.T
    mixed = gathered.reshape(rows.shape[0], 9, feat) * rows[:, :, None]
    invariant = jnp.concatenate([lax.optimization_barrier(jnp.sum(mixed[:, 0:1], axis=1)), lax.optimization_barrier(jnp.sum(mixed[:, 1:4], axis=1)), lax.optimization_barrier(jnp.sum(mixed[:, 4:9], axis=1))], axis=1) * env_weight * TP_SCALE
    joined = jnp.concatenate([latent_half, invariant.astype(jnp.bfloat16)], axis=1)
    update = jax.nn.silu(jnp.dot(joined, w_lat, preferred_element_type=jnp.float32))
    refined = (latent + update).astype(jnp.bfloat16)
    return scaled * jnp.dot(refined, w_out, preferred_element_type=jnp.float32)

def device_terms(comb_pos, comb_spec, center_ids, neighbour_ids, live_mask, w_rad, emb_center, emb_neigh, w_env, w_lat, w_out):
    kinds = jnp.arange(emb_center.shape[0]).astype(jnp.int32)
    onehot_center = (comb_spec[center_ids][:, None] == kinds[None, :]).astype(jnp.bfloat16)
    onehot_neigh = (comb_spec[neighbour_ids][:, None] == kinds[None, :]).astype(jnp.bfloat16)
    displace = comb_pos[:, neighbour_ids] - comb_pos[:, center_ids]

    def contrib(moved):
        _, _, env_weight, harmonic, _ = pair_front(moved, onehot_center, onehot_neigh, live_mask, w_rad, emb_center, emb_neigh, w_env)
        return spread(env_weight, harmonic)

    def energy_of(moved, gathered):
        return pair_energy(moved, gathered, onehot_center, onehot_neigh, live_mask, w_rad, emb_center, emb_neigh, w_env, w_lat, w_out)
    env_sum = jax.ops.segment_sum(contrib(displace), center_ids, num_segments=ATOM_DEV)
    pair_vals, pull_back = jax.vjp(energy_of, displace, env_sum[center_ids])
    d_first, d_gather = pull_back(jnp.ones_like(pair_vals))
    d_env = jax.ops.segment_sum(d_gather, center_ids, num_segments=ATOM_DEV)
    _, pull_second = jax.vjp(contrib, displace)
    d_second = pull_second(d_env[center_ids])[0]
    d_displace = d_first + d_second
    slots_total = comb_pos.shape[1]
    gradient = jnp.zeros((3, slots_total), jnp.float32).at[:, neighbour_ids].add(d_displace).at[:, center_ids].add(-d_displace)
    shares = jnp.zeros((slots_total,), jnp.float32).at[neighbour_ids].add(0.5 * pair_vals).at[center_ids].add(0.5 * pair_vals)
    return (-gradient, shares)

def reference(positions, species, send_lists, centers, neighbours, live_blocks, w_rad, emb_center, emb_neigh, w_env, w_lat, w_out):
    outer_len = N_OUTER
    inner_len = N_INNER

    def device_step(carry, device):
        row_o = device // inner_len
        row_n = device % inner_len
        pieces = [device * ATOM_DEV + jnp.arange(ATOM_DEV).astype(jnp.int32)]
        for listed in range(8):
            step_x, step_y = DIRS[listed]
            source = (row_o - step_x) % outer_len * inner_len + (row_n - step_y) % inner_len
            start = (source * SEND).astype(jnp.int32)
            send_row = lax.dynamic_slice(send_lists, (jnp.asarray(listed, jnp.int32), start), (1, SEND))[0]
            pieces.append((source * ATOM_DEV).astype(jnp.int32) + send_row)
        combined = jnp.concatenate(pieces).astype(jnp.int32)
        first_pair = (device * PAIR_DEV).astype(jnp.int32)
        center_ids = lax.dynamic_slice_in_dim(centers, first_pair, PAIR_DEV)
        neighbour_ids = lax.dynamic_slice_in_dim(neighbours, first_pair, PAIR_DEV)
        live_mask = (jnp.arange(PAIR_DEV) // 128 < live_blocks[device]).astype(jnp.float32)
        force_part, energy_part = device_terms(positions[:, combined], species[combined], center_ids, neighbour_ids, live_mask, w_rad, emb_center, emb_neigh, w_env, w_lat, w_out)
        return ((carry[0].at[:, combined].add(force_part), carry[1].at[combined].add(energy_part)), None)
    start_state = (jnp.zeros((3, ATOMS), jnp.float32), jnp.zeros((ATOMS,), jnp.float32))
    (forces, atom_energy), _ = lax.scan(device_step, start_state, jnp.arange(outer_len * inner_len).astype(jnp.int32))
    return (forces, atom_energy)
```

```python
import math

import jax
import jax.numpy as jnp
from jax import lax
from jax.experimental import pallas as pl
from jax.experimental.pallas import tpu as pltpu
from jax.sharding import PartitionSpec as P

AXES = ("outer", "inner")
CUTOFF = 6.0
ROOT3 = math.sqrt(3.0)
ROOT5 = math.sqrt(5.0)
ROOT15 = math.sqrt(15.0)
LANES = 128
F32 = jnp.float32
BF16 = jnp.bfloat16
ORDER_OF = (0, 1, 1, 1, 2, 2, 2, 2, 2)


def exchange(block, along, parity):
    outer_len = lax.axis_size("outer")
    inner_len = lax.axis_size("inner")
    route = []
    for o in range(outer_len):
        for n in range(inner_len):
            if along == "outer":
                partner = ((o + 1 if o % 2 == parity else o - 1) % outer_len, n)
            else:
                partner = (o, (n + 1 if n % 2 == parity else n - 1) % inner_len)
            route.append((o * inner_len + n, partner[0] * inner_len + partner[1]))
    return lax.ppermute(block, AXES, route)


def dot(lhs, rhs):
    return jnp.dot(lhs, rhs, preferred_element_type=F32)


def dot_lanes(lhs, rhs):
    return lax.dot_general(lhs, rhs, (((1,), (1,)), ((), ())), preferred_element_type=F32)


def dot_rows(lhs, rhs):
    return lax.dot_general(lhs, rhs, (((0,), (0,)), ((), ())), preferred_element_type=F32)


def parts(value, count):
    out = []
    for _ in range(count):
        piece = value.astype(BF16)
        out.append(piece)
        value = value - piece.astype(F32)
    return out


def onehot_low(low_row):
    rows = lax.broadcasted_iota(jnp.int32, (LANES, low_row.shape[1]), 0)
    return jnp.where(rows == low_row, 1.0, 0.0).astype(BF16)


def high_mask(high_row, group):
    rows = lax.broadcasted_iota(jnp.int32, (8, high_row.shape[1]), 0)
    return high_row == 2 * group + jnp.where(rows >= 4, 1, 0)


def gather(table, low_hot, high_row):
    size = table.shape[0]
    found = dot(jnp.concatenate(parts(table, 3), 0), low_hot)
    found = found[0:size] + found[size : 2 * size] + found[2 * size :]
    total = None
    for group in range(size // 8):
        term = jnp.where(high_mask(high_row, group), found[8 * group : 8 * group + 8], 0.0)
        total = term if total is None else total + term
    return total + pltpu.roll(total, 4, 0)


def scatter(values, low_hot, high_row, groups):
    spread = [jnp.where(high_mask(high_row, group), values, 0.0) for group in range(groups)]
    spread = jnp.concatenate(spread, 0)
    size = 8 * groups
    summed = dot_lanes(jnp.concatenate(parts(spread, 3), 0), low_hot)
    return summed[0:size] + summed[size : 2 * size] + summed[2 * size :]


def local_table(pos_ref, spec_ref):
    packed = jnp.concatenate([pos_ref[...], spec_ref[...].astype(F32)], 0)
    return jnp.concatenate([packed[:, j * LANES : (j + 1) * LANES] for j in range(4)], 0)


def padded_lists(lists_ref, wide_ref):
    wide_ref[...] = jnp.zeros_like(wide_ref)
    wide_ref[:, 0 : lists_ref.shape[1]] = lists_ref[...]
    return wide_ref[...]


def send_kernel(pos_ref, spec_ref, lists_ref, first_ref, second_ref, mid_ref, table_ref, wide_ref):
    table = local_table(pos_ref, spec_ref)
    table_ref[...] = table
    lists = padded_lists(lists_ref, wide_ref)
    tiles = []
    rows = lax.broadcasted_iota(jnp.int32, (8, LANES), 0)
    for k in range(8):
        ids = lists[k : k + 1]
        taken = gather(table, onehot_low(ids & 127), ids >> 7)
        tiles.append(jnp.where(rows < 4, taken[:, 0:LANES], taken[:, LANES:]))
    even = lax.axis_index("outer") % 2 == 0
    for j in range(3):
        at = slice(8 * j, 8 * j + 8)
        first_ref[at] = jnp.where(even, tiles[5 + j], tiles[j])
        second_ref[at] = jnp.where(even, tiles[j], tiles[5 + j])
    mid_ref[0:8] = tiles[3]
    mid_ref[8:16] = tiles[4]


def silu_parts(pre):
    sig = 1.0 / (1.0 + jnp.exp(-pre))
    act = pre * sig
    return act, sig + act * (1.0 - sig)


def pair_kernel(
    feat,
    table_ref,
    first_ref,
    second_ref,
    low_ref,
    up_ref,
    centers_ref,
    neigh_ref,
    live_ref,
    w_rad_ref,
    emb_center_ref,
    emb_neigh_ref,
    w_env_ref,
    w_lat_ref,
    w_out_ref,
    local_ref,
    out_a_ref,
    out_b_ref,
    edge_a_ref,
    edge_b_ref,
    same_ref,
    contrib_ref,
    gath_ref,
):
    pair_len = centers_ref.shape[1]
    lat = w_lat_ref.shape[1]
    even_o = lax.axis_index("outer") % 2 == 0
    even_n = lax.axis_index("inner") % 2 == 0

    centers = centers_ref[...]
    for i in range(pair_len // LANES):
        own = centers[:, i * LANES : (i + 1) * LANES].astype(F32)
        down = jnp.broadcast_to(own, (LANES, LANES)).T
        for j in range(pair_len // LANES):
            across = centers[:, j * LANES : (j + 1) * LANES].astype(F32)
            same_ref[i * LANES : (i + 1) * LANES, j * LANES : (j + 1) * LANES] = jnp.where(
                down == across, 1.0, 0.0
            ).astype(BF16)

    first = first_ref[...]
    second = second_ref[...]
    low = low_ref[...]
    up = up_ref[...]
    by_minus = jnp.where(even_n, low, up)
    by_plus = jnp.where(even_n, up, low)
    lead = [
        jnp.where(even_o, first[8:16], second[8:16]),
        jnp.where(even_o, second[8:16], first[8:16]),
    ]
    diag = []
    for arrived in (by_minus, by_plus):
        diag.append(
            (
                jnp.where(even_o, arrived[8:16], arrived[16:24]),
                jnp.where(even_o, arrived[16:24], arrived[8:16]),
            )
        )
    table = jnp.concatenate(
        [
            table_ref[...],
            diag[0][0],
            lead[0],
            diag[1][0],
            by_minus[0:8],
            by_plus[0:8],
            diag[0][1],
            lead[1],
            diag[1][1],
        ],
        0,
    )

    neigh = neigh_ref[...]
    ghost = neigh - 512
    listed = (ghost * 745) >> 17
    entry = ghost - 176 * listed
    is_local = neigh < 512
    neigh_low = jnp.where(is_local, neigh & 127, entry & 127)
    neigh_high = jnp.where(is_local, neigh >> 7, 4 + 2 * listed + (entry >> 7))
    neigh_hot = onehot_low(neigh_low)
    center_hot = onehot_low(centers & 127)
    center_high = centers >> 7
    at_neigh = gather(table, neigh_hot, neigh_high)
    at_center = gather(table_ref[...], center_hot, center_high)
    moved = at_neigh - at_center

    block = lax.broadcasted_iota(jnp.int32, (1, pair_len), 1) // 128
    mask = jnp.where(block < live_ref[0], 1.0, 0.0)

    rx, ry, rz = moved[0:1], moved[1:2], moved[2:3]
    squared = rx * rx + ry * ry + rz * rz + 1.0
    dist = jnp.sqrt(squared)
    inv = 1.0 / dist
    ux, uy, uz = rx * inv, ry * inv, rz * inv
    slack = 1.0 - squared * (1.0 / (CUTOFF * CUTOFF))
    env = slack * slack
    scaled = env * mask
    ns = (lax.broadcasted_iota(jnp.int32, (8, pair_len), 0) + 1).astype(F32)
    turns = ns * (dist * (1.0 / CUTOFF))
    whole = jnp.floor(turns + 0.5)
    rest = (turns - whole) * math.pi
    odd = whole - 2.0 * jnp.floor(whole * 0.5)
    sign = 1.0 - 2.0 * odd
    r2 = rest * rest
    sine = sign * rest * (
        1.0
        + r2 * (-1.0 / 6 + r2 * (1.0 / 120 + r2 * (-1.0 / 5040 + r2 * (1.0 / 362880 - r2 / 39916800.0))))
    )
    cosine = sign * (
        1.0
        + r2
        * (
            -0.5
            + r2
            * (
                1.0 / 24
                + r2 * (-1.0 / 720 + r2 * (1.0 / 40320 + r2 * (-1.0 / 3628800 + r2 / 479001600.0)))
            )
        )
    )
    scale = inv * env
    basis = sine * scale
    w_rad = w_rad_ref[...]
    kinds = lax.broadcasted_iota(jnp.int32, (8, pair_len), 0).astype(F32)
    hot_center = jnp.where(at_center[3:4] == kinds, 1.0, 0.0).astype(BF16)
    hot_neigh = jnp.where(at_neigh[3:4] == kinds, 1.0, 0.0).astype(BF16)
    b1, b2, b3 = parts(basis, 3)
    w1, w2, w3 = parts(w_rad, 3)
    stacked = jnp.concatenate([b1, b1, b2, b1, b2, b3, hot_center, hot_neigh], 0)
    none = jnp.zeros((1, lat), BF16)
    weights = jnp.concatenate(
        [w1, w2, w1, w3, w2, w1, emb_center_ref[...], none, emb_neigh_ref[...], none], 0
    )
    pre = dot_rows(weights, stacked)
    latent, slope = silu_parts(pre)
    half = latent.astype(BF16)
    raw = dot_rows(w_env_ref[...], half)
    weight = raw * scaled
    shape = [
        None,
        ROOT3 * ux,
        ROOT3 * uy,
        ROOT3 * uz,
        ROOT15 * ux * uy,
        ROOT15 * uy * uz,
        0.5 * ROOT5 * (2.0 * uz * uz - ux * ux - uy * uy),
        ROOT15 * ux * uz,
        0.5 * ROOT15 * (ux * ux - uy * uy),
    ]

    def times(value, k):
        return value if k == 0 else value * shape[k]

    def of_order(value, k):
        return value[ORDER_OF[k] * feat : (ORDER_OF[k] + 1) * feat]

    for k in range(9):
        contrib_ref[k * feat : (k + 1) * feat] = times(of_order(weight, k), k).astype(BF16)
    gath_ref[...] = dot(contrib_ref[...], same_ref[...])
    sums = [None, None, None]
    for k in range(9):
        term = times(gath_ref[k * feat : (k + 1) * feat], k)
        order = ORDER_OF[k]
        sums[order] = term if sums[order] is None else sums[order] + term
    sums = jnp.concatenate(sums, 0)
    invariant = (2.0 * weight * sums).astype(BF16)
    w_lat = w_lat_ref[...]
    joined = jnp.concatenate([half, invariant], 0)
    update, slope2 = silu_parts(dot_rows(w_lat, joined))
    refined = (latent + update).astype(BF16)
    w_out = w_out_ref[...].astype(F32)
    raw_energy = jnp.sum(refined.astype(F32) * w_out, axis=0, keepdims=True)
    energy = scaled * raw_energy

    d_refined = scaled * w_out
    d_joined = dot(w_lat, (d_refined * slope2).astype(BF16))
    d_inv2 = 2.0 * d_joined[lat:]
    d_weight = d_inv2 * sums
    d_sums = d_inv2 * weight
    for k in range(9):
        contrib_ref[k * feat : (k + 1) * feat] = times(of_order(d_sums, k), k).astype(BF16)
    back = dot(contrib_ref[...], same_ref[...])
    d_shape = [None] * 9
    d_order = [None, None, None]
    for k in range(9):
        here = back[k * feat : (k + 1) * feat]
        order = ORDER_OF[k]
        term = times(here, k)
        d_order[order] = term if d_order[order] is None else d_order[order] + term
        if k:
            both = of_order(d_sums, k) * gath_ref[k * feat : (k + 1) * feat] + of_order(weight, k) * here
            d_shape[k] = jnp.sum(both, axis=0, keepdims=True)
    d_weight = d_weight + jnp.concatenate(d_order, 0)
    d_scaled = raw_energy + jnp.sum(d_weight * raw, axis=0, keepdims=True)
    d_latent = d_refined + d_joined[:lat] + dot(w_env_ref[...], (d_weight * scaled).astype(BF16))
    d_pre = d_latent * slope
    p1, p2 = parts(d_pre, 2)
    near = dot(jnp.concatenate([w1, w2], 0), p1)
    d_basis = near[0:8] + near[8:16] + dot(w1, p2)

    along = jnp.sum(d_basis * sine, axis=0, keepdims=True)
    turned = jnp.sum(d_basis * cosine * ns, axis=0, keepdims=True)
    d_env = along * inv + mask * d_scaled
    dx = (
        ROOT3 * d_shape[1]
        + ROOT15 * (uy * d_shape[4] + uz * d_shape[7] + ux * d_shape[8])
        - ROOT5 * ux * d_shape[6]
    )
    dy = (
        ROOT3 * d_shape[2]
        + ROOT15 * (ux * d_shape[4] + uz * d_shape[5] - uy * d_shape[8])
        - ROOT5 * uy * d_shape[6]
    )
    dz = (
        ROOT3 * d_shape[3]
        + ROOT15 * (uy * d_shape[5] + ux * d_shape[7])
        + 2.0 * ROOT5 * uz * d_shape[6]
    )
    d_inv = along * env + dx * rx + dy * ry + dz * rz
    d_dist = turned * (math.pi / CUTOFF) * scale - d_inv * inv * inv
    d_squared = 0.5 * inv * d_dist - (2.0 / (CUTOFF * CUTOFF)) * slack * d_env
    gx = dx * inv + 2.0 * rx * d_squared
    gy = dy * inv + 2.0 * ry * d_squared
    gz = dz * inv + 2.0 * rz * d_squared
    half_energy = 0.5 * energy
    rows4 = [gx, gy, gz, half_energy]
    values = jnp.concatenate(rows4 + rows4, 0)
    rows = lax.broadcasted_iota(jnp.int32, (8, pair_len), 0)
    flipped = jnp.where((rows & 3) == 3, values, -values)
    at_neigh = scatter(flipped, neigh_hot, neigh_high, table.shape[0] // 8)
    at_center = scatter(values, center_hot, center_high, 2)
    local_ref[...] = at_neigh[0:16] + at_center

    tile = [at_neigh[16 + 8 * k : 24 + 8 * k] for k in range(8)]
    back_minus = [tile[3], jnp.where(even_o, tile[0], tile[5]), jnp.where(even_o, tile[5], tile[0])]
    back_plus = [tile[4], jnp.where(even_o, tile[2], tile[7]), jnp.where(even_o, tile[7], tile[2])]
    for j in range(3):
        at = slice(8 * j, 8 * j + 8)
        out_a_ref[at] = jnp.where(even_n, back_minus[j], back_plus[j])
        out_b_ref[at] = jnp.where(even_n, back_plus[j], back_minus[j])
    edge_a_ref[...] = jnp.where(even_o, tile[1], tile[6])
    edge_b_ref[...] = jnp.where(even_o, tile[6], tile[1])


def collect_kernel(
    local_ref, lists_ref, first_ref, second_ref, low_ref, up_ref, forces_ref, energy_ref, wide_ref
):
    even_o = lax.axis_index("outer") % 2 == 0
    even_n = lax.axis_index("inner") % 2 == 0
    first = first_ref[...]
    second = second_ref[...]
    plus = jnp.where(even_o, first, second)
    minus = jnp.where(even_o, second, first)
    up = jnp.where(even_n, low_ref[0:8], up_ref[0:8])
    down = jnp.where(even_n, up_ref[0:8], low_ref[0:8])
    tiles = [minus[0:8], minus[8:16], minus[16:24], down, up, plus[0:8], plus[8:16], plus[16:24]]
    lists = padded_lists(lists_ref, wide_ref)
    rows = lax.broadcasted_iota(jnp.int32, (8, LANES), 0)
    total = local_ref[...]
    for k in range(8):
        turned = pltpu.roll(tiles[k], 4, 0)
        values = jnp.concatenate(
            [jnp.where(rows < 4, tiles[k], turned), jnp.where(rows < 4, turned, tiles[k])], 1
        )
        ids = lists[k : k + 1]
        total = total + scatter(values, onehot_low(ids & 127), ids >> 7, 2)
    for j in range(4):
        forces_ref[:, j * LANES : (j + 1) * LANES] = total[4 * j : 4 * j + 3]
        energy_ref[:, j * LANES : (j + 1) * LANES] = total[4 * j + 3 : 4 * j + 4]


def on_device(
    positions,
    species,
    send_lists,
    centers,
    neighbours,
    live_blocks,
    w_rad,
    emb_center,
    emb_neigh,
    w_env,
    w_lat,
    w_out,
):
    pair_len = centers.shape[0]
    atom_count = positions.shape[1]
    feat = w_env.shape[1] // 3
    width = 3 * w_env.shape[1]
    group = jax.ShapeDtypeStruct((24, LANES), F32)
    tile = jax.ShapeDtypeStruct((8, LANES), F32)
    wide = pltpu.VMEM((8, 2 * LANES), jnp.int32)
    first, second, mid, table = pl.pallas_call(
        send_kernel,
        out_shape=[
            group,
            group,
            jax.ShapeDtypeStruct((16, LANES), F32),
            jax.ShapeDtypeStruct((16, LANES), F32),
        ],
        scratch_shapes=[wide],
        name="gather_sends",
    )(positions, species.reshape(1, atom_count), send_lists)

    even_o = lax.axis_index("outer") % 2 == 0
    even_n = lax.axis_index("inner") % 2 == 0
    second = exchange(second, "outer", 1)
    first = exchange(first, "outer", 0)
    by_plus = jnp.concatenate([mid[8:16], first[16:24], second[16:24]], 0)
    by_minus = jnp.concatenate([mid[0:8], first[0:8], second[0:8]], 0)
    up = exchange(jnp.where(even_n, by_minus, by_plus), "inner", 1)
    low = exchange(jnp.where(even_n, by_plus, by_minus), "inner", 0)

    whole = pl.BlockSpec(memory_space=pltpu.VMEM)
    scalar = pl.BlockSpec(memory_space=pltpu.SMEM)
    local, out_a, out_b, edge_a, edge_b = pl.pallas_call(
        lambda *refs: pair_kernel(feat, *refs),
        out_shape=[jax.ShapeDtypeStruct((16, LANES), F32), group, group, tile, tile],
        in_specs=[whole] * 7 + [scalar] + [whole] * 6,
        scratch_shapes=[
            pltpu.VMEM((pair_len, pair_len), BF16),
            pltpu.VMEM((width, pair_len), BF16),
            pltpu.VMEM((width, pair_len), F32),
        ],
        compiler_params=pltpu.CompilerParams(vmem_limit_bytes=48 * 1024 * 1024),
        name="pair_terms",
    )(
        table,
        first,
        second,
        low,
        up,
        centers.reshape(1, pair_len),
        neighbours.reshape(1, pair_len),
        live_blocks,
        w_rad,
        emb_center,
        emb_neigh,
        w_env,
        w_lat,
        w_out.reshape(-1, 1),
    )

    up = exchange(out_b, "inner", 1)
    low = exchange(out_a, "inner", 0)
    by_plus = jnp.where(even_n, low, up)
    by_minus = jnp.where(even_n, up, low)
    second = exchange(
        jnp.concatenate([by_minus[16:24], edge_b, by_plus[16:24]], 0), "outer", 1
    )
    first = exchange(jnp.concatenate([by_minus[8:16], edge_a, by_plus[8:16]], 0), "outer", 0)
    forces, energy = pl.pallas_call(
        collect_kernel,
        out_shape=[
            jax.ShapeDtypeStruct((3, atom_count), F32),
            jax.ShapeDtypeStruct((1, atom_count), F32),
        ],
        scratch_shapes=[wide],
        name="collect_terms",
    )(local, send_lists, first, second, low, up)
    return forces, energy.reshape(atom_count)


def solution(mesh):
    return jax.shard_map(
        on_device,
        mesh=mesh,
        in_specs=(
            P(None, AXES),
            P(AXES),
            P(None, AXES),
            P(AXES),
            P(AXES),
            P(AXES),
            P(),
            P(),
            P(),
            P(),
            P(),
            P(),
        ),
        out_specs=(P(None, AXES), P(AXES)),
        check_vma=False,
    )
```

```python
import math

import jax
import jax.numpy as jnp
from jax import lax
from jax.experimental import pallas as pl
from jax.experimental.pallas import tpu as pltpu
from jax.sharding import PartitionSpec as P

AXES = ("outer", "inner")
CUTOFF = 6.0
ROOT3 = math.sqrt(3.0)
ROOT5 = math.sqrt(5.0)
ROOT15 = math.sqrt(15.0)
LANES = 128
F32 = jnp.float32
BF16 = jnp.bfloat16
SMALL = pltpu.CompilerParams(vmem_limit_bytes=8 * 1024 * 1024)
LARGE = pltpu.CompilerParams(vmem_limit_bytes=32 * 1024 * 1024)
ORDER_OF = (0, 1, 1, 1, 2, 2, 2, 2, 2)


def exchange(block, along, parity):
    outer_len = lax.axis_size("outer")
    inner_len = lax.axis_size("inner")
    route = []
    for o in range(outer_len):
        for n in range(inner_len):
            if along == "outer":
                partner = ((o + 1 if o % 2 == parity else o - 1) % outer_len, n)
            else:
                partner = (o, (n + 1 if n % 2 == parity else n - 1) % inner_len)
            route.append((o * inner_len + n, partner[0] * inner_len + partner[1]))
    return lax.ppermute(block, AXES, route)


def dot(lhs, rhs):
    return jnp.dot(lhs, rhs, preferred_element_type=F32)


def dot_lanes(lhs, rhs):
    return lax.dot_general(lhs, rhs, (((1,), (1,)), ((), ())), preferred_element_type=F32)


def dot_rows(lhs, rhs):
    return lax.dot_general(lhs, rhs, (((0,), (0,)), ((), ())), preferred_element_type=F32)


def parts(value, count):
    out = []
    for _ in range(count):
        piece = value.astype(BF16)
        out.append(piece)
        value = value - piece.astype(F32)
    return out


def onehot_low(low_row):
    rows = lax.broadcasted_iota(jnp.int32, (LANES, low_row.shape[1]), 0)
    return jnp.where(rows == low_row, 1.0, 0.0).astype(BF16)


def high_mask(high_row, group):
    rows = lax.broadcasted_iota(jnp.int32, (8, high_row.shape[1]), 0)
    return high_row == 2 * group + jnp.where(rows >= 4, 1, 0)


def gather(table, low_hot, high_row):
    size = table.shape[0]
    found = dot(jnp.concatenate(parts(table, 3), 0), low_hot)
    found = found[0:size] + found[size : 2 * size] + found[2 * size :]
    total = None
    for group in range(size // 8):
        term = jnp.where(high_mask(high_row, group), found[8 * group : 8 * group + 8], 0.0)
        total = term if total is None else total + term
    return total + pltpu.roll(total, 4, 0)


def scatter(values, low_hot, high_row, groups):
    spread = [jnp.where(high_mask(high_row, group), values, 0.0) for group in range(groups)]
    spread = jnp.concatenate(spread, 0)
    size = 8 * groups
    summed = dot_lanes(jnp.concatenate(parts(spread, 3), 0), low_hot)
    return summed[0:size] + summed[size : 2 * size] + summed[2 * size :]


def local_table(pos_ref, spec_ref):
    packed = jnp.concatenate([pos_ref[...], spec_ref[...].astype(F32)], 0)
    return jnp.concatenate([packed[:, j * LANES : (j + 1) * LANES] for j in range(4)], 0)


def padded_lists(lists_ref, wide_ref):
    wide_ref[...] = jnp.zeros_like(wide_ref)
    wide_ref[:, 0 : lists_ref.shape[1]] = lists_ref[...]
    return wide_ref[...]


def send_kernel(pos_ref, spec_ref, lists_ref, first_ref, second_ref, mid_ref, table_ref, wide_ref):
    table = local_table(pos_ref, spec_ref)
    table_ref[...] = table
    lists = padded_lists(lists_ref, wide_ref)
    tiles = []
    rows = lax.broadcasted_iota(jnp.int32, (8, LANES), 0)
    for k in range(8):
        ids = lists[k : k + 1]
        taken = gather(table, onehot_low(ids & 127), ids >> 7)
        tiles.append(jnp.where(rows < 4, taken[:, 0:LANES], taken[:, LANES:]))
    even = lax.axis_index("outer") % 2 == 0
    for j in range(3):
        at = slice(8 * j, 8 * j + 8)
        first_ref[at] = jnp.where(even, tiles[5 + j], tiles[j])
        second_ref[at] = jnp.where(even, tiles[j], tiles[5 + j])
    mid_ref[0:8] = tiles[3]
    mid_ref[8:16] = tiles[4]


def silu_parts(pre):
    sig = 1.0 / (1.0 + jnp.exp(-pre))
    act = pre * sig
    return act, sig + act * (1.0 - sig)


def pair_kernel(
    feat,
    table_ref,
    second_ref,
    first_ref,
    low_ref,
    up_ref,
    centers_ref,
    neigh_ref,
    live_ref,
    w_rad_ref,
    emb_center_ref,
    emb_neigh_ref,
    w_env_ref,
    w_lat_ref,
    w_out_ref,
    local_ref,
    out_a_ref,
    out_b_ref,
    edge_a_ref,
    edge_b_ref,
    same_ref,
    contrib_ref,
    gath_ref,
):
    pair_len = centers_ref.shape[1]
    lat = w_lat_ref.shape[1]
    even_o = lax.axis_index("outer") % 2 == 0
    even_n = lax.axis_index("inner") % 2 == 0

    centers = centers_ref[...]
    for i in range(pair_len // LANES):
        own = centers[:, i * LANES : (i + 1) * LANES].astype(F32)
        down = jnp.broadcast_to(own, (LANES, LANES)).T
        for j in range(pair_len // LANES):
            across = centers[:, j * LANES : (j + 1) * LANES].astype(F32)
            same_ref[i * LANES : (i + 1) * LANES, j * LANES : (j + 1) * LANES] = jnp.where(
                down == across, 1.0, 0.0
            ).astype(BF16)

    first = first_ref[...]
    second = second_ref[...]
    low = low_ref[...]
    up = up_ref[...]
    by_minus = jnp.where(even_n, low, up)
    by_plus = jnp.where(even_n, up, low)
    lead = [
        jnp.where(even_o, first[8:16], second[8:16]),
        jnp.where(even_o, second[8:16], first[8:16]),
    ]
    diag = []
    for arrived in (by_minus, by_plus):
        diag.append(
            (
                jnp.where(even_o, arrived[8:16], arrived[16:24]),
                jnp.where(even_o, arrived[16:24], arrived[8:16]),
            )
        )
    table = jnp.concatenate(
        [
            table_ref[...],
            diag[0][0],
            lead[0],
            diag[1][0],
            by_minus[0:8],
            by_plus[0:8],
            diag[0][1],
            lead[1],
            diag[1][1],
        ],
        0,
    )

    neigh = neigh_ref[...]
    ghost = neigh - 512
    listed = (ghost * 745) >> 17
    entry = ghost - 176 * listed
    is_local = neigh < 512
    neigh_low = jnp.where(is_local, neigh & 127, entry & 127)
    neigh_high = jnp.where(is_local, neigh >> 7, 4 + 2 * listed + (entry >> 7))
    neigh_hot = onehot_low(neigh_low)
    center_hot = onehot_low(centers & 127)
    center_high = centers >> 7
    at_neigh = gather(table, neigh_hot, neigh_high)
    at_center = gather(table_ref[...], center_hot, center_high)
    moved = at_neigh - at_center

    block = lax.broadcasted_iota(jnp.int32, (1, pair_len), 1) // 128
    mask = jnp.where(block < live_ref[0], 1.0, 0.0)

    rx, ry, rz = moved[0:1], moved[1:2], moved[2:3]
    squared = rx * rx + ry * ry + rz * rz + 1.0
    dist = jnp.sqrt(squared)
    inv = 1.0 / dist
    ux, uy, uz = rx * inv, ry * inv, rz * inv
    slack = 1.0 - squared * (1.0 / (CUTOFF * CUTOFF))
    env = slack * slack
    scaled = env * mask
    ns = (lax.broadcasted_iota(jnp.int32, (8, pair_len), 0) + 1).astype(F32)
    turns = ns * (dist * (1.0 / CUTOFF))
    whole = jnp.floor(turns + 0.5)
    rest = (turns - whole) * math.pi
    odd = whole - 2.0 * jnp.floor(whole * 0.5)
    sign = 1.0 - 2.0 * odd
    r2 = rest * rest
    sine = sign * rest * (
        1.0
        + r2 * (-1.0 / 6 + r2 * (1.0 / 120 + r2 * (-1.0 / 5040 + r2 * (1.0 / 362880 - r2 / 39916800.0))))
    )
    cosine = sign * (
        1.0
        + r2
        * (
            -0.5
            + r2
            * (
                1.0 / 24
                + r2 * (-1.0 / 720 + r2 * (1.0 / 40320 + r2 * (-1.0 / 3628800 + r2 / 479001600.0)))
            )
        )
    )
    scale = inv * env
    basis = sine * scale
    w_rad = w_rad_ref[...]
    kinds = lax.broadcasted_iota(jnp.int32, (8, pair_len), 0).astype(F32)
    hot_center = jnp.where(at_center[3:4] == kinds, 1.0, 0.0).astype(BF16)
    hot_neigh = jnp.where(at_neigh[3:4] == kinds, 1.0, 0.0).astype(BF16)
    b1, b2, b3 = parts(basis, 3)
    w1, w2, w3 = parts(w_rad, 3)
    stacked = jnp.concatenate([b1, b1, b2, b1, b2, b3, hot_center, hot_neigh], 0)
    none = jnp.zeros((1, lat), BF16)
    weights = jnp.concatenate(
        [w1, w2, w1, w3, w2, w1, emb_center_ref[...], none, emb_neigh_ref[...], none], 0
    )
    pre = dot_rows(weights, stacked)
    latent, slope = silu_parts(pre)
    half = latent.astype(BF16)
    raw = dot_rows(w_env_ref[...], half)
    weight = raw * scaled
    shape = [
        None,
        ROOT3 * ux,
        ROOT3 * uy,
        ROOT3 * uz,
        ROOT15 * ux * uy,
        ROOT15 * uy * uz,
        0.5 * ROOT5 * (2.0 * uz * uz - ux * ux - uy * uy),
        ROOT15 * ux * uz,
        0.5 * ROOT15 * (ux * ux - uy * uy),
    ]

    def times(value, k):
        return value if k == 0 else value * shape[k]

    def of_order(value, k):
        return value[ORDER_OF[k] * feat : (ORDER_OF[k] + 1) * feat]

    for k in range(9):
        contrib_ref[k * feat : (k + 1) * feat] = times(of_order(weight, k), k).astype(BF16)
    gath_ref[...] = dot(contrib_ref[...], same_ref[...])
    sums = [None, None, None]
    for k in range(9):
        term = times(gath_ref[k * feat : (k + 1) * feat], k)
        order = ORDER_OF[k]
        sums[order] = term if sums[order] is None else sums[order] + term
    sums = jnp.concatenate(sums, 0)
    invariant = (2.0 * weight * sums).astype(BF16)
    w_lat = w_lat_ref[...]
    joined = jnp.concatenate([half, invariant], 0)
    update, slope2 = silu_parts(dot_rows(w_lat, joined))
    refined = (latent + update).astype(BF16)
    w_out = w_out_ref[...].astype(F32)
    raw_energy = jnp.sum(refined.astype(F32) * w_out, axis=0, keepdims=True)
    energy = scaled * raw_energy

    d_refined = scaled * w_out
    d_joined = dot(w_lat, (d_refined * slope2).astype(BF16))
    d_inv2 = 2.0 * d_joined[lat:]
    d_weight = d_inv2 * sums
    d_sums = d_inv2 * weight
    for k in range(9):
        contrib_ref[k * feat : (k + 1) * feat] = times(of_order(d_sums, k), k).astype(BF16)
    back = dot(contrib_ref[...], same_ref[...])
    d_shape = [None] * 9
    d_order = [None, None, None]
    for k in range(9):
        here = back[k * feat : (k + 1) * feat]
        order = ORDER_OF[k]
        term = times(here, k)
        d_order[order] = term if d_order[order] is None else d_order[order] + term
        if k:
            both = of_order(d_sums, k) * gath_ref[k * feat : (k + 1) * feat] + of_order(weight, k) * here
            d_shape[k] = jnp.sum(both, axis=0, keepdims=True)
    d_weight = d_weight + jnp.concatenate(d_order, 0)
    d_scaled = raw_energy + jnp.sum(d_weight * raw, axis=0, keepdims=True)
    d_latent = d_refined + d_joined[:lat] + dot(w_env_ref[...], (d_weight * scaled).astype(BF16))
    d_pre = d_latent * slope
    p1, p2 = parts(d_pre, 2)
    near = dot(jnp.concatenate([w1, w2], 0), p1)
    d_basis = near[0:8] + near[8:16] + dot(w1, p2)

    along = jnp.sum(d_basis * sine, axis=0, keepdims=True)
    turned = jnp.sum(d_basis * cosine * ns, axis=0, keepdims=True)
    d_env = along * inv + mask * d_scaled
    dx = (
        ROOT3 * d_shape[1]
        + ROOT15 * (uy * d_shape[4] + uz * d_shape[7] + ux * d_shape[8])
        - ROOT5 * ux * d_shape[6]
    )
    dy = (
        ROOT3 * d_shape[2]
        + ROOT15 * (ux * d_shape[4] + uz * d_shape[5] - uy * d_shape[8])
        - ROOT5 * uy * d_shape[6]
    )
    dz = (
        ROOT3 * d_shape[3]
        + ROOT15 * (uy * d_shape[5] + ux * d_shape[7])
        + 2.0 * ROOT5 * uz * d_shape[6]
    )
    d_inv = along * env + dx * rx + dy * ry + dz * rz
    d_dist = turned * (math.pi / CUTOFF) * scale - d_inv * inv * inv
    d_squared = 0.5 * inv * d_dist - (2.0 / (CUTOFF * CUTOFF)) * slack * d_env
    gx = dx * inv + 2.0 * rx * d_squared
    gy = dy * inv + 2.0 * ry * d_squared
    gz = dz * inv + 2.0 * rz * d_squared
    half_energy = 0.5 * energy
    rows4 = [gx, gy, gz, half_energy]
    values = jnp.concatenate(rows4 + rows4, 0)
    rows = lax.broadcasted_iota(jnp.int32, (8, pair_len), 0)
    flipped = jnp.where((rows & 3) == 3, values, -values)
    at_neigh = scatter(flipped, neigh_hot, neigh_high, table.shape[0] // 8)
    at_center = scatter(values, center_hot, center_high, 2)
    local_ref[...] = at_neigh[0:16] + at_center

    tile = [at_neigh[16 + 8 * k : 24 + 8 * k] for k in range(8)]
    back_minus = [tile[3], jnp.where(even_o, tile[0], tile[5]), jnp.where(even_o, tile[5], tile[0])]
    back_plus = [tile[4], jnp.where(even_o, tile[2], tile[7]), jnp.where(even_o, tile[7], tile[2])]
    for j in range(3):
        at = slice(8 * j, 8 * j + 8)
        out_a_ref[at] = jnp.where(even_n, back_minus[j], back_plus[j])
        out_b_ref[at] = jnp.where(even_n, back_plus[j], back_minus[j])
    edge_a_ref[...] = jnp.where(even_o, tile[1], tile[6])
    edge_b_ref[...] = jnp.where(even_o, tile[6], tile[1])


def collect_kernel(
    local_ref, lists_ref, second_ref, first_ref, low_ref, up_ref, forces_ref, energy_ref, wide_ref
):
    even_o = lax.axis_index("outer") % 2 == 0
    even_n = lax.axis_index("inner") % 2 == 0
    first = first_ref[...]
    second = second_ref[...]
    plus = jnp.where(even_o, first, second)
    minus = jnp.where(even_o, second, first)
    up = jnp.where(even_n, low_ref[0:8], up_ref[0:8])
    down = jnp.where(even_n, up_ref[0:8], low_ref[0:8])
    tiles = [minus[0:8], minus[8:16], minus[16:24], down, up, plus[0:8], plus[8:16], plus[16:24]]
    lists = padded_lists(lists_ref, wide_ref)
    rows = lax.broadcasted_iota(jnp.int32, (8, LANES), 0)
    total = local_ref[...]
    for k in range(8):
        turned = pltpu.roll(tiles[k], 4, 0)
        values = jnp.concatenate(
            [jnp.where(rows < 4, tiles[k], turned), jnp.where(rows < 4, turned, tiles[k])], 1
        )
        ids = lists[k : k + 1]
        total = total + scatter(values, onehot_low(ids & 127), ids >> 7, 2)
    for j in range(4):
        forces_ref[:, j * LANES : (j + 1) * LANES] = total[4 * j : 4 * j + 3]
        energy_ref[:, j * LANES : (j + 1) * LANES] = total[4 * j + 3 : 4 * j + 4]


def on_device(
    positions,
    species,
    send_lists,
    centers,
    neighbours,
    live_blocks,
    w_rad,
    emb_center,
    emb_neigh,
    w_env,
    w_lat,
    w_out,
):
    pair_len = centers.shape[0]
    atom_count = positions.shape[1]
    feat = w_env.shape[1] // 3
    width = 3 * w_env.shape[1]
    group = jax.ShapeDtypeStruct((24, LANES), F32)
    tile = jax.ShapeDtypeStruct((8, LANES), F32)
    wide = pltpu.VMEM((8, 2 * LANES), jnp.int32)
    first, second, mid, table = pl.pallas_call(
        send_kernel,
        out_shape=[
            group,
            group,
            jax.ShapeDtypeStruct((16, LANES), F32),
            jax.ShapeDtypeStruct((16, LANES), F32),
        ],
        scratch_shapes=[wide],
        compiler_params=SMALL,
        name="gather_sends",
    )(positions, species.reshape(1, atom_count), send_lists)

    even_o = lax.axis_index("outer") % 2 == 0
    even_n = lax.axis_index("inner") % 2 == 0
    second = exchange(second, "outer", 1)
    first = exchange(first, "outer", 0)
    by_plus = jnp.concatenate([mid[8:16], first[16:24], second[16:24]], 0)
    by_minus = jnp.concatenate([mid[0:8], first[0:8], second[0:8]], 0)
    up = exchange(jnp.where(even_n, by_minus, by_plus), "inner", 1)
    low = exchange(jnp.where(even_n, by_plus, by_minus), "inner", 0)

    whole = pl.BlockSpec(memory_space=pltpu.VMEM)
    scalar = pl.BlockSpec(memory_space=pltpu.SMEM)
    local, out_a, out_b, edge_a, edge_b = pl.pallas_call(
        lambda *refs: pair_kernel(feat, *refs),
        out_shape=[jax.ShapeDtypeStruct((16, LANES), F32), group, group, tile, tile],
        in_specs=[whole] * 7 + [scalar] + [whole] * 6,
        scratch_shapes=[
            pltpu.VMEM((pair_len, pair_len), BF16),
            pltpu.VMEM((width, pair_len), BF16),
            pltpu.VMEM((width, pair_len), F32),
        ],
        compiler_params=LARGE,
        name="pair_terms",
    )(
        table,
        second,
        first,
        low,
        up,
        centers.reshape(1, pair_len),
        neighbours.reshape(1, pair_len),
        live_blocks,
        w_rad,
        emb_center,
        emb_neigh,
        w_env,
        w_lat,
        w_out.reshape(-1, 1),
    )

    up = exchange(out_b, "inner", 1)
    low = exchange(out_a, "inner", 0)
    by_plus = jnp.where(even_n, low, up)
    by_minus = jnp.where(even_n, up, low)
    second = exchange(
        jnp.concatenate([by_minus[16:24], edge_b, by_plus[16:24]], 0), "outer", 1
    )
    first = exchange(jnp.concatenate([by_minus[8:16], edge_a, by_plus[8:16]], 0), "outer", 0)
    forces, energy = pl.pallas_call(
        collect_kernel,
        out_shape=[
            jax.ShapeDtypeStruct((3, atom_count), F32),
            jax.ShapeDtypeStruct((1, atom_count), F32),
        ],
        scratch_shapes=[wide],
        compiler_params=SMALL,
        name="collect_terms",
    )(local, send_lists, second, first, low, up)
    return forces, energy.reshape(atom_count)


def solution(mesh):
    return jax.shard_map(
        on_device,
        mesh=mesh,
        in_specs=(
            P(None, AXES),
            P(AXES),
            P(None, AXES),
            P(AXES),
            P(AXES),
            P(AXES),
            P(),
            P(),
            P(),
            P(),
            P(),
            P(),
        ),
        out_specs=(P(None, AXES), P(AXES)),
        check_vma=False,
    )
```

```python
import math

import jax
import jax.numpy as jnp
from jax import lax
from jax.experimental import pallas as pl
from jax.experimental.pallas import tpu as pltpu
from jax.sharding import PartitionSpec as P

AXES = ("outer", "inner")
CUTOFF = 6.0
ROOT3 = math.sqrt(3.0)
ROOT5 = math.sqrt(5.0)
ROOT15 = math.sqrt(15.0)
LANES = 128
F32 = jnp.float32
BF16 = jnp.bfloat16
SMALL = pltpu.CompilerParams(vmem_limit_bytes=8 * 1024 * 1024)
LARGE = pltpu.CompilerParams(vmem_limit_bytes=32 * 1024 * 1024)
DIRS = ((-1, -1), (-1, 0), (-1, 1), (0, -1), (0, 1), (1, -1), (1, 0), (1, 1))
SPAN = (-1, 0, 1)
TABLE, LISTS, CENTERS, NEIGH, PACKED = 0, 16, 32, 40, 48
LIVE = 38
ORDER_OF = (0, 1, 1, 1, 2, 2, 2, 2, 2)


def exchange(block, along, parity):
    outer_len = lax.axis_size("outer")
    inner_len = lax.axis_size("inner")
    route = []
    for o in range(outer_len):
        for n in range(inner_len):
            if along == "outer":
                partner = ((o + 1 if o % 2 == parity else o - 1) % outer_len, n)
            else:
                partner = (o, (n + 1 if n % 2 == parity else n - 1) % inner_len)
            route.append((o * inner_len + n, partner[0] * inner_len + partner[1]))
    return lax.ppermute(block, AXES, route)


def all_rows(block):
    return lax.all_to_all(block, "outer", 0, 0)


def dot(lhs, rhs):
    return jnp.dot(lhs, rhs, preferred_element_type=F32)


def dot_lanes(lhs, rhs):
    return lax.dot_general(lhs, rhs, (((1,), (1,)), ((), ())), preferred_element_type=F32)


def dot_rows(lhs, rhs):
    return lax.dot_general(lhs, rhs, (((0,), (0,)), ((), ())), preferred_element_type=F32)


def parts(value, count):
    out = []
    for _ in range(count):
        piece = value.astype(BF16)
        out.append(piece)
        value = value - piece.astype(F32)
    return out


def onehot_low(low_row):
    rows = lax.broadcasted_iota(jnp.int32, (LANES, low_row.shape[1]), 0)
    return jnp.where(rows == low_row, 1.0, 0.0).astype(BF16)


def high_mask(high_row, group):
    rows = lax.broadcasted_iota(jnp.int32, (8, high_row.shape[1]), 0)
    return high_row == 2 * group + jnp.where(rows >= 4, 1, 0)


def gather(table, low_hot, high_row):
    size = table.shape[0]
    found = dot(jnp.concatenate(parts(table, 3), 0), low_hot)
    found = found[0:size] + found[size : 2 * size] + found[2 * size :]
    total = None
    for group in range(size // 8):
        term = jnp.where(high_mask(high_row, group), found[8 * group : 8 * group + 8], 0.0)
        total = term if total is None else total + term
    return total + pltpu.roll(total, 4, 0)


def scatter(values, low_hot, high_row, groups):
    spread = [jnp.where(high_mask(high_row, group), values, 0.0) for group in groups]
    spread = jnp.concatenate(spread, 0)
    size = 8 * len(groups)
    summed = dot_lanes(jnp.concatenate(parts(spread, 3), 0), low_hot)
    return summed[0:size] + summed[size : 2 * size] + summed[2 * size :]


def pack_kernel(
    pos_hbm,
    spec_hbm,
    lists_hbm,
    centers_hbm,
    neigh_hbm,
    live_ref,
    out_ref,
    pos,
    spec,
    lists,
    centers,
    neigh,
    sems,
):
    fetched = []
    for j, (src, dst) in enumerate(
        (
            (pos_hbm, pos),
            (spec_hbm, spec),
            (lists_hbm, lists),
            (centers_hbm, centers),
            (neigh_hbm, neigh),
        )
    ):
        copy = pltpu.make_async_copy(src, dst, sems.at[j])
        copy.start()
        fetched.append(copy)
    for copy in fetched:
        copy.wait()
    rows = []
    for j in range(4):
        at = slice(j * LANES, (j + 1) * LANES)
        rows.append(pos[:, at])
        rows.append(spec[:, at].astype(F32))
    ids = lists[...].astype(F32)
    rest = ids.shape[1] - LANES
    rows.append(ids[:, 0:LANES])
    rows.append(jnp.concatenate([ids[:, LANES:], jnp.zeros((8, LANES - rest), F32)], 1))
    rows.append(centers[...].astype(F32))
    rows.append(jnp.full((1, LANES), live_ref[0].astype(F32)))
    rows.append(jnp.zeros((1, LANES), F32))
    rows.append(neigh[...].astype(F32))
    rows.append(jnp.zeros((2, LANES), F32))
    packed = jnp.concatenate(rows, 0)
    for q in range(out_ref.shape[0]):
        out_ref[q] = packed


def row_slot(offset):
    count = lax.axis_size("outer")
    return lax.rem(lax.axis_index("outer") + offset + count, count)


def tile_of(a, dx):
    return 3 * (a + 1) + dx + 1


def sends_kernel(raw_ref, far_ref, near_ref, mid_ref):
    even_n = lax.axis_index("inner") % 2 == 0
    rows = lax.broadcasted_iota(jnp.int32, (8, LANES), 0)
    for source in range(-2, 3):
        raw = raw_ref.at[row_slot(source)]
        wanted = [
            k for k in range(8) if abs(source + DIRS[k][0]) <= 1
        ]
        low = raw[LISTS : LISTS + 8].astype(jnp.int32)
        high = raw[LISTS + 8 : LISTS + 16].astype(jnp.int32)
        ids = [part[k : k + 1] for k in wanted for part in (low, high)]
        ids = jnp.concatenate(ids, 1)
        taken = gather(raw[TABLE : TABLE + 16], onehot_low(ids & 127), ids >> 7)
        tiles = {}
        for j, k in enumerate(wanted):
            at = 2 * j * LANES
            tiles[k] = jnp.where(
                rows < 4, taken[:, at : at + LANES], taken[:, at + LANES : at + 2 * LANES]
            )
        for dx in SPAN:
            a = source + dx
            if abs(a) > 1:
                continue
            t = tile_of(a, dx)
            minus, plus = tiles[DIRS.index((dx, -1))], tiles[DIRS.index((dx, 1))]
            far_ref[8 * t : 8 * t + 8] = jnp.where(even_n, minus, plus)
            near_ref[8 * t : 8 * t + 8] = jnp.where(even_n, plus, minus)
            if dx:
                m = 2 * (a + 1) + (dx + 1) // 2
                mid_ref[8 * m : 8 * m + 8] = tiles[DIRS.index((dx, 0))]


def silu_parts(pre):
    sig = 1.0 / (1.0 + jnp.exp(-pre))
    act = pre * sig
    return act, sig + act * (1.0 - sig)


def pair_kernel(
    feat,
    pair_len,
    raw_ref,
    mid_ref,
    up_ref,
    low_ref,
    w_rad_ref,
    emb_center_ref,
    emb_neigh_ref,
    w_env_ref,
    w_lat_ref,
    w_out_ref,
    local_ref,
    own_ref,
    back_far_ref,
    back_near_ref,
    same_ref,
    contrib_ref,
    gath_ref,
):
    chunks = pair_len // LANES
    width = len(SPAN) * pair_len
    lat = w_lat_ref.shape[1]
    even_n = lax.axis_index("inner") % 2 == 0

    def as_row(tile):
        return jnp.concatenate([tile[i : i + 1] for i in range(chunks)], 1)

    found_neigh, found_center, masks = [], [], []
    neigh_hots, neigh_highs = [], []
    for d, a in enumerate(SPAN):
        raw = raw_ref.at[row_slot(a)]
        centers = raw[CENTERS : CENTERS + 8]
        for i in range(chunks):
            down = jnp.broadcast_to(centers[i : i + 1], (LANES, LANES)).T
            for j in range(chunks):
                same_ref[d, i * LANES : (i + 1) * LANES, j * LANES : (j + 1) * LANES] = jnp.where(
                    down == centers[j : j + 1], 1.0, 0.0
                ).astype(BF16)
        table = [raw[TABLE : TABLE + 16]]
        for dx, dy in DIRS:
            t = 8 * tile_of(a, dx)
            if dy == 0:
                m = 8 * (2 * (a + 1) + (dx + 1) // 2)
                table.append(mid_ref[m : m + 8])
                continue
            by_low, by_up = low_ref[t : t + 8], up_ref[t : t + 8]
            if dy < 0:
                table.append(jnp.where(even_n, by_low, by_up))
            else:
                table.append(jnp.where(even_n, by_up, by_low))
        table = jnp.concatenate(table, 0)
        neigh = raw[NEIGH : NEIGH + 8].astype(jnp.int32)
        ghost = neigh - 512
        listed = (ghost * 745) >> 17
        entry = ghost - 176 * listed
        is_local = neigh < 512
        neigh_low = as_row(jnp.where(is_local, neigh & 127, entry & 127))
        neigh_high = as_row(jnp.where(is_local, neigh >> 7, 4 + 2 * listed + (entry >> 7)))
        center_ids = as_row(centers.astype(jnp.int32))
        neigh_hot = onehot_low(neigh_low)
        center_hot = onehot_low(center_ids & 127)
        center_high = center_ids >> 7
        found_neigh.append(gather(table, neigh_hot, neigh_high))
        found_center.append(gather(table[0:16], center_hot, center_high))
        neigh_hots.append(neigh_hot)
        neigh_highs.append(neigh_high)
        if a == 0:
            own_hot, own_high = center_hot, center_high
        block = lax.broadcasted_iota(jnp.int32, (1, pair_len), 1) // 128
        masks.append(jnp.where(block.astype(F32) < raw[LIVE : LIVE + 1, 0:1], 1.0, 0.0))
    at_neigh = jnp.concatenate(found_neigh, 1)
    at_center = jnp.concatenate(found_center, 1)
    mask = jnp.concatenate(masks, 1)
    moved = at_neigh - at_center

    rx, ry, rz = moved[0:1], moved[1:2], moved[2:3]
    squared = rx * rx + ry * ry + rz * rz + 1.0
    dist = jnp.sqrt(squared)
    inv = 1.0 / dist
    ux, uy, uz = rx * inv, ry * inv, rz * inv
    slack = 1.0 - squared * (1.0 / (CUTOFF * CUTOFF))
    env = slack * slack
    scaled = env * mask
    ns = (lax.broadcasted_iota(jnp.int32, (8, width), 0) + 1).astype(F32)
    turns = ns * (dist * (1.0 / CUTOFF))
    whole = jnp.floor(turns + 0.5)
    rest = (turns - whole) * math.pi
    odd = whole - 2.0 * jnp.floor(whole * 0.5)
    sign = 1.0 - 2.0 * odd
    r2 = rest * rest
    sine = sign * rest * (
        1.0
        + r2 * (-1.0 / 6 + r2 * (1.0 / 120 + r2 * (-1.0 / 5040 + r2 * (1.0 / 362880 - r2 / 39916800.0))))
    )
    cosine = sign * (
        1.0
        + r2
        * (
            -0.5
            + r2
            * (
                1.0 / 24
                + r2 * (-1.0 / 720 + r2 * (1.0 / 40320 + r2 * (-1.0 / 3628800 + r2 / 479001600.0)))
            )
        )
    )
    scale = inv * env
    basis = sine * scale
    w_rad = w_rad_ref[...]
    kinds = lax.broadcasted_iota(jnp.int32, (8, width), 0).astype(F32)
    hot_center = jnp.where(at_center[3:4] == kinds, 1.0, 0.0).astype(BF16)
    hot_neigh = jnp.where(at_neigh[3:4] == kinds, 1.0, 0.0).astype(BF16)
    b1, b2, b3 = parts(basis, 3)
    w1, w2, w3 = parts(w_rad, 3)
    stacked = jnp.concatenate([b1, b1, b2, b1, b2, b3, hot_center, hot_neigh], 0)
    none = jnp.zeros((1, lat), BF16)
    weights = jnp.concatenate(
        [w1, w2, w1, w3, w2, w1, emb_center_ref[...], none, emb_neigh_ref[...], none], 0
    )
    pre = dot_rows(weights, stacked)
    latent, slope = silu_parts(pre)
    half = latent.astype(BF16)
    raw = dot(w_env_ref[...], half)
    weight = raw * scaled
    shape = [
        None,
        ROOT3 * ux,
        ROOT3 * uy,
        ROOT3 * uz,
        ROOT15 * ux * uy,
        ROOT15 * uy * uz,
        0.5 * ROOT5 * (2.0 * uz * uz - ux * ux - uy * uy),
        ROOT15 * ux * uz,
        0.5 * ROOT15 * (ux * ux - uy * uy),
    ]

    def times(value, k):
        return value if k == 0 else value * shape[k]

    def of_order(value, k):
        return value[ORDER_OF[k] * feat : (ORDER_OF[k] + 1) * feat]

    for k in range(9):
        contrib_ref[k * feat : (k + 1) * feat] = times(of_order(weight, k), k).astype(BF16)
    for d in range(len(SPAN)):
        at = slice(d * pair_len, (d + 1) * pair_len)
        gath_ref[:, at] = dot(contrib_ref[:, at], same_ref[d])
    sums = [None, None, None]
    for k in range(9):
        term = times(gath_ref[k * feat : (k + 1) * feat], k)
        order = ORDER_OF[k]
        sums[order] = term if sums[order] is None else sums[order] + term
    sums = jnp.concatenate(sums, 0)
    invariant = (2.0 * weight * sums).astype(BF16)
    w_lat = w_lat_ref[...]
    joined = jnp.concatenate([half, invariant], 0)
    update, slope2 = silu_parts(dot_rows(w_lat, joined))
    refined = (latent + update).astype(BF16)
    w_out = jnp.broadcast_to(w_out_ref[...].astype(F32), (8, lat)).T[:, 0:1]
    raw_energy = jnp.sum(refined.astype(F32) * w_out, axis=0, keepdims=True)
    energy = scaled * raw_energy

    d_refined = scaled * w_out
    d_joined = dot(w_lat, (d_refined * slope2).astype(BF16))
    d_inv2 = 2.0 * d_joined[lat:]
    d_weight = d_inv2 * sums
    d_sums = d_inv2 * weight
    for k in range(9):
        contrib_ref[k * feat : (k + 1) * feat] = times(of_order(d_sums, k), k).astype(BF16)
    back = jnp.concatenate(
        [
            dot(contrib_ref[:, d * pair_len : (d + 1) * pair_len], same_ref[d])
            for d in range(len(SPAN))
        ],
        1,
    )
    d_shape = [None] * 9
    d_order = [None, None, None]
    for k in range(9):
        here = back[k * feat : (k + 1) * feat]
        order = ORDER_OF[k]
        term = times(here, k)
        d_order[order] = term if d_order[order] is None else d_order[order] + term
        if k:
            both = of_order(d_sums, k) * gath_ref[k * feat : (k + 1) * feat] + of_order(weight, k) * here
            d_shape[k] = jnp.sum(both, axis=0, keepdims=True)
    d_weight = d_weight + jnp.concatenate(d_order, 0)
    d_scaled = raw_energy + jnp.sum(d_weight * raw, axis=0, keepdims=True)
    d_latent = d_refined + d_joined[:lat] + dot_rows(w_env_ref[...], (d_weight * scaled).astype(BF16))
    d_pre = d_latent * slope
    p1, p2 = parts(d_pre, 2)
    low_half = dot(jnp.concatenate([w1, w2], 0), p1)
    d_basis = low_half[0:8] + low_half[8:16] + dot(w1, p2)

    along = jnp.sum(d_basis * sine, axis=0, keepdims=True)
    turned = jnp.sum(d_basis * cosine * ns, axis=0, keepdims=True)
    d_env = along * inv + mask * d_scaled
    dx = (
        ROOT3 * d_shape[1]
        + ROOT15 * (uy * d_shape[4] + uz * d_shape[7] + ux * d_shape[8])
        - ROOT5 * ux * d_shape[6]
    )
    dy = (
        ROOT3 * d_shape[2]
        + ROOT15 * (ux * d_shape[4] + uz * d_shape[5] - uy * d_shape[8])
        - ROOT5 * uy * d_shape[6]
    )
    dz = (
        ROOT3 * d_shape[3]
        + ROOT15 * (uy * d_shape[5] + ux * d_shape[7])
        + 2.0 * ROOT5 * uz * d_shape[6]
    )
    d_inv = along * env + dx * rx + dy * ry + dz * rz
    d_dist = turned * (math.pi / CUTOFF) * scale - d_inv * inv * inv
    d_squared = 0.5 * inv * d_dist - (2.0 / (CUTOFF * CUTOFF)) * slack * d_env
    gx = dx * inv + 2.0 * rx * d_squared
    gy = dy * inv + 2.0 * ry * d_squared
    gz = dz * inv + 2.0 * rz * d_squared
    half_energy = 0.5 * energy
    rows4 = [gx, gy, gz, half_energy]
    values = jnp.concatenate(rows4 + rows4, 0)
    rows = lax.broadcasted_iota(jnp.int32, (8, width), 0)
    flipped = jnp.where((rows & 3) == 3, values, -values)
    back_minus, back_plus = [], []
    for d, a in enumerate(SPAN):
        at = slice(d * pair_len, (d + 1) * pair_len)
        groups = [2 + DIRS.index((a, -1)), 2 + DIRS.index((a, 1))]
        groups += [2 + DIRS.index((a, 0))] if a else [0, 1]
        terms = scatter(flipped[:, at], neigh_hots[d], neigh_highs[d], groups)
        back_minus.append(terms[0:8])
        back_plus.append(terms[8:16])
        if a:
            own_ref[8 * (d // 2) : 8 * (d // 2) + 8] = terms[16:24]
        else:
            local_ref[...] = terms[16:32] + scatter(values[:, at], own_hot, own_high, (0, 1))
    for d in range(len(SPAN)):
        at = slice(8 * d, 8 * d + 8)
        back_far_ref[at] = jnp.where(even_n, back_plus[d], back_minus[d])
        back_near_ref[at] = jnp.where(even_n, back_minus[d], back_plus[d])


def collect_kernel(local_ref, own_ref, raw_ref, up_ref, low_ref, forces_ref, energy_ref):
    even_n = lax.axis_index("inner") % 2 == 0
    plus = jnp.where(even_n, low_ref[...], up_ref[...])
    minus = jnp.where(even_n, up_ref[...], low_ref[...])
    lists_low = raw_ref[0, LISTS : LISTS + 8].astype(jnp.int32)
    lists_high = raw_ref[0, LISTS + 8 : LISTS + 16].astype(jnp.int32)
    rows = lax.broadcasted_iota(jnp.int32, (8, LANES), 0)
    ids, values = [], []
    for k, (dx, dy) in enumerate(DIRS):
        ids += [lists_low[k : k + 1], lists_high[k : k + 1]]
        if dy == 0:
            at = 8 * ((dx + 1) // 2)
            tile = own_ref[at : at + 8]
        else:
            at = 8 * (dx + 1)
            tile = (minus if dy < 0 else plus)[at : at + 8]
        turned = pltpu.roll(tile, 4, 0)
        values += [jnp.where(rows < 4, tile, turned), jnp.where(rows < 4, turned, tile)]
    ids = jnp.concatenate(ids, 1)
    values = jnp.concatenate(values, 1)
    total = local_ref[...] + scatter(values, onehot_low(ids & 127), ids >> 7, (0, 1))
    for j in range(4):
        forces_ref[:, j * LANES : (j + 1) * LANES] = total[4 * j : 4 * j + 3]
        energy_ref[:, j * LANES : (j + 1) * LANES] = total[4 * j + 3 : 4 * j + 4]


def on_device(
    positions,
    species,
    send_lists,
    centers,
    neighbours,
    live_blocks,
    w_rad,
    emb_center,
    emb_neigh,
    w_env,
    w_lat,
    w_out,
):
    pair_len = centers.shape[0]
    atom_count = positions.shape[1]
    feat = w_env.shape[1] // 3
    width = len(SPAN) * pair_len
    chunks = pair_len // LANES

    def rows(count):
        return jax.ShapeDtypeStruct((count, LANES), F32)

    packed = pl.pallas_call(
        pack_kernel,
        out_shape=jax.ShapeDtypeStruct((lax.axis_size("outer"), PACKED, LANES), F32),
        in_specs=[pl.BlockSpec(memory_space=pltpu.HBM)] * 5
        + [pl.BlockSpec(memory_space=pltpu.SMEM)],
        scratch_shapes=[
            pltpu.VMEM(positions.shape, F32),
            pltpu.VMEM((1, atom_count), jnp.int32),
            pltpu.VMEM(send_lists.shape, jnp.int32),
            pltpu.VMEM((chunks, LANES), jnp.int32),
            pltpu.VMEM((chunks, LANES), jnp.int32),
            pltpu.SemaphoreType.DMA((5,)),
        ],
        compiler_params=SMALL,
        name="pack_domain",
    )(
        *(
            pltpu.with_memory_space_constraint(value, pltpu.HBM)
            for value in (
                positions,
                species.reshape(1, atom_count),
                send_lists,
                centers.reshape(chunks, LANES),
                neighbours.reshape(chunks, LANES),
            )
        ),
        live_blocks,
    )
    raw = all_rows(packed)
    far, near, mid = pl.pallas_call(
        sends_kernel,
        out_shape=[rows(72), rows(72), rows(48)],
        compiler_params=SMALL,
        name="gather_sends",
    )(raw)
    up = exchange(far, "inner", 1)
    low = exchange(near, "inner", 0)
    local, own, far, near = pl.pallas_call(
        lambda *refs: pair_kernel(feat, pair_len, *refs),
        out_shape=[rows(16), rows(16), rows(24), rows(24)],
        scratch_shapes=[
            pltpu.VMEM((len(SPAN), pair_len, pair_len), BF16),
            pltpu.VMEM((9 * feat, width), BF16),
            pltpu.VMEM((9 * feat, width), F32),
        ],
        compiler_params=LARGE,
        name="pair_terms",
    )(raw, mid, up, low, w_rad, emb_center, emb_neigh, w_env.T, w_lat, w_out.reshape(1, -1))
    up = exchange(far, "inner", 1)
    low = exchange(near, "inner", 0)
    forces, energy = pl.pallas_call(
        collect_kernel,
        out_shape=[
            jax.ShapeDtypeStruct((3, atom_count), F32),
            jax.ShapeDtypeStruct((1, atom_count), F32),
        ],
        compiler_params=SMALL,
        name="collect_terms",
    )(local, own, packed, up, low)
    return forces, energy.reshape(atom_count)


def solution(mesh):
    return jax.shard_map(
        on_device,
        mesh=mesh,
        in_specs=(
            P(None, AXES),
            P(AXES),
            P(None, AXES),
            P(AXES),
            P(AXES),
            P(AXES),
            P(),
            P(),
            P(),
            P(),
            P(),
            P(),
        ),
        out_specs=(P(None, AXES), P(AXES)),
        check_vma=False,
    )
```

```python
import math

import jax
import jax.numpy as jnp
from jax import lax
from jax.experimental import pallas as pl
from jax.experimental.pallas import tpu as pltpu
from jax.sharding import PartitionSpec as P

AXES = ("outer", "inner")
CUTOFF = 6.0
ROOT3 = math.sqrt(3.0)
ROOT5 = math.sqrt(5.0)
ROOT15 = math.sqrt(15.0)
LANES = 128
F32 = jnp.float32
BF16 = jnp.bfloat16
SMALL = pltpu.CompilerParams(vmem_limit_bytes=8 * 1024 * 1024)
LARGE = pltpu.CompilerParams(vmem_limit_bytes=32 * 1024 * 1024)
DIRS = ((-1, -1), (-1, 0), (-1, 1), (0, -1), (0, 1), (1, -1), (1, 0), (1, 1))
SPAN = (-1, 0, 1)
TABLE, LISTS, CENTERS, NEIGH, PACKED = 0, 16, 32, 40, 48
LIVE = 38
ORDER_OF = (0, 1, 1, 1, 2, 2, 2, 2, 2)


def exchange(block, along, parity, step=1):
    outer_len = lax.axis_size("outer")
    inner_len = lax.axis_size("inner")

    def partner(i, count):
        return (i + step if i // step % 2 == parity else i - step) % count

    route = []
    for o in range(outer_len):
        for n in range(inner_len):
            if along == "outer":
                there = (partner(o, outer_len), n)
            else:
                there = (o, partner(n, inner_len))
            route.append((o * inner_len + n, there[0] * inner_len + there[1]))
    return lax.ppermute(block, AXES, route)


def dot(lhs, rhs):
    return jnp.dot(lhs, rhs, preferred_element_type=F32)


def dot_rows(lhs, rhs):
    return lax.dot_general(lhs, rhs, (((0,), (0,)), ((), ())), preferred_element_type=F32)


def parts(value, count):
    out = []
    for _ in range(count):
        piece = value.astype(BF16)
        out.append(piece)
        value = value - piece.astype(F32)
    return out


def hits(left, right):
    return jnp.where(left == right, jnp.ones((), BF16), jnp.zeros((), BF16))


def down_lanes(row):
    return jnp.broadcast_to(row, (LANES, LANES)).T.astype(BF16)


def onehot_low(low_row):
    rows = lax.broadcasted_iota(jnp.int32, (LANES, low_row.shape[1]), 0).astype(F32).astype(BF16)
    return hits(rows, low_row.astype(F32).astype(BF16))


def high_mask(high_row, group):
    rows = lax.broadcasted_iota(jnp.int32, (8, high_row.shape[1]), 0)
    return high_row == 2 * group + jnp.where(rows >= 4, 1, 0)


def gather(table, low_hot, high_row):
    size = table.shape[0]
    found = dot(jnp.concatenate(parts(table, 3), 0), low_hot)
    found = found[0:size] + found[size : 2 * size] + found[2 * size :]
    total = None
    for group in range(size // 8):
        term = jnp.where(high_mask(high_row, group), found[8 * group : 8 * group + 8], 0.0)
        total = term if total is None else total + term
    return total + pltpu.roll(total, 4, 0)


def scatter(values, low_hot_t, high_row, groups):
    spread = [jnp.where(high_mask(high_row, group), values, 0.0) for group in groups]
    spread = jnp.concatenate(spread, 0)
    size = 8 * len(groups)
    summed = dot(jnp.concatenate(parts(spread, 2), 0), low_hot_t)
    return summed[0:size] + summed[size:]


def pack_kernel(
    pos_hbm,
    spec_hbm,
    lists_hbm,
    centers_hbm,
    neigh_hbm,
    live_ref,
    out_ref,
    pos,
    spec,
    lists,
    centers,
    neigh,
    sems,
):
    fetched = []
    for j, (src, dst) in enumerate(
        (
            (pos_hbm, pos),
            (spec_hbm, spec),
            (lists_hbm, lists),
            (centers_hbm, centers),
            (neigh_hbm, neigh),
        )
    ):
        copy = pltpu.make_async_copy(src, dst, sems.at[j])
        copy.start()
        fetched.append(copy)
    for copy in fetched:
        copy.wait()
    rows = []
    for j in range(4):
        at = slice(j * LANES, (j + 1) * LANES)
        rows.append(pos[:, at])
        rows.append(spec[:, at].astype(F32))
    ids = lists[...].astype(F32)
    rest = ids.shape[1] - LANES
    rows.append(ids[:, 0:LANES])
    rows.append(jnp.concatenate([ids[:, LANES:], jnp.zeros((8, LANES - rest), F32)], 1))
    rows.append(centers[...].astype(F32))
    rows.append(jnp.full((1, LANES), live_ref[0].astype(F32)))
    rows.append(jnp.zeros((1, LANES), F32))
    rows.append(neigh[...].astype(F32))
    rows.append(jnp.zeros((2, LANES), F32))
    out_ref[...] = jnp.concatenate(rows, 0)


def weights_kernel(
    w_rad_hbm,
    emb_center_hbm,
    emb_neigh_hbm,
    w_env_hbm,
    w_lat_hbm,
    w_out_hbm,
    front_ref,
    w_env_ref,
    w_lat_ref,
    w_out_ref,
    w_rad,
    emb_center,
    emb_neigh,
    w_out,
    sems,
):
    fetched = []
    for j, (src, dst) in enumerate(
        (
            (w_rad_hbm, w_rad),
            (emb_center_hbm, emb_center),
            (emb_neigh_hbm, emb_neigh),
            (w_env_hbm, w_env_ref),
            (w_lat_hbm, w_lat_ref),
            (w_out_hbm, w_out),
        )
    ):
        copy = pltpu.make_async_copy(src, dst, sems.at[j])
        copy.start()
        fetched.append(copy)
    for copy in fetched:
        copy.wait()
    lat = w_lat_ref.shape[1]
    w1, w2, w3 = parts(w_rad[...], 3)
    none = jnp.zeros((1, lat), BF16)
    front_ref[...] = jnp.concatenate(
        [w1, w2, w1, w3, w2, w1, emb_center[...], none, emb_neigh[...], none], 0
    )
    w_lat_ref[lat:] = w_lat_ref[lat:] * jnp.full((), 2.0, BF16)
    w_out_ref[...] = jnp.broadcast_to(w_out[...], (16, lat))


def tile_of(a, dx):
    return 3 * (a + 1) + dx + 1


def sends_kernel(
    own_ref, near2_ref, near1_ref, far1_ref, far2_ref, _, far_ref, near_ref, mid_ref, raw_ref
):
    even_n = lax.axis_index("inner") % 2 == 0
    outer = lax.axis_index("outer")
    even_o = outer % 2 == 0
    even_o2 = outer // 2 % 2 == 0
    by_source = {
        -2: jnp.where(even_o2, far2_ref[...], near2_ref[...]),
        -1: jnp.where(even_o, far1_ref[...], near1_ref[...]),
        0: own_ref[...],
        1: jnp.where(even_o, near1_ref[...], far1_ref[...]),
        2: jnp.where(even_o2, near2_ref[...], far2_ref[...]),
    }
    for d, a in enumerate(SPAN):
        raw_ref[d] = by_source[a]
    rows = lax.broadcasted_iota(jnp.int32, (8, LANES), 0)
    for source in range(-2, 3):
        raw = by_source[source]
        wanted = [
            k for k in range(8) if abs(source + DIRS[k][0]) <= 1
        ]
        low = raw[LISTS : LISTS + 8].astype(jnp.int32)
        high = raw[LISTS + 8 : LISTS + 16].astype(jnp.int32)
        ids = [part[k : k + 1] for k in wanted for part in (low, high)]
        ids = jnp.concatenate(ids, 1)
        taken = gather(raw[TABLE : TABLE + 16], onehot_low(ids & 127), ids >> 7)
        tiles = {}
        for j, k in enumerate(wanted):
            at = 2 * j * LANES
            tiles[k] = jnp.where(
                rows < 4, taken[:, at : at + LANES], taken[:, at + LANES : at + 2 * LANES]
            )
        for dx in SPAN:
            a = source + dx
            if abs(a) > 1:
                continue
            t = tile_of(a, dx)
            minus, plus = tiles[DIRS.index((dx, -1))], tiles[DIRS.index((dx, 1))]
            far_ref[8 * t : 8 * t + 8] = jnp.where(even_n, minus, plus)
            near_ref[8 * t : 8 * t + 8] = jnp.where(even_n, plus, minus)
            if dx:
                m = 2 * (a + 1) + (dx + 1) // 2
                mid_ref[8 * m : 8 * m + 8] = tiles[DIRS.index((dx, 0))]


def silu_parts(pre):
    sig = 0.5 * jnp.tanh(0.5 * pre) + 0.5
    act = pre * sig
    return act, sig + act - act * sig


def half_turns(value):
    whole = jnp.floor(value + 0.5)
    rest = (value - whole) * math.pi
    sign = 1.0 - 2.0 * (whole - 2.0 * jnp.floor(whole * 0.5))
    r2 = rest * rest
    sine, cosine = -1.0 / 39916800, 1.0 / 479001600
    for term in (1.0 / 362880, -1.0 / 5040, 1.0 / 120, -1.0 / 6, 1.0):
        sine = term + r2 * sine
    for term in (-1.0 / 3628800, 1.0 / 40320, -1.0 / 720, 1.0 / 24, -0.5, 1.0):
        cosine = term + r2 * cosine
    return sign * rest * sine, sign * cosine


def pair_kernel(
    feat,
    pair_len,
    raw_ref,
    mid_ref,
    up_ref,
    low_ref,
    front_ref,
    w_env_ref,
    w_lat_ref,
    w_out_ref,
    local_ref,
    own_ref,
    back_far_ref,
    back_near_ref,
    same_ref,
    hot_t_ref,
    contrib_ref,
    gath_ref,
    back_ref,
):
    chunks = pair_len // LANES
    lat = w_lat_ref.shape[1]
    even_n = lax.axis_index("inner") % 2 == 0
    lanes = lax.broadcasted_iota(jnp.int32, (1, LANES), 1).astype(F32).astype(BF16)

    front = front_ref[...]
    w1, w2 = front[0:8], front[8:16]
    w_env = w_env_ref[...]
    w_lat = w_lat_ref[...]
    w_out = w_out_ref[0:8].astype(F32).T[:, 0:1]

    def as_row(tile):
        return jnp.concatenate([tile[i : i + 1] for i in range(chunks)], 1)

    def onehot_t(low_tile):
        return jnp.concatenate(
            [hits(down_lanes(low_tile[i : i + 1].astype(F32)), lanes) for i in range(chunks)], 0
        )

    def feat_rows(k):
        return slice(k * feat, (k + 1) * feat)

    def of_order(value, k):
        return value[feat_rows(ORDER_OF[k])]

    def domain(d):
        return slice(d * pair_len, (d + 1) * pair_len)

    def build_same(d):
        shifted = raw_ref[d, CENTERS : CENTERS + 8] - 256.0
        across = shifted.astype(BF16)
        for i in range(chunks):
            down = down_lanes(shifted[i : i + 1])
            for j in range(chunks):
                same_ref[d, i * LANES : (i + 1) * LANES, j * LANES : (j + 1) * LANES] = hits(
                    down, across[j : j + 1]
                )

    def place(d):
        a = SPAN[d]
        raw = raw_ref.at[d]
        centers = raw[CENTERS : CENTERS + 8]
        table = [raw[TABLE : TABLE + 16]]
        for dx, dy in DIRS:
            t = 8 * tile_of(a, dx)
            if dy == 0:
                m = 8 * (2 * (a + 1) + (dx + 1) // 2)
                table.append(mid_ref[m : m + 8])
                continue
            by_low, by_up = low_ref[t : t + 8], up_ref[t : t + 8]
            if dy < 0:
                table.append(jnp.where(even_n, by_low, by_up))
            else:
                table.append(jnp.where(even_n, by_up, by_low))
        table = jnp.concatenate(table, 0)
        neigh = raw[NEIGH : NEIGH + 8].astype(jnp.int32)
        ghost = neigh - 512
        listed = (ghost * 745) >> 17
        entry = ghost - 176 * listed
        is_local = neigh < 512
        neigh_low = jnp.where(is_local, neigh & 127, entry & 127)
        hot_t_ref[d] = onehot_t(neigh_low)
        neigh_high = as_row(jnp.where(is_local, neigh >> 7, 4 + 2 * listed + (entry >> 7)))
        center_ids = as_row(centers.astype(jnp.int32))
        center_high = center_ids >> 7
        at_neigh = gather(table, onehot_low(as_row(neigh_low)), neigh_high)
        at_center = gather(table[0:16], onehot_low(center_ids & 127), center_high)
        if a == 0:
            hot_t_ref[len(SPAN)] = onehot_t(centers.astype(jnp.int32) & 127)
        block = lax.broadcasted_iota(jnp.int32, (1, pair_len), 1) // 128
        mask = jnp.where(block.astype(F32) < raw[LIVE : LIVE + 1, 0:1], 1.0, 0.0)
        return at_neigh, at_center, mask, neigh_high, center_high

    placed = [place(d) for d in range(len(SPAN))]
    at_neigh, at_center, mask = (jnp.concatenate([p[i] for p in placed], 1) for i in range(3))
    width = mask.shape[1]
    moved = at_neigh - at_center
    rx, ry, rz = moved[0:1], moved[1:2], moved[2:3]
    squared = rx * rx + ry * ry + rz * rz + 1.0
    inv = lax.rsqrt(squared)
    dist = squared * inv
    ux, uy, uz = rx * inv, ry * inv, rz * inv
    slack = 1.0 - squared * (1.0 / (CUTOFF * CUTOFF))
    env = slack * slack
    scaled = env * mask
    ns = (lax.broadcasted_iota(jnp.int32, (8, width), 0) + 1).astype(F32)
    sine, cosine = half_turns(ns * (dist * (1.0 / CUTOFF)))
    scale = inv * env
    kinds = lax.broadcasted_iota(jnp.int32, (8, width), 0).astype(F32)
    hot_center = jnp.where(at_center[3:4] == kinds, 1.0, 0.0).astype(BF16)
    hot_neigh = jnp.where(at_neigh[3:4] == kinds, 1.0, 0.0).astype(BF16)
    b1, b2, b3 = parts(sine * scale, 3)
    pre = dot_rows(front, jnp.concatenate([b1, b1, b2, b1, b2, b3, hot_center, hot_neigh], 0))
    for d in range(len(SPAN)):
        build_same(d)
    latent, slope = silu_parts(pre)
    half = latent.astype(BF16)
    raw = dot(w_env, half)
    weight = raw * scaled
    shape = [
        None,
        ROOT3 * ux,
        ROOT3 * uy,
        ROOT3 * uz,
        ROOT15 * ux * uy,
        ROOT15 * uy * uz,
        0.5 * ROOT5 * (2.0 * uz * uz - ux * ux - uy * uy),
        ROOT15 * ux * uz,
        0.5 * ROOT15 * (ux * ux - uy * uy),
    ]
    shape_half = [None] + [row.astype(BF16) for row in shape[1:]]

    def spread_same(d, value, out_ref):
        at = domain(d)
        value = value[:, at]
        for k in range(9):
            rows = of_order(value, k)
            contrib_ref[d, feat_rows(k)] = (rows if k == 0 else rows * shape[k][:, at]).astype(BF16)
        out_ref[d] = dot(contrib_ref[d], same_ref[d])

    def gathered_sums(d, in_ref):
        at = domain(d)
        sums = [None, None, None]
        for k in range(9):
            term = in_ref[d, feat_rows(k)]
            if k:
                term = term * shape[k][:, at]
            order = ORDER_OF[k]
            sums[order] = term if sums[order] is None else sums[order] + term
        return jnp.concatenate(sums, 0)

    for d in range(len(SPAN)):
        spread_same(d, weight, gath_ref)
    sums = jnp.concatenate([gathered_sums(d, gath_ref) for d in range(len(SPAN))], 1)
    joined = jnp.concatenate([half, (weight * sums).astype(BF16)], 0)
    update, slope2 = silu_parts(dot_rows(w_lat, joined))
    refined = (latent + update).astype(BF16)
    raw_energy = dot(w_out_ref[...], refined)[0:1]
    d_refined = scaled * w_out
    d_joined = dot(w_lat, (d_refined * slope2).astype(BF16))
    d_latent = d_refined + d_joined[:lat]
    d_inv = d_joined[lat:]
    d_weight = d_inv * sums
    d_sums = d_inv * weight
    for d in range(len(SPAN)):
        spread_same(d, d_sums, back_ref)
    d_order, d_shape = [], []
    for d in range(len(SPAN)):
        at = domain(d)
        d_order.append(gathered_sums(d, back_ref))
        here = []
        for k in range(1, 9):
            both = (
                of_order(d_sums, k)[:, at] * gath_ref[d, feat_rows(k)]
                + of_order(weight, k)[:, at] * back_ref[d, feat_rows(k)]
            )
            here.append(jnp.sum(both, axis=0, keepdims=True))
        d_shape.append(here)
    d_weight = d_weight + jnp.concatenate(d_order, 1)
    d_shape = [None] + [jnp.concatenate([here[k] for here in d_shape], 1) for k in range(8)]
    d_scaled = raw_energy + jnp.sum(d_weight * raw, axis=0, keepdims=True)
    d_latent = d_latent + scaled * dot_rows(w_env, d_weight.astype(BF16))
    d_pre = (d_latent * slope).astype(BF16)
    d_basis = dot(jnp.concatenate([w1, w2], 0), d_pre)
    d_basis = d_basis[0:8] + d_basis[8:16]

    along = jnp.sum(d_basis * sine, axis=0, keepdims=True)
    turned = jnp.sum(d_basis * cosine * ns, axis=0, keepdims=True)
    d_env = along * inv + mask * d_scaled
    dx = (
        ROOT3 * d_shape[1]
        + ROOT15 * (uy * d_shape[4] + uz * d_shape[7] + ux * d_shape[8])
        - ROOT5 * ux * d_shape[6]
    )
    dy = (
        ROOT3 * d_shape[2]
        + ROOT15 * (ux * d_shape[4] + uz * d_shape[5] - uy * d_shape[8])
        - ROOT5 * uy * d_shape[6]
    )
    dz = (
        ROOT3 * d_shape[3]
        + ROOT15 * (uy * d_shape[5] + ux * d_shape[7])
        + 2.0 * ROOT5 * uz * d_shape[6]
    )
    d_inv = along * env + dx * rx + dy * ry + dz * rz
    d_dist = turned * (math.pi / CUTOFF) * scale - d_inv * inv * inv
    d_squared = 0.5 * inv * d_dist - (2.0 / (CUTOFF * CUTOFF)) * slack * d_env
    gx = dx * inv + 2.0 * rx * d_squared
    gy = dy * inv + 2.0 * ry * d_squared
    gz = dz * inv + 2.0 * rz * d_squared
    rows4 = [gx, gy, gz, 0.5 * scaled * raw_energy]
    values = jnp.concatenate(rows4 + rows4, 0)
    rows = lax.broadcasted_iota(jnp.int32, (8, width), 0)
    flipped = jnp.where((rows & 3) == 3, values, -values)
    for d, a in enumerate(SPAN):
        neigh_high, center_high = placed[d][3:]
        groups = [2 + DIRS.index((a, -1)), 2 + DIRS.index((a, 1))]
        groups += [2 + DIRS.index((a, 0))] if a else [0, 1]
        terms = scatter(flipped[:, domain(d)], hot_t_ref[d], neigh_high, groups)
        minus, plus = terms[0:8], terms[8:16]
        at = slice(8 * d, 8 * d + 8)
        back_far_ref[at] = jnp.where(even_n, plus, minus)
        back_near_ref[at] = jnp.where(even_n, minus, plus)
        if a:
            own_ref[8 * (d // 2) : 8 * (d // 2) + 8] = terms[16:24]
        else:
            center_terms = scatter(values[:, domain(d)], hot_t_ref[len(SPAN)], center_high, (0, 1))
            local_ref[...] = terms[16:32] + center_terms


def collect_kernel(local_ref, own_ref, raw_ref, up_ref, low_ref, forces_ref, energy_ref):
    even_n = lax.axis_index("inner") % 2 == 0
    plus = jnp.where(even_n, low_ref[...], up_ref[...])
    minus = jnp.where(even_n, up_ref[...], low_ref[...])
    lists_low = raw_ref[LISTS : LISTS + 8].astype(jnp.int32)
    lists_high = raw_ref[LISTS + 8 : LISTS + 16].astype(jnp.int32)
    rows = lax.broadcasted_iota(jnp.int32, (8, LANES), 0)
    ids, values = [], []
    for k, (dx, dy) in enumerate(DIRS):
        ids += [lists_low[k : k + 1], lists_high[k : k + 1]]
        if dy == 0:
            at = 8 * ((dx + 1) // 2)
            tile = own_ref[at : at + 8]
        else:
            at = 8 * (dx + 1)
            tile = (minus if dy < 0 else plus)[at : at + 8]
        turned = pltpu.roll(tile, 4, 0)
        values += [jnp.where(rows < 4, tile, turned), jnp.where(rows < 4, turned, tile)]
    ids = jnp.concatenate(ids, 1)
    values = jnp.concatenate(values, 1)
    hot_t = []
    lanes = lax.broadcasted_iota(jnp.int32, (1, LANES), 1).astype(F32).astype(BF16)
    for k in range(len(DIRS)):
        for tile in (lists_low, lists_high):
            hot_t.append(hits(down_lanes((tile[k : k + 1] & 127).astype(F32)), lanes))
    total = local_ref[...] + scatter(values, jnp.concatenate(hot_t, 0), ids >> 7, (0, 1))
    for j in range(4):
        forces_ref[:, j * LANES : (j + 1) * LANES] = total[4 * j : 4 * j + 3]
        energy_ref[:, j * LANES : (j + 1) * LANES] = total[4 * j + 3 : 4 * j + 4]


def on_device(
    positions,
    species,
    send_lists,
    centers,
    neighbours,
    live_blocks,
    w_rad,
    emb_center,
    emb_neigh,
    w_env,
    w_lat,
    w_out,
):
    pair_len = centers.shape[0]
    atom_count = positions.shape[1]
    feat = w_env.shape[1] // 3
    lat = w_env.shape[0]
    chunks = pair_len // LANES

    def rows(count):
        return jax.ShapeDtypeStruct((count, LANES), F32)

    packed = pl.pallas_call(
        pack_kernel,
        out_shape=rows(PACKED),
        in_specs=[pl.BlockSpec(memory_space=pltpu.HBM)] * 5
        + [pl.BlockSpec(memory_space=pltpu.SMEM)],
        scratch_shapes=[
            pltpu.VMEM(positions.shape, F32),
            pltpu.VMEM((1, atom_count), jnp.int32),
            pltpu.VMEM(send_lists.shape, jnp.int32),
            pltpu.VMEM((chunks, LANES), jnp.int32),
            pltpu.VMEM((chunks, LANES), jnp.int32),
            pltpu.SemaphoreType.DMA((5,)),
        ],
        compiler_params=SMALL,
        name="pack_domain",
    )(
        *(
            pltpu.with_memory_space_constraint(value, pltpu.HBM)
            for value in (
                positions,
                species.reshape(1, atom_count),
                send_lists,
                centers.reshape(chunks, LANES),
                neighbours.reshape(chunks, LANES),
            )
        ),
        live_blocks,
    )
    weights = pl.pallas_call(
        weights_kernel,
        out_shape=[
            jax.ShapeDtypeStruct((64, lat), BF16),
            jax.ShapeDtypeStruct((w_env.shape[1], lat), BF16),
            jax.ShapeDtypeStruct(w_lat.shape, BF16),
            jax.ShapeDtypeStruct((16, lat), BF16),
        ],
        in_specs=[pl.BlockSpec(memory_space=pltpu.HBM)] * 6,
        scratch_shapes=[
            pltpu.VMEM(w_rad.shape, F32),
            pltpu.VMEM(emb_center.shape, BF16),
            pltpu.VMEM(emb_neigh.shape, BF16),
            pltpu.VMEM((1, lat), BF16),
            pltpu.SemaphoreType.DMA((6,)),
        ],
        compiler_params=SMALL,
        cost_estimate=pl.CostEstimate(flops=0, bytes_accessed=4_000_000, transcendentals=0),
        name="place_weights",
    )(
        *(
            pltpu.with_memory_space_constraint(value, pltpu.HBM)
            for value in (w_rad, emb_center, emb_neigh, w_env.T, w_lat, w_out.reshape(1, -1))
        )
    )
    far2 = exchange(packed, "outer", 1, 2)
    far1 = exchange(packed, "outer", 1)
    near1 = exchange(packed, "outer", 0)
    near2 = exchange(packed, "outer", 0, 2)
    far, near, mid, raw = pl.pallas_call(
        sends_kernel,
        out_shape=[
            rows(72),
            rows(72),
            rows(48),
            jax.ShapeDtypeStruct((len(SPAN), PACKED, LANES), F32),
        ],
        compiler_params=SMALL,
        name="gather_sends",
    )(packed, near2, near1, far1, far2, weights[3])
    up = exchange(far, "inner", 1)
    low = exchange(near, "inner", 0)
    local, own, far, near = pl.pallas_call(
        lambda *refs: pair_kernel(feat, pair_len, *refs),
        out_shape=[rows(16), rows(16), rows(24), rows(24)],
        scratch_shapes=[
            pltpu.VMEM((len(SPAN), pair_len, pair_len), BF16),
            pltpu.VMEM((len(SPAN) + 1, pair_len, LANES), BF16),
            pltpu.VMEM((len(SPAN), 9 * feat, pair_len), BF16),
            pltpu.VMEM((len(SPAN), 9 * feat, pair_len), F32),
            pltpu.VMEM((len(SPAN), 9 * feat, pair_len), F32),
        ],
        compiler_params=LARGE,
        name="pair_terms",
    )(raw, mid, up, low, *weights)
    up = exchange(far, "inner", 1)
    low = exchange(near, "inner", 0)
    forces, energy = pl.pallas_call(
        collect_kernel,
        out_shape=[
            jax.ShapeDtypeStruct((3, atom_count), F32),
            jax.ShapeDtypeStruct((1, atom_count), F32),
        ],
        compiler_params=SMALL,
        name="collect_terms",
    )(local, own, packed, up, low)
    return forces, energy.reshape(atom_count)


def solution(mesh):
    return jax.shard_map(
        on_device,
        mesh=mesh,
        in_specs=(
            P(None, AXES),
            P(AXES),
            P(None, AXES),
            P(AXES),
            P(AXES),
            P(AXES),
            P(),
            P(),
            P(),
            P(),
            P(),
            P(),
        ),
        out_specs=(P(None, AXES), P(AXES)),
        check_vma=False,
    )
```

```python
import math

import jax
import jax.numpy as jnp
from jax import lax
from jax.experimental import pallas as pl
from jax.experimental.pallas import tpu as pltpu
from jax.sharding import PartitionSpec as P

AXES = ("outer", "inner")
CUTOFF = 6.0
ROOT3 = math.sqrt(3.0)
ROOT5 = math.sqrt(5.0)
ROOT15 = math.sqrt(15.0)
LANES = 128
F32 = jnp.float32
BF16 = jnp.bfloat16
SMALL = pltpu.CompilerParams(vmem_limit_bytes=8 * 1024 * 1024)
LARGE = pltpu.CompilerParams(vmem_limit_bytes=32 * 1024 * 1024)
DIRS = ((-1, -1), (-1, 0), (-1, 1), (0, -1), (0, 1), (1, -1), (1, 0), (1, 1))
TABLE, LISTS, CENTERS, NEIGH, PACKED = 0, 16, 32, 40, 48
LIVE = 38
ORDER_OF = (0, 1, 1, 1, 2, 2, 2, 2, 2)


def permute(block, place):
    outer_len = lax.axis_size("outer")
    inner_len = lax.axis_size("inner")
    route = []
    for o in range(outer_len):
        for n in range(inner_len):
            there = place(o, n)
            if there is not None:
                to = there[0] % outer_len * inner_len + there[1] % inner_len
                route.append((o * inner_len + n, to))
    return lax.ppermute(block, AXES, route)


def swap_inner(block, parity):
    return permute(block, lambda o, n: (o, n + 1 if n % 2 == parity else n - 1))


def swap_outer(block, parity, rows):
    def place(o, n):
        return (o + 1 if o % 2 == parity else o - 1, n) if o in rows else None

    return permute(block, place)


def over_border(block):
    def place(o, n):
        return {1: (o - 2, n), 2: (o + 2, n)}.get(o % 4)

    return permute(block, place)


def dot(lhs, rhs):
    return jnp.dot(lhs, rhs, preferred_element_type=F32)


def dot_rows(lhs, rhs):
    return lax.dot_general(lhs, rhs, (((0,), (0,)), ((), ())), preferred_element_type=F32)


def parts(value, count):
    out = []
    for _ in range(count):
        piece = value.astype(BF16)
        out.append(piece)
        value = value - piece.astype(F32)
    return out


def hits(left, right):
    return jnp.where(left == right, jnp.ones((), BF16), jnp.zeros((), BF16))


def down_lanes(row):
    return jnp.broadcast_to(row, (LANES, LANES)).T.astype(BF16)


def onehot_low(low_row):
    rows = lax.broadcasted_iota(jnp.int32, (LANES, low_row.shape[1]), 0).astype(F32).astype(BF16)
    return hits(rows, low_row.astype(F32).astype(BF16))


def high_mask(high_row, group):
    rows = lax.broadcasted_iota(jnp.int32, (8, high_row.shape[1]), 0)
    return high_row == 2 * group + jnp.where(rows >= 4, 1, 0)


def gather(table, low_hot, high_row):
    size = table.shape[0]
    found = dot(jnp.concatenate(parts(table, 3), 0), low_hot)
    found = found[0:size] + found[size : 2 * size] + found[2 * size :]
    total = None
    for group in range(size // 8):
        term = jnp.where(high_mask(high_row, group), found[8 * group : 8 * group + 8], 0.0)
        total = term if total is None else total + term
    return total + pltpu.roll(total, 4, 0)


def scatter(values, low_hot_t, high_row, groups):
    spread = [jnp.where(high_mask(high_row, group), values, 0.0) for group in groups]
    spread = jnp.concatenate(spread, 0)
    size = 8 * len(groups)
    summed = dot(jnp.concatenate(parts(spread, 2), 0), low_hot_t)
    return summed[0:size] + summed[size:]


def pack_kernel(
    pos_hbm,
    spec_hbm,
    lists_hbm,
    centers_hbm,
    neigh_hbm,
    live_ref,
    out_ref,
    pos,
    spec,
    lists,
    centers,
    neigh,
    sems,
):
    fetched = []
    for j, (src, dst) in enumerate(
        (
            (pos_hbm, pos),
            (spec_hbm, spec),
            (lists_hbm, lists),
            (centers_hbm, centers),
            (neigh_hbm, neigh),
        )
    ):
        copy = pltpu.make_async_copy(src, dst, sems.at[j])
        copy.start()
        fetched.append(copy)
    for copy in fetched:
        copy.wait()
    rows = []
    for j in range(4):
        at = slice(j * LANES, (j + 1) * LANES)
        rows.append(pos[:, at])
        rows.append(spec[:, at].astype(F32))
    ids = lists[...].astype(F32)
    rest = ids.shape[1] - LANES
    rows.append(ids[:, 0:LANES])
    rows.append(jnp.concatenate([ids[:, LANES:], jnp.zeros((8, LANES - rest), F32)], 1))
    rows.append(centers[...].astype(F32))
    rows.append(jnp.full((1, LANES), live_ref[0].astype(F32)))
    rows.append(jnp.zeros((1, LANES), F32))
    rows.append(neigh[...].astype(F32))
    rows.append(jnp.zeros((2, LANES), F32))
    out_ref[...] = jnp.concatenate(rows, 0)


def weights_kernel(
    w_rad_hbm,
    emb_center_hbm,
    emb_neigh_hbm,
    w_env_hbm,
    w_lat_hbm,
    w_out_hbm,
    front_ref,
    w_env_ref,
    w_lat_ref,
    w_out_ref,
    w_rad,
    emb_center,
    emb_neigh,
    w_out,
    sems,
):
    fetched = []
    for j, (src, dst) in enumerate(
        (
            (w_rad_hbm, w_rad),
            (emb_center_hbm, emb_center),
            (emb_neigh_hbm, emb_neigh),
            (w_env_hbm, w_env_ref),
            (w_lat_hbm, w_lat_ref),
            (w_out_hbm, w_out),
        )
    ):
        copy = pltpu.make_async_copy(src, dst, sems.at[j])
        copy.start()
        fetched.append(copy)
    for copy in fetched:
        copy.wait()
    lat = w_lat_ref.shape[1]
    w1, w2, w3 = parts(w_rad[...], 3)
    none = jnp.zeros((1, lat), BF16)
    front_ref[...] = jnp.concatenate(
        [w1, w2, w1, w3, w2, w1, emb_center[...], none, emb_neigh[...], none], 0
    )
    w_lat_ref[lat:] = w_lat_ref[lat:] * jnp.full((), 2.0, BF16)
    w_out_ref[...] = jnp.broadcast_to(w_out[...], (16, lat))


def tile_at(extra, side):
    return 8 * (3 * extra + 1 - side)


def sends_kernel(
    own_ref, low_ref, border_ref, cross_ref, high_ref, _, far_ref, near_ref, mid_ref, raw_ref
):
    even_n = lax.axis_index("inner") % 2 == 0
    outer = lax.axis_index("outer")
    odd = outer % 2 == 1
    rows = lax.broadcasted_iota(jnp.int32, (8, LANES), 0)
    own, cross = own_ref[...], cross_ref[...]
    beside = jnp.where(outer < lax.axis_size("outer") // 2, low_ref[...], high_ref[...])
    raw_ref[0] = own
    raw_ref[1] = cross

    def tiles_of(raw, sides):
        halves = [raw[LISTS + 8 * i : LISTS + 8 * i + 8].astype(jnp.int32) for i in range(2)]
        names, ids = [], []
        for side in sides:
            if side == 0:
                picked = [half[3:5] for half in halves]
                names += [(0, -1), (0, 1)]
            else:
                upper = odd if side > 0 else jnp.logical_not(odd)
                picked = [jnp.where(upper, half[5:8], half[0:3]) for half in halves]
                names += [(side, dy) for dy in (-1, 0, 1)]
            for i in range(picked[0].shape[0]):
                ids += [picked[0][i : i + 1], picked[1][i : i + 1]]
        ids = jnp.concatenate(ids, 1)
        taken = gather(raw[TABLE : TABLE + 16], onehot_low(ids & 127), ids >> 7)
        tiles = {}
        for j, name in enumerate(names):
            at = 2 * j * LANES
            tiles[name] = jnp.where(
                rows < 4, taken[:, at : at + LANES], taken[:, at + LANES : at + 2 * LANES]
            )
        return tiles

    by_own = tiles_of(own, (1, 0))
    by_cross = tiles_of(cross, (0, -1))
    by_beside = tiles_of(beside, (1,))
    by_border = tiles_of(border_ref[...], (-1,))
    sources = ({1: by_beside, 0: by_own, -1: by_cross}, {1: by_own, 0: by_cross, -1: by_border})
    for extra in range(2):
        for side in (1, 0, -1):
            tiles = sources[extra][side]
            minus, plus = tiles[side, -1], tiles[side, 1]
            at = tile_at(extra, side)
            far_ref[at : at + 8] = jnp.where(even_n, minus, plus)
            near_ref[at : at + 8] = jnp.where(even_n, plus, minus)
            if side:
                m = 8 * (2 * extra + (1 - side) // 2)
                mid_ref[m : m + 8] = tiles[side, 0]


def silu_parts(pre):
    sig = 0.5 * jnp.tanh(0.5 * pre) + 0.5
    act = pre * sig
    return act, sig + act - act * sig


def half_turns(value):
    whole = jnp.floor(value + 0.5)
    rest = (value - whole) * math.pi
    sign = 1.0 - 2.0 * (whole - 2.0 * jnp.floor(whole * 0.5))
    r2 = rest * rest
    sine, cosine = -1.0 / 39916800, 1.0 / 479001600
    for term in (1.0 / 362880, -1.0 / 5040, 1.0 / 120, -1.0 / 6, 1.0):
        sine = term + r2 * sine
    for term in (-1.0 / 3628800, 1.0 / 40320, -1.0 / 720, 1.0 / 24, -0.5, 1.0):
        cosine = term + r2 * cosine
    return sign * rest * sine, sign * cosine


def pair_kernel(feat, pair_len, *refs):
    place = lax.axis_index("outer") % 4
    at_border = (place == 0) | (place == 3)
    pl.when(at_border)(lambda: pair_body(2, feat, pair_len, *refs))
    pl.when(jnp.logical_not(at_border))(lambda: pair_body(1, feat, pair_len, *refs))


def pair_body(
    count,
    feat,
    pair_len,
    raw_ref,
    mid_ref,
    up_ref,
    low_ref,
    front_ref,
    w_env_ref,
    w_lat_ref,
    w_out_ref,
    local_ref,
    edge_near_ref,
    edge_far_ref,
    back_far_ref,
    back_near_ref,
    same_ref,
    hot_t_ref,
    contrib_ref,
    gath_ref,
    back_ref,
):
    chunks = pair_len // LANES
    lat = w_lat_ref.shape[1]
    even_n = lax.axis_index("inner") % 2 == 0
    odd = lax.axis_index("outer") % 2 == 1
    lanes = lax.broadcasted_iota(jnp.int32, (1, LANES), 1).astype(F32).astype(BF16)

    front = front_ref[...]
    w1, w2 = front[0:8], front[8:16]
    w_env = w_env_ref[...]
    w_lat = w_lat_ref[...]
    w_out = w_out_ref[0:8].astype(F32).T[:, 0:1]

    def as_row(tile):
        return jnp.concatenate([tile[i : i + 1] for i in range(chunks)], 1)

    def onehot_t(low_tile):
        return jnp.concatenate(
            [hits(down_lanes(low_tile[i : i + 1].astype(F32)), lanes) for i in range(chunks)], 0
        )

    def feat_rows(k):
        return slice(k * feat, (k + 1) * feat)

    def of_order(value, k):
        return value[feat_rows(ORDER_OF[k])]

    def domain(d):
        return slice(d * pair_len, (d + 1) * pair_len)

    def build_same(d):
        shifted = raw_ref[d, CENTERS : CENTERS + 8] - 256.0
        across = shifted.astype(BF16)
        for i in range(chunks):
            down = down_lanes(shifted[i : i + 1])
            for j in range(chunks):
                same_ref[d, i * LANES : (i + 1) * LANES, j * LANES : (j + 1) * LANES] = hits(
                    down, across[j : j + 1]
                )

    def place(d):
        raw = raw_ref.at[d]
        centers = raw[CENTERS : CENTERS + 8]
        table = [raw[TABLE : TABLE + 16]]

        def ghost_tile(side, dy):
            if dy == 0:
                m = 8 * (2 * d + (1 - side) // 2)
                return mid_ref[m : m + 8]
            t = tile_at(d, side)
            by_low, by_up = low_ref[t : t + 8], up_ref[t : t + 8]
            return jnp.where(even_n, by_low, by_up) if dy < 0 else jnp.where(even_n, by_up, by_low)

        for dx, dy in DIRS:
            if dx == 0:
                table.append(ghost_tile(0, dy))
            else:
                table.append(jnp.where(odd, ghost_tile(dx, dy), ghost_tile(-dx, dy)))
        table = jnp.concatenate(table, 0)
        neigh = raw[NEIGH : NEIGH + 8].astype(jnp.int32)
        ghost = neigh - 512
        listed = (ghost * 745) >> 17
        entry = ghost - 176 * listed
        is_local = neigh < 512
        neigh_low = jnp.where(is_local, neigh & 127, entry & 127)
        hot_t_ref[d] = onehot_t(neigh_low)
        neigh_high = as_row(jnp.where(is_local, neigh >> 7, 4 + 2 * listed + (entry >> 7)))
        center_ids = as_row(centers.astype(jnp.int32))
        center_high = center_ids >> 7
        at_neigh = gather(table, onehot_low(as_row(neigh_low)), neigh_high)
        at_center = gather(table[0:16], onehot_low(center_ids & 127), center_high)
        if d == 0:
            hot_t_ref[2] = onehot_t(centers.astype(jnp.int32) & 127)
        block = lax.broadcasted_iota(jnp.int32, (1, pair_len), 1) // 128
        mask = jnp.where(block.astype(F32) < raw[LIVE : LIVE + 1, 0:1], 1.0, 0.0)
        return at_neigh, at_center, mask, neigh_high, center_high

    placed = [place(d) for d in range(count)]
    at_neigh, at_center, mask = (jnp.concatenate([p[i] for p in placed], 1) for i in range(3))
    width = mask.shape[1]
    moved = at_neigh - at_center
    rx, ry, rz = moved[0:1], moved[1:2], moved[2:3]
    squared = rx * rx + ry * ry + rz * rz + 1.0
    inv = lax.rsqrt(squared)
    dist = squared * inv
    ux, uy, uz = rx * inv, ry * inv, rz * inv
    slack = 1.0 - squared * (1.0 / (CUTOFF * CUTOFF))
    env = slack * slack
    scaled = env * mask
    ns = (lax.broadcasted_iota(jnp.int32, (8, width), 0) + 1).astype(F32)
    sine, cosine = half_turns(ns * (dist * (1.0 / CUTOFF)))
    scale = inv * env
    kinds = lax.broadcasted_iota(jnp.int32, (8, width), 0).astype(F32)
    hot_center = jnp.where(at_center[3:4] == kinds, 1.0, 0.0).astype(BF16)
    hot_neigh = jnp.where(at_neigh[3:4] == kinds, 1.0, 0.0).astype(BF16)
    b1, b2, b3 = parts(sine * scale, 3)
    pre = dot_rows(front, jnp.concatenate([b1, b1, b2, b1, b2, b3, hot_center, hot_neigh], 0))
    for d in range(count):
        build_same(d)
    latent, slope = silu_parts(pre)
    half = latent.astype(BF16)
    raw = dot(w_env, half)
    weight = raw * scaled
    shape = [
        None,
        ROOT3 * ux,
        ROOT3 * uy,
        ROOT3 * uz,
        ROOT15 * ux * uy,
        ROOT15 * uy * uz,
        0.5 * ROOT5 * (2.0 * uz * uz - ux * ux - uy * uy),
        ROOT15 * ux * uz,
        0.5 * ROOT15 * (ux * ux - uy * uy),
    ]
    shape_half = [None] + [row.astype(BF16) for row in shape[1:]]

    def spread_same(d, value, out_ref):
        at = domain(d)
        value = value[:, at]
        for k in range(9):
            rows = of_order(value, k)
            contrib_ref[d, feat_rows(k)] = (rows if k == 0 else rows * shape[k][:, at]).astype(BF16)
        out_ref[d] = dot(contrib_ref[d], same_ref[d])

    def gathered_sums(d, in_ref):
        at = domain(d)
        sums = [None, None, None]
        for k in range(9):
            term = in_ref[d, feat_rows(k)]
            if k:
                term = term * shape[k][:, at]
            order = ORDER_OF[k]
            sums[order] = term if sums[order] is None else sums[order] + term
        return jnp.concatenate(sums, 0)

    for d in range(count):
        spread_same(d, weight, gath_ref)
    sums = jnp.concatenate([gathered_sums(d, gath_ref) for d in range(count)], 1)
    joined = jnp.concatenate([half, (weight * sums).astype(BF16)], 0)
    update, slope2 = silu_parts(dot_rows(w_lat, joined))
    refined = (latent + update).astype(BF16)
    raw_energy = dot(w_out_ref[...], refined)[0:1]
    d_refined = scaled * w_out
    d_joined = dot(w_lat, (d_refined * slope2).astype(BF16))
    d_latent = d_refined + d_joined[:lat]
    d_inv = d_joined[lat:]
    d_weight = d_inv * sums
    d_sums = d_inv * weight
    for d in range(count):
        spread_same(d, d_sums, back_ref)
    d_order, d_shape = [], []
    for d in range(count):
        at = domain(d)
        d_order.append(gathered_sums(d, back_ref))
        here = []
        for k in range(1, 9):
            both = (
                of_order(d_sums, k)[:, at] * gath_ref[d, feat_rows(k)]
                + of_order(weight, k)[:, at] * back_ref[d, feat_rows(k)]
            )
            here.append(jnp.sum(both, axis=0, keepdims=True))
        d_shape.append(here)
    d_weight = d_weight + jnp.concatenate(d_order, 1)
    d_shape = [None] + [jnp.concatenate([here[k] for here in d_shape], 1) for k in range(8)]
    d_scaled = raw_energy + jnp.sum(d_weight * raw, axis=0, keepdims=True)
    d_latent = d_latent + scaled * dot_rows(w_env, d_weight.astype(BF16))
    d_pre = (d_latent * slope).astype(BF16)
    d_basis = dot(jnp.concatenate([w1, w2], 0), d_pre)
    d_basis = d_basis[0:8] + d_basis[8:16]

    along = jnp.sum(d_basis * sine, axis=0, keepdims=True)
    turned = jnp.sum(d_basis * cosine * ns, axis=0, keepdims=True)
    d_env = along * inv + mask * d_scaled
    dx = (
        ROOT3 * d_shape[1]
        + ROOT15 * (uy * d_shape[4] + uz * d_shape[7] + ux * d_shape[8])
        - ROOT5 * ux * d_shape[6]
    )
    dy = (
        ROOT3 * d_shape[2]
        + ROOT15 * (ux * d_shape[4] + uz * d_shape[5] - uy * d_shape[8])
        - ROOT5 * uy * d_shape[6]
    )
    dz = (
        ROOT3 * d_shape[3]
        + ROOT15 * (uy * d_shape[5] + ux * d_shape[7])
        + 2.0 * ROOT5 * uz * d_shape[6]
    )
    d_inv = along * env + dx * rx + dy * ry + dz * rz
    d_dist = turned * (math.pi / CUTOFF) * scale - d_inv * inv * inv
    d_squared = 0.5 * inv * d_dist - (2.0 / (CUTOFF * CUTOFF)) * slack * d_env
    gx = dx * inv + 2.0 * rx * d_squared
    gy = dy * inv + 2.0 * ry * d_squared
    gz = dz * inv + 2.0 * rz * d_squared
    rows4 = [gx, gy, gz, 0.5 * scaled * raw_energy]
    values = jnp.concatenate(rows4 + rows4, 0)
    rows = lax.broadcasted_iota(jnp.int32, (8, width), 0)
    flipped = jnp.where((rows & 3) == 3, values, -values)
    first = jnp.where(odd, 5, 0)

    def groups_of(side):
        return [2 + (first if side > 0 else 5 - first) + i for i in range(3)]

    neigh_high, center_high = placed[0][3:]
    groups = [0, 1, 2 + 3, 2 + 4] + groups_of(1) + (groups_of(-1) if count == 1 else [])
    terms = scatter(flipped[:, domain(0)], hot_t_ref[0], neigh_high, groups)
    center_terms = scatter(values[:, domain(0)], hot_t_ref[2], center_high, (0, 1))
    local_ref[...] = terms[0:16] + center_terms
    tiles = [terms[8 * i : 8 * i + 8] for i in range(2, len(groups))]
    if count == 2:
        terms = scatter(flipped[:, domain(1)], hot_t_ref[1], placed[1][3], groups_of(1))
        tiles += [terms[8 * i : 8 * i + 8] for i in range(3)]
    edge_near_ref[...] = tiles[3]
    edge_far_ref[...] = tiles[6]
    for j, (minus, plus) in enumerate(
        ((tiles[0], tiles[1]), (tiles[2], tiles[4]), (tiles[5], tiles[7]))
    ):
        at = slice(8 * j, 8 * j + 8)
        back_far_ref[at] = jnp.where(even_n, plus, minus)
        back_near_ref[at] = jnp.where(even_n, minus, plus)


def collect_kernel(
    local_ref,
    raw_ref,
    up_ref,
    low_ref,
    edge_far_ref,
    cross_ref,
    beside_ref,
    forces_ref,
    energy_ref,
):
    even_n = lax.axis_index("inner") % 2 == 0
    odd = lax.axis_index("outer") % 2 == 1
    place = lax.axis_index("outer") % 4
    at_border = (place == 0) | (place == 3)
    plus = jnp.where(even_n, low_ref[...], up_ref[...])
    minus = jnp.where(even_n, up_ref[...], low_ref[...])
    over = jnp.concatenate([minus[16:24], edge_far_ref[...], plus[16:24]], 0)
    toward = jnp.where(at_border, over, cross_ref[...])
    away = beside_ref[...]
    above = jnp.where(odd, toward, away)
    below = jnp.where(odd, away, toward)
    lists_low = raw_ref[LISTS : LISTS + 8].astype(jnp.int32)
    lists_high = raw_ref[LISTS + 8 : LISTS + 16].astype(jnp.int32)
    rows = lax.broadcasted_iota(jnp.int32, (8, LANES), 0)
    ids, values = [], []
    for k, (dx, dy) in enumerate(DIRS):
        ids += [lists_low[k : k + 1], lists_high[k : k + 1]]
        if dx == 0:
            tile = (minus if dy < 0 else plus)[0:8]
        else:
            at = 8 * (dy + 1)
            tile = (above if dx > 0 else below)[at : at + 8]
        turned = pltpu.roll(tile, 4, 0)
        values += [jnp.where(rows < 4, tile, turned), jnp.where(rows < 4, turned, tile)]
    ids = jnp.concatenate(ids, 1)
    values = jnp.concatenate(values, 1)
    hot_t = []
    lanes = lax.broadcasted_iota(jnp.int32, (1, LANES), 1).astype(F32).astype(BF16)
    for k in range(len(DIRS)):
        for tile in (lists_low, lists_high):
            hot_t.append(hits(down_lanes((tile[k : k + 1] & 127).astype(F32)), lanes))
    total = local_ref[...] + scatter(values, jnp.concatenate(hot_t, 0), ids >> 7, (0, 1))
    for j in range(4):
        forces_ref[:, j * LANES : (j + 1) * LANES] = total[4 * j : 4 * j + 3]
        energy_ref[:, j * LANES : (j + 1) * LANES] = total[4 * j + 3 : 4 * j + 4]


def on_device(
    positions,
    species,
    send_lists,
    centers,
    neighbours,
    live_blocks,
    w_rad,
    emb_center,
    emb_neigh,
    w_env,
    w_lat,
    w_out,
):
    pair_len = centers.shape[0]
    atom_count = positions.shape[1]
    feat = w_env.shape[1] // 3
    lat = w_env.shape[0]
    chunks = pair_len // LANES

    def rows(count):
        return jax.ShapeDtypeStruct((count, LANES), F32)

    packed = pl.pallas_call(
        pack_kernel,
        out_shape=rows(PACKED),
        in_specs=[pl.BlockSpec(memory_space=pltpu.HBM)] * 5
        + [pl.BlockSpec(memory_space=pltpu.SMEM)],
        scratch_shapes=[
            pltpu.VMEM(positions.shape, F32),
            pltpu.VMEM((1, atom_count), jnp.int32),
            pltpu.VMEM(send_lists.shape, jnp.int32),
            pltpu.VMEM((chunks, LANES), jnp.int32),
            pltpu.VMEM((chunks, LANES), jnp.int32),
            pltpu.SemaphoreType.DMA((5,)),
        ],
        compiler_params=SMALL,
        name="pack_domain",
    )(
        *(
            pltpu.with_memory_space_constraint(value, pltpu.HBM)
            for value in (
                positions,
                species.reshape(1, atom_count),
                send_lists,
                centers.reshape(chunks, LANES),
                neighbours.reshape(chunks, LANES),
            )
        ),
        live_blocks,
    )
    weights = pl.pallas_call(
        weights_kernel,
        out_shape=[
            jax.ShapeDtypeStruct((64, lat), BF16),
            jax.ShapeDtypeStruct((w_env.shape[1], lat), BF16),
            jax.ShapeDtypeStruct(w_lat.shape, BF16),
            jax.ShapeDtypeStruct((16, lat), BF16),
        ],
        in_specs=[pl.BlockSpec(memory_space=pltpu.HBM)] * 6,
        scratch_shapes=[
            pltpu.VMEM(w_rad.shape, F32),
            pltpu.VMEM(emb_center.shape, BF16),
            pltpu.VMEM(emb_neigh.shape, BF16),
            pltpu.VMEM((1, lat), BF16),
            pltpu.SemaphoreType.DMA((6,)),
        ],
        compiler_params=SMALL,
        cost_estimate=pl.CostEstimate(flops=0, bytes_accessed=4_000_000, transcendentals=0),
        name="place_weights",
    )(
        *(
            pltpu.with_memory_space_constraint(value, pltpu.HBM)
            for value in (w_rad, emb_center, emb_neigh, w_env.T, w_lat, w_out.reshape(1, -1))
        )
    )
    row_count = lax.axis_size("outer")
    low_half = range(row_count // 2)
    high_half = range(row_count // 2, row_count)
    beside_low = swap_outer(packed, 0, low_half)
    border = over_border(packed)
    cross = swap_outer(packed, 1, range(row_count))
    beside_high = swap_outer(packed, 0, high_half)
    far, near, mid, raw = pl.pallas_call(
        sends_kernel,
        out_shape=[
            rows(48),
            rows(48),
            rows(32),
            jax.ShapeDtypeStruct((2, PACKED, LANES), F32),
        ],
        compiler_params=SMALL,
        name="gather_sends",
    )(packed, beside_low, border, cross, beside_high, weights[3])
    up = swap_inner(far, 1)
    low = swap_inner(near, 0)
    local, edge_near, edge_far, far, near = pl.pallas_call(
        lambda *refs: pair_kernel(feat, pair_len, *refs),
        out_shape=[rows(16), rows(8), rows(8), rows(24), rows(24)],
        scratch_shapes=[
            pltpu.VMEM((2, pair_len, pair_len), BF16),
            pltpu.VMEM((3, pair_len, LANES), BF16),
            pltpu.VMEM((2, 9 * feat, pair_len), BF16),
            pltpu.VMEM((2, 9 * feat, pair_len), F32),
            pltpu.VMEM((2, 9 * feat, pair_len), F32),
        ],
        compiler_params=LARGE,
        name="pair_terms",
    )(raw, mid, up, low, *weights)
    up = swap_inner(far, 1)
    low = swap_inner(near, 0)
    even_n = lax.axis_index("inner") % 2 == 0
    plus = jnp.where(even_n, low, up)
    minus = jnp.where(even_n, up, low)
    inside = [o for o in range(row_count) if o % 4 in (1, 2)]
    cross = swap_outer(
        jnp.concatenate([minus[16:24], edge_far, plus[16:24]], 0), 1, inside
    )
    beside = swap_outer(
        jnp.concatenate([minus[8:16], edge_near, plus[8:16]], 0), 0, range(row_count)
    )
    forces, energy = pl.pallas_call(
        collect_kernel,
        out_shape=[
            jax.ShapeDtypeStruct((3, atom_count), F32),
            jax.ShapeDtypeStruct((1, atom_count), F32),
        ],
        compiler_params=SMALL,
        name="collect_terms",
    )(local, packed, up, low, edge_far, cross, beside)
    return forces, energy.reshape(atom_count)


def solution(mesh):
    return jax.shard_map(
        on_device,
        mesh=mesh,
        in_specs=(
            P(None, AXES),
            P(AXES),
            P(None, AXES),
            P(AXES),
            P(AXES),
            P(AXES),
            P(),
            P(),
            P(),
            P(),
            P(),
            P(),
        ),
        out_specs=(P(None, AXES), P(AXES)),
        check_vma=False,
    )
```

```python
import math

import jax
import jax.numpy as jnp
from jax import lax
from jax.experimental import pallas as pl
from jax.experimental.pallas import tpu as pltpu
from jax.sharding import PartitionSpec as P

AXES = ("outer", "inner")
CUTOFF = 6.0
ROOT3 = math.sqrt(3.0)
ROOT5 = math.sqrt(5.0)
ROOT15 = math.sqrt(15.0)
LANES = 128
F32 = jnp.float32
BF16 = jnp.bfloat16
SMALL = pltpu.CompilerParams(vmem_limit_bytes=8 * 1024 * 1024)
LARGE = pltpu.CompilerParams(vmem_limit_bytes=32 * 1024 * 1024)
DIRS = ((-1, -1), (-1, 0), (-1, 1), (0, -1), (0, 1), (1, -1), (1, 0), (1, 1))
TABLE, LISTS, CENTERS, NEIGH, PACKED = 0, 16, 32, 40, 48
LIVE = 38
ORDER_OF = (0, 1, 1, 1, 2, 2, 2, 2, 2)


def permute(block, place):
    outer_len = lax.axis_size("outer")
    inner_len = lax.axis_size("inner")
    route = []
    for o in range(outer_len):
        for n in range(inner_len):
            there = place(o, n)
            if there is not None:
                to = there[0] % outer_len * inner_len + there[1] % inner_len
                route.append((o * inner_len + n, to))
    return lax.ppermute(block, AXES, route)


def swap_inner(block, parity):
    return permute(block, lambda o, n: (o, n + 1 if n % 2 == parity else n - 1))


def swap_outer(block, parity, rows):
    def place(o, n):
        return (o + 1 if o % 2 == parity else o - 1, n) if o in rows else None

    return permute(block, place)


def over_border(block):
    def place(o, n):
        return {1: (o - 2, n), 2: (o + 2, n)}.get(o % 4)

    return permute(block, place)


def dot(lhs, rhs):
    return jnp.dot(lhs, rhs, preferred_element_type=F32)


def dot_rows(lhs, rhs):
    return lax.dot_general(lhs, rhs, (((0,), (0,)), ((), ())), preferred_element_type=F32)


def parts(value, count):
    out = []
    for _ in range(count):
        piece = value.astype(BF16)
        out.append(piece)
        value = value - piece.astype(F32)
    return out


def hits(left, right):
    return jnp.where(left == right, jnp.ones((), BF16), jnp.zeros((), BF16))


def down_lanes(row):
    return jnp.broadcast_to(row, (LANES, LANES)).T.astype(BF16)


def onehot_low(low_row):
    rows = lax.broadcasted_iota(jnp.int32, (LANES, low_row.shape[1]), 0).astype(F32).astype(BF16)
    return hits(rows, low_row.astype(F32).astype(BF16))


def high_mask(high_row, group):
    rows = lax.broadcasted_iota(jnp.int32, (8, high_row.shape[1]), 0)
    return high_row == 2 * group + jnp.where(rows >= 4, 1, 0)


def gather(table, low_hot, high_row):
    size = table.shape[0]
    found = dot(jnp.concatenate(parts(table, 3), 0), low_hot)
    found = found[0:size] + found[size : 2 * size] + found[2 * size :]
    total = None
    for group in range(size // 8):
        term = jnp.where(high_mask(high_row, group), found[8 * group : 8 * group + 8], 0.0)
        total = term if total is None else total + term
    return total + pltpu.roll(total, 4, 0)


def scatter(values, low_hot_t, high_row, groups):
    spread = [jnp.where(high_mask(high_row, group), values, 0.0) for group in groups]
    spread = jnp.concatenate(spread, 0)
    size = 8 * len(groups)
    summed = dot(jnp.concatenate(parts(spread, 2), 0), low_hot_t)
    return summed[0:size] + summed[size:]


def pack_kernel(
    pos_hbm,
    spec_hbm,
    lists_hbm,
    centers_hbm,
    neigh_hbm,
    live_ref,
    out_ref,
    pos,
    spec,
    lists,
    centers,
    neigh,
    sems,
):
    fetched = []
    for j, (src, dst) in enumerate(
        (
            (pos_hbm, pos),
            (spec_hbm, spec),
            (lists_hbm, lists),
            (centers_hbm, centers),
            (neigh_hbm, neigh),
        )
    ):
        copy = pltpu.make_async_copy(src, dst, sems.at[j])
        copy.start()
        fetched.append(copy)
    for copy in fetched:
        copy.wait()
    rows = []
    for j in range(4):
        at = slice(j * LANES, (j + 1) * LANES)
        rows.append(pos[:, at])
        rows.append(spec[:, at].astype(F32))
    ids = lists[...].astype(F32)
    rest = ids.shape[1] - LANES
    rows.append(ids[:, 0:LANES])
    rows.append(jnp.concatenate([ids[:, LANES:], jnp.zeros((8, LANES - rest), F32)], 1))
    rows.append(centers[...].astype(F32))
    rows.append(jnp.full((1, LANES), live_ref[0].astype(F32)))
    rows.append(jnp.zeros((1, LANES), F32))
    rows.append(neigh[...].astype(F32))
    rows.append(jnp.zeros((2, LANES), F32))
    out_ref[...] = jnp.concatenate(rows, 0)


def weights_kernel(
    w_rad_hbm,
    emb_center_hbm,
    emb_neigh_hbm,
    w_env_hbm,
    w_lat_hbm,
    w_out_hbm,
    front_ref,
    w_env_ref,
    w_lat_ref,
    w_out_ref,
    w_rad,
    emb_center,
    emb_neigh,
    w_out,
    sems,
):
    fetched = []
    for j, (src, dst) in enumerate(
        (
            (w_rad_hbm, w_rad),
            (emb_center_hbm, emb_center),
            (emb_neigh_hbm, emb_neigh),
            (w_env_hbm, w_env_ref),
            (w_lat_hbm, w_lat_ref),
            (w_out_hbm, w_out),
        )
    ):
        copy = pltpu.make_async_copy(src, dst, sems.at[j])
        copy.start()
        fetched.append(copy)
    for copy in fetched:
        copy.wait()
    lat = w_lat_ref.shape[1]
    w1, w2, w3 = parts(w_rad[...], 3)
    none = jnp.zeros((1, lat), BF16)
    front_ref[...] = jnp.concatenate(
        [w1, w2, w1, w3, w2, w1, emb_center[...], none, emb_neigh[...], none], 0
    )
    w_lat_ref[lat:] = w_lat_ref[lat:] * jnp.full((), 2.0, BF16)
    w_out_ref[...] = jnp.broadcast_to(w_out[...], (16, lat))


def tile_at(extra, side):
    return 8 * (3 * extra + 1 - side)


def sends_kernel(
    own_ref, low_ref, border_ref, cross_ref, high_ref, _, far_ref, near_ref, mid_ref, raw_ref
):
    even_n = lax.axis_index("inner") % 2 == 0
    outer = lax.axis_index("outer")
    odd = outer % 2 == 1
    rows = lax.broadcasted_iota(jnp.int32, (8, LANES), 0)
    own, cross = own_ref[...], cross_ref[...]
    beside = jnp.where(outer < lax.axis_size("outer") // 2, low_ref[...], high_ref[...])
    raw_ref[0] = own
    raw_ref[1] = cross

    def tiles_of(raw, sides):
        halves = [raw[LISTS + 8 * i : LISTS + 8 * i + 8].astype(jnp.int32) for i in range(2)]
        names, ids = [], []
        for side in sides:
            if side == 0:
                picked = [half[3:5] for half in halves]
                names += [(0, -1), (0, 1)]
            else:
                upper = odd if side > 0 else jnp.logical_not(odd)
                picked = [jnp.where(upper, half[5:8], half[0:3]) for half in halves]
                names += [(side, dy) for dy in (-1, 0, 1)]
            for i in range(picked[0].shape[0]):
                ids += [picked[0][i : i + 1], picked[1][i : i + 1]]
        ids = jnp.concatenate(ids, 1)
        taken = gather(raw[TABLE : TABLE + 16], onehot_low(ids & 127), ids >> 7)
        tiles = {}
        for j, name in enumerate(names):
            at = 2 * j * LANES
            tiles[name] = jnp.where(
                rows < 4, taken[:, at : at + LANES], taken[:, at + LANES : at + 2 * LANES]
            )
        return tiles

    by_own = tiles_of(own, (1, 0))
    by_cross = tiles_of(cross, (0, -1))
    by_beside = tiles_of(beside, (1,))
    by_border = tiles_of(border_ref[...], (-1,))
    sources = ({1: by_beside, 0: by_own, -1: by_cross}, {1: by_own, 0: by_cross, -1: by_border})
    for extra in range(2):
        for side in (1, 0, -1):
            tiles = sources[extra][side]
            minus, plus = tiles[side, -1], tiles[side, 1]
            at = tile_at(extra, side)
            far_ref[at : at + 8] = jnp.where(even_n, minus, plus)
            near_ref[at : at + 8] = jnp.where(even_n, plus, minus)
            if side:
                m = 8 * (2 * extra + (1 - side) // 2)
                mid_ref[m : m + 8] = tiles[side, 0]


def silu_parts(pre):
    sig = 0.5 * jnp.tanh(0.5 * pre) + 0.5
    act = pre * sig
    return act, sig + act - act * sig


def half_turns(value):
    whole = jnp.floor(value + 0.5)
    rest = (value - whole) * math.pi
    sign = 1.0 - 2.0 * (whole - 2.0 * jnp.floor(whole * 0.5))
    r2 = rest * rest
    sine, cosine = -1.0 / 39916800, 1.0 / 479001600
    for term in (1.0 / 362880, -1.0 / 5040, 1.0 / 120, -1.0 / 6, 1.0):
        sine = term + r2 * sine
    for term in (-1.0 / 3628800, 1.0 / 40320, -1.0 / 720, 1.0 / 24, -0.5, 1.0):
        cosine = term + r2 * cosine
    return sign * rest * sine, sign * cosine


def pair_kernel(feat, pair_len, *refs):
    place = lax.axis_index("outer") % 4
    at_border = (place == 0) | (place == 3)
    pl.when(at_border)(lambda: pair_body(2, feat, pair_len, *refs))
    pl.when(jnp.logical_not(at_border))(lambda: pair_body(1, feat, pair_len, *refs))


def pair_body(
    count,
    feat,
    pair_len,
    raw_ref,
    mid_ref,
    up_ref,
    low_ref,
    front_ref,
    w_env_ref,
    w_lat_ref,
    w_out_ref,
    local_ref,
    edge_near_ref,
    edge_far_ref,
    back_far_ref,
    back_near_ref,
    same_ref,
    hot_t_ref,
    contrib_ref,
    gath_ref,
    back_ref,
):
    chunks = pair_len // LANES
    lat = w_lat_ref.shape[1]
    even_n = lax.axis_index("inner") % 2 == 0
    odd = lax.axis_index("outer") % 2 == 1
    lanes = lax.broadcasted_iota(jnp.int32, (1, LANES), 1).astype(F32).astype(BF16)

    front = front_ref[...]
    w1, w2 = front[0:8], front[8:16]
    w_env = w_env_ref[...]
    w_lat = w_lat_ref[...]
    w_out = w_out_ref[0:8].astype(F32).T[:, 0:1]

    def as_row(tile):
        return jnp.concatenate([tile[i : i + 1] for i in range(chunks)], 1)

    def onehot_t(low_tile):
        return jnp.concatenate(
            [hits(down_lanes(low_tile[i : i + 1].astype(F32)), lanes) for i in range(chunks)], 0
        )

    def feat_rows(k):
        return slice(k * feat, (k + 1) * feat)

    def of_order(value, k):
        return value[feat_rows(ORDER_OF[k])]

    def domain(d):
        return slice(d * pair_len, (d + 1) * pair_len)

    def build_same(d):
        shifted = raw_ref[d, CENTERS : CENTERS + 8] - 256.0
        across = shifted.astype(BF16)
        for i in range(chunks):
            down = down_lanes(shifted[i : i + 1])
            for j in range(chunks):
                same_ref[d, i * LANES : (i + 1) * LANES, j * LANES : (j + 1) * LANES] = hits(
                    down, across[j : j + 1]
                )

    def place(d):
        raw = raw_ref.at[d]
        centers = raw[CENTERS : CENTERS + 8]
        table = [raw[TABLE : TABLE + 16]]

        def ghost_tile(side, dy):
            if dy == 0:
                m = 8 * (2 * d + (1 - side) // 2)
                return mid_ref[m : m + 8]
            t = tile_at(d, side)
            by_low, by_up = low_ref[t : t + 8], up_ref[t : t + 8]
            return jnp.where(even_n, by_low, by_up) if dy < 0 else jnp.where(even_n, by_up, by_low)

        for dx, dy in DIRS:
            if dx == 0:
                table.append(ghost_tile(0, dy))
            else:
                table.append(jnp.where(odd, ghost_tile(dx, dy), ghost_tile(-dx, dy)))
        table = jnp.concatenate(table, 0)
        neigh = raw[NEIGH : NEIGH + 8].astype(jnp.int32)
        ghost = neigh - 512
        listed = (ghost * 745) >> 17
        entry = ghost - 176 * listed
        is_local = neigh < 512
        neigh_low = jnp.where(is_local, neigh & 127, entry & 127)
        hot_t_ref[d] = onehot_t(neigh_low)
        neigh_high = as_row(jnp.where(is_local, neigh >> 7, 4 + 2 * listed + (entry >> 7)))
        center_ids = as_row(centers.astype(jnp.int32))
        center_high = center_ids >> 7
        at_neigh = gather(table, onehot_low(as_row(neigh_low)), neigh_high)
        at_center = gather(table[0:16], onehot_low(center_ids & 127), center_high)
        if d == 0:
            hot_t_ref[2] = onehot_t(centers.astype(jnp.int32) & 127)
        block = lax.broadcasted_iota(jnp.int32, (1, pair_len), 1) // 128
        mask = jnp.where(block.astype(F32) < raw[LIVE : LIVE + 1, 0:1], 1.0, 0.0)
        return at_neigh, at_center, mask, neigh_high, center_high

    placed = [place(d) for d in range(count)]
    at_neigh, at_center, mask = (jnp.concatenate([p[i] for p in placed], 1) for i in range(3))
    width = mask.shape[1]
    moved = at_neigh - at_center
    rx, ry, rz = moved[0:1], moved[1:2], moved[2:3]
    squared = rx * rx + ry * ry + rz * rz + 1.0
    inv = lax.rsqrt(squared)
    dist = squared * inv
    ux, uy, uz = rx * inv, ry * inv, rz * inv
    slack = 1.0 - squared * (1.0 / (CUTOFF * CUTOFF))
    env = slack * slack
    scaled = env * mask
    ns = (lax.broadcasted_iota(jnp.int32, (8, width), 0) + 1).astype(F32)
    sine, cosine = half_turns(ns * (dist * (1.0 / CUTOFF)))
    scale = inv * env
    kinds = lax.broadcasted_iota(jnp.int32, (8, width), 0).astype(F32)
    hot_center = jnp.where(at_center[3:4] == kinds, 1.0, 0.0).astype(BF16)
    hot_neigh = jnp.where(at_neigh[3:4] == kinds, 1.0, 0.0).astype(BF16)
    b1, b2, b3 = parts(sine * scale, 3)
    pre = dot_rows(front, jnp.concatenate([b1, b1, b2, b1, b2, b3, hot_center, hot_neigh], 0))
    for d in range(count):
        build_same(d)
    latent, slope = silu_parts(pre)
    half = latent.astype(BF16)
    raw = dot(w_env, half)
    weight = raw * scaled
    shape = [
        None,
        ROOT3 * ux,
        ROOT3 * uy,
        ROOT3 * uz,
        ROOT15 * ux * uy,
        ROOT15 * uy * uz,
        0.5 * ROOT5 * (2.0 * uz * uz - ux * ux - uy * uy),
        ROOT15 * ux * uz,
        0.5 * ROOT15 * (ux * ux - uy * uy),
    ]
    shape_half = [None] + [row.astype(BF16) for row in shape[1:]]

    def spread_same(d, value, out_ref):
        at = domain(d)
        value = value[:, at]
        for k in range(9):
            rows = of_order(value, k)
            contrib_ref[d, feat_rows(k)] = (rows if k == 0 else rows * shape[k][:, at]).astype(BF16)
        out_ref[d] = dot(contrib_ref[d], same_ref[d])

    def gathered_sums(d, in_ref):
        at = domain(d)
        sums = [None, None, None]
        for k in range(9):
            term = in_ref[d, feat_rows(k)]
            if k:
                term = term * shape[k][:, at]
            order = ORDER_OF[k]
            sums[order] = term if sums[order] is None else sums[order] + term
        return jnp.concatenate(sums, 0)

    for d in range(count):
        spread_same(d, weight, gath_ref)
    sums = jnp.concatenate([gathered_sums(d, gath_ref) for d in range(count)], 1)
    joined = jnp.concatenate([half, (weight * sums).astype(BF16)], 0)
    update, slope2 = silu_parts(dot_rows(w_lat, joined))
    refined = (latent + update).astype(BF16)
    raw_energy = dot(w_out_ref[...], refined)[0:1]
    d_refined = scaled * w_out
    d_joined = dot(w_lat, (d_refined * slope2).astype(BF16))
    d_latent = d_refined + d_joined[:lat]
    d_inv = d_joined[lat:]
    d_weight = d_inv * sums
    d_sums = d_inv * weight
    for d in range(count):
        spread_same(d, d_sums, back_ref)
    d_order, d_shape = [], []
    for d in range(count):
        at = domain(d)
        d_order.append(gathered_sums(d, back_ref))
        here = []
        for k in range(1, 9):
            both = (
                of_order(d_sums, k)[:, at] * gath_ref[d, feat_rows(k)]
                + of_order(weight, k)[:, at] * back_ref[d, feat_rows(k)]
            )
            here.append(jnp.sum(both, axis=0, keepdims=True))
        d_shape.append(here)
    d_weight = d_weight + jnp.concatenate(d_order, 1)
    d_shape = [None] + [jnp.concatenate([here[k] for here in d_shape], 1) for k in range(8)]
    d_scaled = raw_energy + jnp.sum(d_weight * raw, axis=0, keepdims=True)
    d_latent = d_latent + scaled * dot_rows(w_env, d_weight.astype(BF16))
    d_pre = (d_latent * slope).astype(BF16)
    d_basis = dot(jnp.concatenate([w1, w2], 0), d_pre)
    d_basis = d_basis[0:8] + d_basis[8:16]

    along = jnp.sum(d_basis * sine, axis=0, keepdims=True)
    turned = jnp.sum(d_basis * cosine * ns, axis=0, keepdims=True)
    d_env = along * inv + mask * d_scaled
    dx = (
        ROOT3 * d_shape[1]
        + ROOT15 * (uy * d_shape[4] + uz * d_shape[7] + ux * d_shape[8])
        - ROOT5 * ux * d_shape[6]
    )
    dy = (
        ROOT3 * d_shape[2]
        + ROOT15 * (ux * d_shape[4] + uz * d_shape[5] - uy * d_shape[8])
        - ROOT5 * uy * d_shape[6]
    )
    dz = (
        ROOT3 * d_shape[3]
        + ROOT15 * (uy * d_shape[5] + ux * d_shape[7])
        + 2.0 * ROOT5 * uz * d_shape[6]
    )
    d_inv = along * env + dx * rx + dy * ry + dz * rz
    d_dist = turned * (math.pi / CUTOFF) * scale - d_inv * inv * inv
    d_squared = 0.5 * inv * d_dist - (2.0 / (CUTOFF * CUTOFF)) * slack * d_env
    gx = dx * inv + 2.0 * rx * d_squared
    gy = dy * inv + 2.0 * ry * d_squared
    gz = dz * inv + 2.0 * rz * d_squared
    rows4 = [gx, gy, gz, 0.5 * scaled * raw_energy]
    values = jnp.concatenate(rows4 + rows4, 0)
    rows = lax.broadcasted_iota(jnp.int32, (8, width), 0)
    flipped = jnp.where((rows & 3) == 3, values, -values)
    first = jnp.where(odd, 5, 0)

    def groups_of(side):
        return [2 + (first if side > 0 else 5 - first) + i for i in range(3)]

    neigh_high, center_high = placed[0][3:]
    groups = [0, 1, 2 + 3, 2 + 4] + groups_of(1) + (groups_of(-1) if count == 1 else [])
    terms = scatter(flipped[:, domain(0)], hot_t_ref[0], neigh_high, groups)
    center_terms = scatter(values[:, domain(0)], hot_t_ref[2], center_high, (0, 1))
    local_ref[...] = terms[0:16] + center_terms
    tiles = [terms[8 * i : 8 * i + 8] for i in range(2, len(groups))]
    if count == 2:
        terms = scatter(flipped[:, domain(1)], hot_t_ref[1], placed[1][3], groups_of(1))
        tiles += [terms[8 * i : 8 * i + 8] for i in range(3)]
    edge_near_ref[...] = tiles[3]
    edge_far_ref[...] = tiles[6]
    for j, (minus, plus) in enumerate(
        ((tiles[0], tiles[1]), (tiles[2], tiles[4]), (tiles[5], tiles[7]))
    ):
        at = slice(8 * j, 8 * j + 8)
        back_far_ref[at] = jnp.where(even_n, plus, minus)
        back_near_ref[at] = jnp.where(even_n, minus, plus)


def collect_kernel(
    local_ref,
    raw_ref,
    up_ref,
    low_ref,
    edge_far_ref,
    beside_ref,
    cross_ref,
    forces_ref,
    energy_ref,
):
    even_n = lax.axis_index("inner") % 2 == 0
    odd = lax.axis_index("outer") % 2 == 1
    place = lax.axis_index("outer") % 4
    at_border = (place == 0) | (place == 3)
    plus = jnp.where(even_n, low_ref[...], up_ref[...])
    minus = jnp.where(even_n, up_ref[...], low_ref[...])
    over = jnp.concatenate([minus[16:24], edge_far_ref[...], plus[16:24]], 0)
    toward = jnp.where(at_border, over, cross_ref[...])
    away = beside_ref[...]
    above = jnp.where(odd, toward, away)
    below = jnp.where(odd, away, toward)
    lists_low = raw_ref[LISTS : LISTS + 8].astype(jnp.int32)
    lists_high = raw_ref[LISTS + 8 : LISTS + 16].astype(jnp.int32)
    rows = lax.broadcasted_iota(jnp.int32, (8, LANES), 0)
    ids, values = [], []
    for k, (dx, dy) in enumerate(DIRS):
        ids += [lists_low[k : k + 1], lists_high[k : k + 1]]
        if dx == 0:
            tile = (minus if dy < 0 else plus)[0:8]
        else:
            at = 8 * (dy + 1)
            tile = (above if dx > 0 else below)[at : at + 8]
        turned = pltpu.roll(tile, 4, 0)
        values += [jnp.where(rows < 4, tile, turned), jnp.where(rows < 4, turned, tile)]
    ids = jnp.concatenate(ids, 1)
    values = jnp.concatenate(values, 1)
    hot_t = []
    lanes = lax.broadcasted_iota(jnp.int32, (1, LANES), 1).astype(F32).astype(BF16)
    for k in range(len(DIRS)):
        for tile in (lists_low, lists_high):
            hot_t.append(hits(down_lanes((tile[k : k + 1] & 127).astype(F32)), lanes))
    total = local_ref[...] + scatter(values, jnp.concatenate(hot_t, 0), ids >> 7, (0, 1))
    for j in range(4):
        forces_ref[:, j * LANES : (j + 1) * LANES] = total[4 * j : 4 * j + 3]
        energy_ref[:, j * LANES : (j + 1) * LANES] = total[4 * j + 3 : 4 * j + 4]


def on_device(
    positions,
    species,
    send_lists,
    centers,
    neighbours,
    live_blocks,
    w_rad,
    emb_center,
    emb_neigh,
    w_env,
    w_lat,
    w_out,
):
    pair_len = centers.shape[0]
    atom_count = positions.shape[1]
    feat = w_env.shape[1] // 3
    lat = w_env.shape[0]
    chunks = pair_len // LANES

    def rows(count):
        return jax.ShapeDtypeStruct((count, LANES), F32)

    packed = pl.pallas_call(
        pack_kernel,
        out_shape=rows(PACKED),
        in_specs=[pl.BlockSpec(memory_space=pltpu.HBM)] * 5
        + [pl.BlockSpec(memory_space=pltpu.SMEM)],
        scratch_shapes=[
            pltpu.VMEM(positions.shape, F32),
            pltpu.VMEM((1, atom_count), jnp.int32),
            pltpu.VMEM(send_lists.shape, jnp.int32),
            pltpu.VMEM((chunks, LANES), jnp.int32),
            pltpu.VMEM((chunks, LANES), jnp.int32),
            pltpu.SemaphoreType.DMA((5,)),
        ],
        compiler_params=SMALL,
        name="pack_domain",
    )(
        *(
            pltpu.with_memory_space_constraint(value, pltpu.HBM)
            for value in (
                positions,
                species.reshape(1, atom_count),
                send_lists,
                centers.reshape(chunks, LANES),
                neighbours.reshape(chunks, LANES),
            )
        ),
        live_blocks,
    )
    weights = pl.pallas_call(
        weights_kernel,
        out_shape=[
            jax.ShapeDtypeStruct((64, lat), BF16),
            jax.ShapeDtypeStruct((w_env.shape[1], lat), BF16),
            jax.ShapeDtypeStruct(w_lat.shape, BF16),
            jax.ShapeDtypeStruct((16, lat), BF16),
        ],
        in_specs=[pl.BlockSpec(memory_space=pltpu.HBM)] * 6,
        scratch_shapes=[
            pltpu.VMEM(w_rad.shape, F32),
            pltpu.VMEM(emb_center.shape, BF16),
            pltpu.VMEM(emb_neigh.shape, BF16),
            pltpu.VMEM((1, lat), BF16),
            pltpu.SemaphoreType.DMA((6,)),
        ],
        compiler_params=SMALL,
        cost_estimate=pl.CostEstimate(flops=0, bytes_accessed=4_000_000, transcendentals=0),
        name="place_weights",
    )(
        *(
            pltpu.with_memory_space_constraint(value, pltpu.HBM)
            for value in (w_rad, emb_center, emb_neigh, w_env.T, w_lat, w_out.reshape(1, -1))
        )
    )
    row_count = lax.axis_size("outer")
    low_half = range(row_count // 2)
    high_half = range(row_count // 2, row_count)
    beside_low = swap_outer(packed, 0, low_half)
    border = over_border(packed)
    cross = swap_outer(packed, 1, range(row_count))
    beside_high = swap_outer(packed, 0, high_half)
    far, near, mid, raw = pl.pallas_call(
        sends_kernel,
        out_shape=[
            rows(48),
            rows(48),
            rows(32),
            jax.ShapeDtypeStruct((2, PACKED, LANES), F32),
        ],
        compiler_params=SMALL,
        name="gather_sends",
    )(packed, beside_low, border, cross, beside_high, weights[3])
    up = swap_inner(far, 1)
    low = swap_inner(near, 0)
    local, edge_near, edge_far, far, near = pl.pallas_call(
        lambda *refs: pair_kernel(feat, pair_len, *refs),
        out_shape=[rows(16), rows(8), rows(8), rows(24), rows(24)],
        scratch_shapes=[
            pltpu.VMEM((2, pair_len, pair_len), BF16),
            pltpu.VMEM((3, pair_len, LANES), BF16),
            pltpu.VMEM((2, 9 * feat, pair_len), BF16),
            pltpu.VMEM((2, 9 * feat, pair_len), F32),
            pltpu.VMEM((2, 9 * feat, pair_len), F32),
        ],
        compiler_params=LARGE,
        name="pair_terms",
    )(raw, mid, up, low, *weights)
    up = swap_inner(far, 1)
    low = swap_inner(near, 0)
    even_n = lax.axis_index("inner") % 2 == 0
    plus = jnp.where(even_n, low, up)
    minus = jnp.where(even_n, up, low)
    inside = [o for o in range(row_count) if o % 4 in (1, 2)]
    cross = swap_outer(
        jnp.concatenate([minus[16:24], edge_far, plus[16:24]], 0), 1, inside
    )
    beside = swap_outer(
        jnp.concatenate([minus[8:16], edge_near, plus[8:16]], 0), 0, range(row_count)
    )
    forces, energy = pl.pallas_call(
        collect_kernel,
        out_shape=[
            jax.ShapeDtypeStruct((3, atom_count), F32),
            jax.ShapeDtypeStruct((1, atom_count), F32),
        ],
        compiler_params=SMALL,
        name="collect_terms",
    )(local, packed, up, low, edge_far, beside, cross)
    return forces, energy.reshape(atom_count)


def solution(mesh):
    return jax.shard_map(
        on_device,
        mesh=mesh,
        in_specs=(
            P(None, AXES),
            P(AXES),
            P(None, AXES),
            P(AXES),
            P(AXES),
            P(AXES),
            P(),
            P(),
            P(),
            P(),
            P(),
            P(),
        ),
        out_specs=(P(None, AXES), P(AXES)),
        check_vma=False,
    )
```

```python
import math

import jax
import jax.numpy as jnp
from jax import lax
from jax.experimental import pallas as pl
from jax.experimental.pallas import tpu as pltpu
from jax.sharding import PartitionSpec as P

AXES = ("outer", "inner")
CUTOFF = 6.0
ROOT3 = math.sqrt(3.0)
ROOT5 = math.sqrt(5.0)
ROOT15 = math.sqrt(15.0)
LANES = 128
F32 = jnp.float32
BF16 = jnp.bfloat16
SMALL = pltpu.CompilerParams(vmem_limit_bytes=8 * 1024 * 1024)
LARGE = pltpu.CompilerParams(vmem_limit_bytes=32 * 1024 * 1024)
DIRS = ((-1, -1), (-1, 0), (-1, 1), (0, -1), (0, 1), (1, -1), (1, 0), (1, 1))
TABLE, LISTS, CENTERS, NEIGH, PACKED = 0, 16, 32, 40, 48
LIVE = 38
ORDER_OF = (0, 1, 1, 1, 2, 2, 2, 2, 2)


def permute(block, place):
    outer_len = lax.axis_size("outer")
    inner_len = lax.axis_size("inner")
    route = []
    for o in range(outer_len):
        for n in range(inner_len):
            there = place(o, n)
            if there is not None:
                to = there[0] % outer_len * inner_len + there[1] % inner_len
                route.append((o * inner_len + n, to))
    return lax.ppermute(block, AXES, route)


def swap_inner(block, parity):
    return permute(block, lambda o, n: (o, n + 1 if n % 2 == parity else n - 1))


def swap_outer(block, parity, rows):
    def place(o, n):
        return (o + 1 if o % 2 == parity else o - 1, n) if o in rows else None

    return permute(block, place)


def copy_rows(block, rows):
    return permute(block, lambda o, n: (rows[o], n) if o in rows else None)


def row_kind():
    half = lax.axis_size("outer") // 2
    row = lax.axis_index("outer")
    place = lax.rem(row, half)
    return row < half, (place == 0) | (place == half - 1)


def dot(lhs, rhs):
    return jnp.dot(lhs, rhs, preferred_element_type=F32)


def dot_rows(lhs, rhs):
    return lax.dot_general(lhs, rhs, (((0,), (0,)), ((), ())), preferred_element_type=F32)


def parts(value, count):
    out = []
    for _ in range(count):
        piece = value.astype(BF16)
        out.append(piece)
        value = value - piece.astype(F32)
    return out


def hits(left, right):
    return jnp.where(left == right, jnp.ones((), BF16), jnp.zeros((), BF16))


def down_lanes(row):
    return jnp.broadcast_to(row, (LANES, LANES)).T.astype(BF16)


def onehot_low(low_row):
    rows = lax.broadcasted_iota(jnp.int32, (LANES, low_row.shape[1]), 0).astype(F32).astype(BF16)
    return hits(rows, low_row.astype(F32).astype(BF16))


def high_mask(high_row, group):
    rows = lax.broadcasted_iota(jnp.int32, (8, high_row.shape[1]), 0)
    return high_row == 2 * group + jnp.where(rows >= 4, 1, 0)


def gather(table, low_hot, high_row):
    size = table.shape[0]
    found = dot(jnp.concatenate(parts(table, 3), 0), low_hot)
    found = found[0:size] + found[size : 2 * size] + found[2 * size :]
    total = None
    for group in range(size // 8):
        term = jnp.where(high_mask(high_row, group), found[8 * group : 8 * group + 8], 0.0)
        total = term if total is None else total + term
    return total + pltpu.roll(total, 4, 0)


def scatter(values, low_hot_t, high_row, groups):
    spread = [jnp.where(high_mask(high_row, group), values, 0.0) for group in groups]
    spread = jnp.concatenate(spread, 0)
    size = 8 * len(groups)
    summed = dot(jnp.concatenate(parts(spread, 2), 0), low_hot_t)
    return summed[0:size] + summed[size:]


def pack_kernel(
    pos_hbm,
    spec_hbm,
    lists_hbm,
    centers_hbm,
    neigh_hbm,
    live_ref,
    out_ref,
    pos,
    spec,
    lists,
    centers,
    neigh,
    sems,
):
    fetched = []
    for j, (src, dst) in enumerate(
        (
            (pos_hbm, pos),
            (spec_hbm, spec),
            (lists_hbm, lists),
            (centers_hbm, centers),
            (neigh_hbm, neigh),
        )
    ):
        copy = pltpu.make_async_copy(src, dst, sems.at[j])
        copy.start()
        fetched.append(copy)
    for copy in fetched:
        copy.wait()
    rows = []
    for j in range(4):
        at = slice(j * LANES, (j + 1) * LANES)
        rows.append(pos[:, at])
        rows.append(spec[:, at].astype(F32))
    ids = lists[...].astype(F32)
    rest = ids.shape[1] - LANES
    rows.append(ids[:, 0:LANES])
    rows.append(jnp.concatenate([ids[:, LANES:], jnp.zeros((8, LANES - rest), F32)], 1))
    rows.append(centers[...].astype(F32))
    rows.append(jnp.full((1, LANES), live_ref[0].astype(F32)))
    rows.append(jnp.zeros((1, LANES), F32))
    rows.append(neigh[...].astype(F32))
    rows.append(jnp.zeros((2, LANES), F32))
    out_ref[...] = jnp.concatenate(rows, 0)


def weights_kernel(
    w_rad_hbm,
    emb_center_hbm,
    emb_neigh_hbm,
    w_env_hbm,
    w_lat_hbm,
    w_out_hbm,
    front_ref,
    w_env_ref,
    w_lat_ref,
    w_out_ref,
    w_rad,
    emb_center,
    emb_neigh,
    w_out,
    sems,
):
    fetched = []
    for j, (src, dst) in enumerate(
        (
            (w_rad_hbm, w_rad),
            (emb_center_hbm, emb_center),
            (emb_neigh_hbm, emb_neigh),
            (w_env_hbm, w_env_ref),
            (w_lat_hbm, w_lat_ref),
            (w_out_hbm, w_out),
        )
    ):
        copy = pltpu.make_async_copy(src, dst, sems.at[j])
        copy.start()
        fetched.append(copy)
    for copy in fetched:
        copy.wait()
    lat = w_lat_ref.shape[1]
    w1, w2, w3 = parts(w_rad[...], 3)
    none = jnp.zeros((1, lat), BF16)
    front_ref[...] = jnp.concatenate(
        [w1, w2, w1, w3, w2, w1, emb_center[...], none, emb_neigh[...], none], 0
    )
    w_lat_ref[lat:] = w_lat_ref[lat:] * jnp.full((), 2.0, BF16)
    w_out_ref[...] = jnp.broadcast_to(w_out[...], (16, lat))


def tile_at(extra, side):
    return 8 * (3 * extra + 1 - side)


def sends_kernel(
    own_ref, high_ref, cross_ref, second_ref, first_ref, _, far_ref, near_ref, mid_ref, raw_ref
):
    even_n = lax.axis_index("inner") % 2 == 0
    odd = lax.axis_index("outer") % 2 == 1
    low_half, at_border = row_kind()
    rows = lax.broadcasted_iota(jnp.int32, (8, LANES), 0)
    own, cross = own_ref[...], cross_ref[...]
    beside = jnp.where(at_border, second_ref[...], first_ref[...])
    beside = jnp.where(low_half, beside, high_ref[...])
    raw_ref[0] = own
    raw_ref[1] = cross

    def tiles_of(raw, sides):
        halves = [raw[LISTS + 8 * i : LISTS + 8 * i + 8].astype(jnp.int32) for i in range(2)]
        names, ids = [], []
        for side in sides:
            if side == 0:
                picked = [half[3:5] for half in halves]
                names += [(0, -1), (0, 1)]
            else:
                upper = odd if side > 0 else jnp.logical_not(odd)
                picked = [jnp.where(upper, half[5:8], half[0:3]) for half in halves]
                names += [(side, dy) for dy in (-1, 0, 1)]
            for i in range(picked[0].shape[0]):
                ids += [picked[0][i : i + 1], picked[1][i : i + 1]]
        ids = jnp.concatenate(ids, 1)
        taken = gather(raw[TABLE : TABLE + 16], onehot_low(ids & 127), ids >> 7)
        tiles = {}
        for j, name in enumerate(names):
            at = 2 * j * LANES
            tiles[name] = jnp.where(
                rows < 4, taken[:, at : at + LANES], taken[:, at + LANES : at + 2 * LANES]
            )
        return tiles

    by_own = tiles_of(own, (1, 0))
    by_cross = tiles_of(cross, (0, -1))
    by_beside = tiles_of(beside, (1,))
    by_border = tiles_of(first_ref[...], (-1,))
    sources = ({1: by_beside, 0: by_own, -1: by_cross}, {1: by_own, 0: by_cross, -1: by_border})
    for extra in range(2):
        for side in (1, 0, -1):
            tiles = sources[extra][side]
            minus, plus = tiles[side, -1], tiles[side, 1]
            at = tile_at(extra, side)
            far_ref[at : at + 8] = jnp.where(even_n, minus, plus)
            near_ref[at : at + 8] = jnp.where(even_n, plus, minus)
            if side:
                m = 8 * (2 * extra + (1 - side) // 2)
                mid_ref[m : m + 8] = tiles[side, 0]


def silu_parts(pre):
    sig = 0.5 * jnp.tanh(0.5 * pre) + 0.5
    act = pre * sig
    return act, sig + act - act * sig


def half_turns(value):
    whole = jnp.floor(value + 0.5)
    rest = (value - whole) * math.pi
    sign = 1.0 - 2.0 * (whole - 2.0 * jnp.floor(whole * 0.5))
    r2 = rest * rest
    sine, cosine = -1.0 / 39916800, 1.0 / 479001600
    for term in (1.0 / 362880, -1.0 / 5040, 1.0 / 120, -1.0 / 6, 1.0):
        sine = term + r2 * sine
    for term in (-1.0 / 3628800, 1.0 / 40320, -1.0 / 720, 1.0 / 24, -0.5, 1.0):
        cosine = term + r2 * cosine
    return sign * rest * sine, sign * cosine


def pair_kernel(feat, pair_len, *refs):
    low_half, at_border = row_kind()
    two = low_half & at_border
    pl.when(two)(lambda: pair_body(2, feat, pair_len, *refs))
    pl.when(jnp.logical_not(two))(lambda: pair_body(1, feat, pair_len, *refs))


def pair_body(
    count,
    feat,
    pair_len,
    raw_ref,
    mid_ref,
    up_ref,
    low_ref,
    front_ref,
    w_env_ref,
    w_lat_ref,
    w_out_ref,
    local_ref,
    edge_near_ref,
    edge_far_ref,
    edge_over_ref,
    back_far_ref,
    back_near_ref,
    same_ref,
    hot_t_ref,
    contrib_ref,
    gath_ref,
    back_ref,
):
    chunks = pair_len // LANES
    lat = w_lat_ref.shape[1]
    even_n = lax.axis_index("inner") % 2 == 0
    odd = lax.axis_index("outer") % 2 == 1
    lanes = lax.broadcasted_iota(jnp.int32, (1, LANES), 1).astype(F32).astype(BF16)

    front = front_ref[...]
    w1, w2 = front[0:8], front[8:16]
    w_env = w_env_ref[...]
    w_lat = w_lat_ref[...]
    w_out = w_out_ref[0:8].astype(F32).T[:, 0:1]

    def as_row(tile):
        return jnp.concatenate([tile[i : i + 1] for i in range(chunks)], 1)

    def onehot_t(low_tile):
        return jnp.concatenate(
            [hits(down_lanes(low_tile[i : i + 1].astype(F32)), lanes) for i in range(chunks)], 0
        )

    def feat_rows(k):
        return slice(k * feat, (k + 1) * feat)

    def of_order(value, k):
        return value[feat_rows(ORDER_OF[k])]

    def domain(d):
        return slice(d * pair_len, (d + 1) * pair_len)

    def build_same(d):
        shifted = raw_ref[d, CENTERS : CENTERS + 8] - 256.0
        across = shifted.astype(BF16)
        for i in range(chunks):
            down = down_lanes(shifted[i : i + 1])
            for j in range(chunks):
                same_ref[d, i * LANES : (i + 1) * LANES, j * LANES : (j + 1) * LANES] = hits(
                    down, across[j : j + 1]
                )

    def place(d):
        raw = raw_ref.at[d]
        centers = raw[CENTERS : CENTERS + 8]
        table = [raw[TABLE : TABLE + 16]]

        def ghost_tile(side, dy):
            if dy == 0:
                m = 8 * (2 * d + (1 - side) // 2)
                return mid_ref[m : m + 8]
            t = tile_at(d, side)
            by_low, by_up = low_ref[t : t + 8], up_ref[t : t + 8]
            return jnp.where(even_n, by_low, by_up) if dy < 0 else jnp.where(even_n, by_up, by_low)

        for dx, dy in DIRS:
            if dx == 0:
                table.append(ghost_tile(0, dy))
            else:
                table.append(jnp.where(odd, ghost_tile(dx, dy), ghost_tile(-dx, dy)))
        table = jnp.concatenate(table, 0)
        neigh = raw[NEIGH : NEIGH + 8].astype(jnp.int32)
        ghost = neigh - 512
        listed = (ghost * 745) >> 17
        entry = ghost - 176 * listed
        is_local = neigh < 512
        neigh_low = jnp.where(is_local, neigh & 127, entry & 127)
        hot_t_ref[d] = onehot_t(neigh_low)
        neigh_high = as_row(jnp.where(is_local, neigh >> 7, 4 + 2 * listed + (entry >> 7)))
        center_ids = as_row(centers.astype(jnp.int32))
        center_high = center_ids >> 7
        at_neigh = gather(table, onehot_low(as_row(neigh_low)), neigh_high)
        at_center = gather(table[0:16], onehot_low(center_ids & 127), center_high)
        if d == 0:
            hot_t_ref[2] = onehot_t(centers.astype(jnp.int32) & 127)
        block = lax.broadcasted_iota(jnp.int32, (1, pair_len), 1) // 128
        mask = jnp.where(block.astype(F32) < raw[LIVE : LIVE + 1, 0:1], 1.0, 0.0)
        return at_neigh, at_center, mask, neigh_high, center_high

    placed = [place(d) for d in range(count)]
    at_neigh, at_center, mask = (jnp.concatenate([p[i] for p in placed], 1) for i in range(3))
    width = mask.shape[1]
    moved = at_neigh - at_center
    rx, ry, rz = moved[0:1], moved[1:2], moved[2:3]
    squared = rx * rx + ry * ry + rz * rz + 1.0
    inv = lax.rsqrt(squared)
    dist = squared * inv
    ux, uy, uz = rx * inv, ry * inv, rz * inv
    slack = 1.0 - squared * (1.0 / (CUTOFF * CUTOFF))
    env = slack * slack
    scaled = env * mask
    ns = (lax.broadcasted_iota(jnp.int32, (8, width), 0) + 1).astype(F32)
    sine, cosine = half_turns(ns * (dist * (1.0 / CUTOFF)))
    scale = inv * env
    kinds = lax.broadcasted_iota(jnp.int32, (8, width), 0).astype(F32)
    hot_center = jnp.where(at_center[3:4] == kinds, 1.0, 0.0).astype(BF16)
    hot_neigh = jnp.where(at_neigh[3:4] == kinds, 1.0, 0.0).astype(BF16)
    b1, b2, b3 = parts(sine * scale, 3)
    pre = dot_rows(front, jnp.concatenate([b1, b1, b2, b1, b2, b3, hot_center, hot_neigh], 0))
    for d in range(count):
        build_same(d)
    latent, slope = silu_parts(pre)
    half = latent.astype(BF16)
    raw = dot(w_env, half)
    weight = raw * scaled
    shape = [
        None,
        ROOT3 * ux,
        ROOT3 * uy,
        ROOT3 * uz,
        ROOT15 * ux * uy,
        ROOT15 * uy * uz,
        0.5 * ROOT5 * (2.0 * uz * uz - ux * ux - uy * uy),
        ROOT15 * ux * uz,
        0.5 * ROOT15 * (ux * ux - uy * uy),
    ]
    shape_half = [None] + [row.astype(BF16) for row in shape[1:]]

    def spread_same(d, value, out_ref):
        at = domain(d)
        value = value[:, at]
        for k in range(9):
            rows = of_order(value, k)
            contrib_ref[d, feat_rows(k)] = (rows if k == 0 else rows * shape[k][:, at]).astype(BF16)
        out_ref[d] = dot(contrib_ref[d], same_ref[d])

    def gathered_sums(d, in_ref):
        at = domain(d)
        sums = [None, None, None]
        for k in range(9):
            term = in_ref[d, feat_rows(k)]
            if k:
                term = term * shape[k][:, at]
            order = ORDER_OF[k]
            sums[order] = term if sums[order] is None else sums[order] + term
        return jnp.concatenate(sums, 0)

    for d in range(count):
        spread_same(d, weight, gath_ref)
    sums = jnp.concatenate([gathered_sums(d, gath_ref) for d in range(count)], 1)
    joined = jnp.concatenate([half, (weight * sums).astype(BF16)], 0)
    update, slope2 = silu_parts(dot_rows(w_lat, joined))
    refined = (latent + update).astype(BF16)
    raw_energy = dot(w_out_ref[...], refined)[0:1]
    d_refined = scaled * w_out
    d_joined = dot(w_lat, (d_refined * slope2).astype(BF16))
    d_latent = d_refined + d_joined[:lat]
    d_inv = d_joined[lat:]
    d_weight = d_inv * sums
    d_sums = d_inv * weight
    for d in range(count):
        spread_same(d, d_sums, back_ref)
    d_order, d_shape = [], []
    for d in range(count):
        at = domain(d)
        d_order.append(gathered_sums(d, back_ref))
        here = []
        for k in range(1, 9):
            both = (
                of_order(d_sums, k)[:, at] * gath_ref[d, feat_rows(k)]
                + of_order(weight, k)[:, at] * back_ref[d, feat_rows(k)]
            )
            here.append(jnp.sum(both, axis=0, keepdims=True))
        d_shape.append(here)
    d_weight = d_weight + jnp.concatenate(d_order, 1)
    d_shape = [None] + [jnp.concatenate([here[k] for here in d_shape], 1) for k in range(8)]
    d_scaled = raw_energy + jnp.sum(d_weight * raw, axis=0, keepdims=True)
    d_latent = d_latent + scaled * dot_rows(w_env, d_weight.astype(BF16))
    d_pre = (d_latent * slope).astype(BF16)
    d_basis = dot(jnp.concatenate([w1, w2], 0), d_pre)
    d_basis = d_basis[0:8] + d_basis[8:16]

    along = jnp.sum(d_basis * sine, axis=0, keepdims=True)
    turned = jnp.sum(d_basis * cosine * ns, axis=0, keepdims=True)
    d_env = along * inv + mask * d_scaled
    dx = (
        ROOT3 * d_shape[1]
        + ROOT15 * (uy * d_shape[4] + uz * d_shape[7] + ux * d_shape[8])
        - ROOT5 * ux * d_shape[6]
    )
    dy = (
        ROOT3 * d_shape[2]
        + ROOT15 * (ux * d_shape[4] + uz * d_shape[5] - uy * d_shape[8])
        - ROOT5 * uy * d_shape[6]
    )
    dz = (
        ROOT3 * d_shape[3]
        + ROOT15 * (uy * d_shape[5] + ux * d_shape[7])
        + 2.0 * ROOT5 * uz * d_shape[6]
    )
    d_inv = along * env + dx * rx + dy * ry + dz * rz
    d_dist = turned * (math.pi / CUTOFF) * scale - d_inv * inv * inv
    d_squared = 0.5 * inv * d_dist - (2.0 / (CUTOFF * CUTOFF)) * slack * d_env
    gx = dx * inv + 2.0 * rx * d_squared
    gy = dy * inv + 2.0 * ry * d_squared
    gz = dz * inv + 2.0 * rz * d_squared
    rows4 = [gx, gy, gz, 0.5 * scaled * raw_energy]
    values = jnp.concatenate(rows4 + rows4, 0)
    rows = lax.broadcasted_iota(jnp.int32, (8, width), 0)
    flipped = jnp.where((rows & 3) == 3, values, -values)
    first = jnp.where(odd, 5, 0)

    def groups_of(side):
        return [2 + (first if side > 0 else 5 - first) + i for i in range(3)]

    neigh_high, center_high = placed[0][3:]
    groups = [0, 1, 2 + 3, 2 + 4] + groups_of(1) + groups_of(-1)
    terms = scatter(flipped[:, domain(0)], hot_t_ref[0], neigh_high, groups)
    center_terms = scatter(values[:, domain(0)], hot_t_ref[2], center_high, (0, 1))
    local_ref[...] = terms[0:16] + center_terms
    tiles = [terms[8 * i : 8 * i + 8] for i in range(2, len(groups))]
    if count == 2:
        terms = scatter(flipped[:, domain(1)], hot_t_ref[1], placed[1][3], groups_of(1))
        tiles += [terms[8 * i : 8 * i + 8] for i in range(3)]
    else:
        tiles += [jnp.zeros((8, LANES), F32)] * 3
    edge_near_ref[...] = tiles[3]
    edge_far_ref[...] = tiles[6]
    edge_over_ref[...] = tiles[9]
    for j, (minus, plus) in enumerate(
        (
            (tiles[0], tiles[1]),
            (tiles[2], tiles[4]),
            (tiles[5], tiles[7]),
            (tiles[8], tiles[10]),
        )
    ):
        at = slice(8 * j, 8 * j + 8)
        back_far_ref[at] = jnp.where(even_n, plus, minus)
        back_near_ref[at] = jnp.where(even_n, minus, plus)


def list_rows(raw_ref):
    odd = lax.axis_index("outer") % 2 == 1
    low = raw_ref[LISTS : LISTS + 8].astype(jnp.int32)
    high = raw_ref[LISTS + 8 : LISTS + 16].astype(jnp.int32)
    wide = jnp.concatenate([low, high], 1)
    below, above = wide[0:3], wide[5:8]
    return jnp.where(odd, below, above), jnp.where(odd, above, below), wide[3:5]


def flat(ids):
    return jnp.concatenate([ids[i : i + 1] for i in range(ids.shape[0])], 1)


def spread_tile(tile):
    rows = lax.broadcasted_iota(jnp.int32, (8, LANES), 0)
    turned = pltpu.roll(tile, 4, 0)
    return [jnp.where(rows < 4, tile, turned), jnp.where(rows < 4, turned, tile)]


def hot_rows(ids):
    lanes = lax.broadcasted_iota(jnp.int32, (1, LANES), 1).astype(F32).astype(BF16)
    low = (ids & 127).astype(F32)
    return jnp.concatenate(
        [
            hits(down_lanes(low[:, i : i + LANES]), lanes)
            for i in range(0, ids.shape[1], LANES)
        ],
        0,
    )


def begin_kernel(
    local_ref, raw_ref, up_ref, low_ref, edge_far_ref, total_ref, hot_ref, toward_ref
):
    even_n = lax.axis_index("inner") % 2 == 0
    away, toward, along = list_rows(raw_ref)
    plus = jnp.where(even_n, low_ref[...], up_ref[...])
    minus = jnp.where(even_n, up_ref[...], low_ref[...])
    toward_ref[0:8] = minus[16:24]
    toward_ref[8:16] = edge_far_ref[...]
    toward_ref[16:24] = plus[16:24]
    ids = flat(along)
    values = jnp.concatenate(spread_tile(minus[0:8]) + spread_tile(plus[0:8]), 1)
    total_ref[...] = local_ref[...] + scatter(values, hot_rows(ids), ids >> 7, (0, 1))
    hot_ref[...] = hot_rows(jnp.concatenate([flat(away), flat(toward)], 1))


def collect_kernel(
    total_ref,
    hot_ref,
    raw_ref,
    up_ref,
    low_ref,
    edge_over_ref,
    over_ref,
    inside_ref,
    beside_ref,
    forces_ref,
    energy_ref,
):
    even_n = lax.axis_index("inner") % 2 == 0
    low_half, at_border = row_kind()
    plus = jnp.where(even_n, low_ref[24:32], up_ref[24:32])
    minus = jnp.where(even_n, up_ref[24:32], low_ref[24:32])
    toward = jnp.concatenate([minus, edge_over_ref[...], plus], 0)
    toward = jnp.where(low_half, toward, over_ref[...])
    toward = jnp.where(at_border, toward, inside_ref[...])
    away = beside_ref[...]
    ids = list_rows(raw_ref)
    ids = jnp.concatenate([flat(ids[0]), flat(ids[1])], 1)
    values = []
    for tiles in (away, toward):
        for j in range(3):
            values += spread_tile(tiles[8 * j : 8 * j + 8])
    values = jnp.concatenate(values, 1)
    total = total_ref[...] + scatter(values, hot_ref[...], ids >> 7, (0, 1))
    for j in range(4):
        forces_ref[:, j * LANES : (j + 1) * LANES] = total[4 * j : 4 * j + 3]
        energy_ref[:, j * LANES : (j + 1) * LANES] = total[4 * j + 3 : 4 * j + 4]


def on_device(
    positions,
    species,
    send_lists,
    centers,
    neighbours,
    live_blocks,
    w_rad,
    emb_center,
    emb_neigh,
    w_env,
    w_lat,
    w_out,
):
    pair_len = centers.shape[0]
    atom_count = positions.shape[1]
    feat = w_env.shape[1] // 3
    lat = w_env.shape[0]
    chunks = pair_len // LANES

    def rows(count):
        return jax.ShapeDtypeStruct((count, LANES), F32)

    packed = pl.pallas_call(
        pack_kernel,
        out_shape=rows(PACKED),
        in_specs=[pl.BlockSpec(memory_space=pltpu.HBM)] * 5
        + [pl.BlockSpec(memory_space=pltpu.SMEM)],
        scratch_shapes=[
            pltpu.VMEM(positions.shape, F32),
            pltpu.VMEM((1, atom_count), jnp.int32),
            pltpu.VMEM(send_lists.shape, jnp.int32),
            pltpu.VMEM((chunks, LANES), jnp.int32),
            pltpu.VMEM((chunks, LANES), jnp.int32),
            pltpu.SemaphoreType.DMA((5,)),
        ],
        compiler_params=SMALL,
        name="pack_domain",
    )(
        *(
            pltpu.with_memory_space_constraint(value, pltpu.HBM)
            for value in (
                positions,
                species.reshape(1, atom_count),
                send_lists,
                centers.reshape(chunks, LANES),
                neighbours.reshape(chunks, LANES),
            )
        ),
        live_blocks,
    )
    weights = pl.pallas_call(
        weights_kernel,
        out_shape=[
            jax.ShapeDtypeStruct((64, lat), BF16),
            jax.ShapeDtypeStruct((w_env.shape[1], lat), BF16),
            jax.ShapeDtypeStruct(w_lat.shape, BF16),
            jax.ShapeDtypeStruct((16, lat), BF16),
        ],
        in_specs=[pl.BlockSpec(memory_space=pltpu.HBM)] * 6,
        scratch_shapes=[
            pltpu.VMEM(w_rad.shape, F32),
            pltpu.VMEM(emb_center.shape, BF16),
            pltpu.VMEM(emb_neigh.shape, BF16),
            pltpu.VMEM((1, lat), BF16),
            pltpu.SemaphoreType.DMA((6,)),
        ],
        compiler_params=SMALL,
        cost_estimate=pl.CostEstimate(flops=0, bytes_accessed=4_000_000, transcendentals=0),
        name="place_weights",
    )(
        *(
            pltpu.with_memory_space_constraint(value, pltpu.HBM)
            for value in (w_rad, emb_center, emb_neigh, w_env.T, w_lat, w_out.reshape(1, -1))
        )
    )
    count = lax.axis_size("outer")
    half = count // 2
    first = copy_rows(packed, {0: 1, half - 1: half - 2, half + 1: half - 1, count - 2: 0})
    second = copy_rows(packed, {1: 0, half - 2: half - 1})
    cross = swap_outer(packed, 1, range(count))
    high = swap_outer(packed, 0, range(half, count))
    far, near, mid, raw = pl.pallas_call(
        sends_kernel,
        out_shape=[
            rows(48),
            rows(48),
            rows(32),
            jax.ShapeDtypeStruct((2, PACKED, LANES), F32),
        ],
        compiler_params=SMALL,
        name="gather_sends",
    )(packed, high, cross, second, first, weights[3])
    up = swap_inner(far, 1)
    low = swap_inner(near, 0)
    local, edge_near, edge_far, edge_over, far, near = pl.pallas_call(
        lambda *refs: pair_kernel(feat, pair_len, *refs),
        out_shape=[rows(16), rows(8), rows(8), rows(8), rows(32), rows(32)],
        scratch_shapes=[
            pltpu.VMEM((2, pair_len, pair_len), BF16),
            pltpu.VMEM((3, pair_len, LANES), BF16),
            pltpu.VMEM((2, 9 * feat, pair_len), BF16),
            pltpu.VMEM((2, 9 * feat, pair_len), F32),
            pltpu.VMEM((2, 9 * feat, pair_len), F32),
        ],
        compiler_params=LARGE,
        name="pair_terms",
    )(raw, mid, up, low, *weights)
    up = swap_inner(far, 1)
    low = swap_inner(near, 0)
    even_n = lax.axis_index("inner") % 2 == 0
    plus = jnp.where(even_n, low, up)
    minus = jnp.where(even_n, up, low)
    toward = jnp.concatenate([minus[16:24], edge_far, plus[16:24]], 0)
    away = jnp.concatenate([minus[8:16], edge_near, plus[8:16]], 0)
    inside = swap_outer(toward, 1, [o for o in range(count) if o % half not in (0, half - 1)])
    beside = swap_outer(away, 0, range(count))
    total, hot, toward = pl.pallas_call(
        begin_kernel,
        out_shape=[rows(16), jax.ShapeDtypeStruct((6 * 2 * LANES, LANES), BF16), rows(24)],
        compiler_params=SMALL,
        cost_estimate=pl.CostEstimate(flops=0, bytes_accessed=4_000_000, transcendentals=0),
        name="begin_terms",
    )(local, packed, up, low, edge_far)
    over = copy_rows(toward, {0: count - 1, half - 1: half})
    forces, energy = pl.pallas_call(
        collect_kernel,
        out_shape=[
            jax.ShapeDtypeStruct((3, atom_count), F32),
            jax.ShapeDtypeStruct((1, atom_count), F32),
        ],
        compiler_params=SMALL,
        name="collect_terms",
    )(total, hot, packed, up, low, edge_over, over, inside, beside)
    return forces, energy.reshape(atom_count)


def solution(mesh):
    return jax.shard_map(
        on_device,
        mesh=mesh,
        in_specs=(
            P(None, AXES),
            P(AXES),
            P(None, AXES),
            P(AXES),
            P(AXES),
            P(AXES),
            P(),
            P(),
            P(),
            P(),
            P(),
            P(),
        ),
        out_specs=(P(None, AXES), P(AXES)),
        check_vma=False,
    )
```

```python
import math

import jax
import jax.numpy as jnp
from jax import lax
from jax.experimental import pallas as pl
from jax.experimental.pallas import tpu as pltpu
from jax.sharding import PartitionSpec as P

AXES = ("outer", "inner")
CUTOFF = 6.0
ROOT3 = math.sqrt(3.0)
ROOT5 = math.sqrt(5.0)
ROOT15 = math.sqrt(15.0)
LANES = 128
F32 = jnp.float32
BF16 = jnp.bfloat16
SMALL = pltpu.CompilerParams(vmem_limit_bytes=8 * 1024 * 1024)
LARGE = pltpu.CompilerParams(vmem_limit_bytes=32 * 1024 * 1024)
DIRS = ((-1, -1), (-1, 0), (-1, 1), (0, -1), (0, 1), (1, -1), (1, 0), (1, 1))
TABLE, LISTS, CENTERS, NEIGH, PACKED = 0, 16, 32, 40, 48
LIVE = 38
ORDER_OF = (0, 1, 1, 1, 2, 2, 2, 2, 2)


def permute(block, place):
    outer_len = lax.axis_size("outer")
    inner_len = lax.axis_size("inner")
    route = []
    for o in range(outer_len):
        for n in range(inner_len):
            there = place(o, n)
            if there is not None:
                to = there[0] % outer_len * inner_len + there[1] % inner_len
                route.append((o * inner_len + n, to))
    return lax.ppermute(block, AXES, route)


def swap_inner(block, parity):
    return permute(block, lambda o, n: (o, n + 1 if n % 2 == parity else n - 1))


def swap_outer(block, parity, rows):
    def place(o, n):
        return (o + 1 if o % 2 == parity else o - 1, n) if o in rows else None

    return permute(block, place)


def copy_rows(block, rows):
    return permute(block, lambda o, n: (rows[o], n) if o in rows else None)


def row_kind():
    half = lax.axis_size("outer") // 2
    row = lax.axis_index("outer")
    place = lax.rem(row, half)
    return row < half, (place == 0) | (place == half - 1)


def dot(lhs, rhs):
    return jnp.dot(lhs, rhs, preferred_element_type=F32)


def dot_rows(lhs, rhs):
    return lax.dot_general(lhs, rhs, (((0,), (0,)), ((), ())), preferred_element_type=F32)


def parts(value, count):
    out = []
    for _ in range(count):
        piece = value.astype(BF16)
        out.append(piece)
        value = value - piece.astype(F32)
    return out


def hits(left, right):
    return jnp.where(left == right, jnp.ones((), BF16), jnp.zeros((), BF16))


def down_lanes(row):
    return jnp.broadcast_to(row, (LANES, LANES)).T.astype(BF16)


def onehot_low(low_row):
    rows = lax.broadcasted_iota(jnp.int32, (LANES, low_row.shape[1]), 0).astype(F32).astype(BF16)
    return hits(rows, low_row.astype(F32).astype(BF16))


def high_mask(high_row, group):
    rows = lax.broadcasted_iota(jnp.int32, (8, high_row.shape[1]), 0)
    return high_row == 2 * group + jnp.where(rows >= 4, 1, 0)


def gather(table, low_hot, high_row):
    size = table.shape[0]
    found = dot(jnp.concatenate(parts(table, 3), 0), low_hot)
    found = found[0:size] + found[size : 2 * size] + found[2 * size :]
    total = None
    for group in range(size // 8):
        term = jnp.where(high_mask(high_row, group), found[8 * group : 8 * group + 8], 0.0)
        total = term if total is None else total + term
    return total + pltpu.roll(total, 4, 0)


def scatter(values, low_hot_t, high_row, groups):
    spread = [jnp.where(high_mask(high_row, group), values, 0.0) for group in groups]
    spread = jnp.concatenate(spread, 0)
    size = 8 * len(groups)
    summed = dot(jnp.concatenate(parts(spread, 2), 0), low_hot_t)
    return summed[0:size] + summed[size:]


def pack_kernel(
    pos_hbm,
    spec_hbm,
    lists_hbm,
    centers_hbm,
    neigh_hbm,
    live_ref,
    out_ref,
    pos,
    spec,
    lists,
    centers,
    neigh,
    sems,
):
    fetched = []
    for j, (src, dst) in enumerate(
        (
            (pos_hbm, pos),
            (spec_hbm, spec),
            (lists_hbm, lists),
            (centers_hbm, centers),
            (neigh_hbm, neigh),
        )
    ):
        copy = pltpu.make_async_copy(src, dst, sems.at[j])
        copy.start()
        fetched.append(copy)
    for copy in fetched:
        copy.wait()
    rows = []
    for j in range(4):
        at = slice(j * LANES, (j + 1) * LANES)
        rows.append(pos[:, at])
        rows.append(spec[:, at].astype(F32))
    ids = lists[...].astype(F32)
    rest = ids.shape[1] - LANES
    rows.append(ids[:, 0:LANES])
    rows.append(jnp.concatenate([ids[:, LANES:], jnp.zeros((8, LANES - rest), F32)], 1))
    rows.append(centers[...].astype(F32))
    rows.append(jnp.full((1, LANES), live_ref[0].astype(F32)))
    rows.append(jnp.zeros((1, LANES), F32))
    rows.append(neigh[...].astype(F32))
    rows.append(jnp.zeros((2, LANES), F32))
    out_ref[...] = jnp.concatenate(rows, 0)


def weights_kernel(
    w_rad_hbm,
    emb_center_hbm,
    emb_neigh_hbm,
    w_env_hbm,
    w_lat_hbm,
    w_out_hbm,
    front_ref,
    w_env_ref,
    w_lat_ref,
    w_out_ref,
    w_rad,
    emb_center,
    emb_neigh,
    w_out,
    sems,
):
    fetched = []
    for j, (src, dst) in enumerate(
        (
            (w_rad_hbm, w_rad),
            (emb_center_hbm, emb_center),
            (emb_neigh_hbm, emb_neigh),
            (w_env_hbm, w_env_ref),
            (w_lat_hbm, w_lat_ref),
            (w_out_hbm, w_out),
        )
    ):
        copy = pltpu.make_async_copy(src, dst, sems.at[j])
        copy.start()
        fetched.append(copy)
    for copy in fetched:
        copy.wait()
    lat = w_lat_ref.shape[1]
    w1, w2, w3 = parts(w_rad[...], 3)
    none = jnp.zeros((1, lat), BF16)
    front_ref[...] = jnp.concatenate(
        [w1, w2, w1, w3, w2, w1, emb_center[...], none, emb_neigh[...], none], 0
    )
    w_lat_ref[lat:] = w_lat_ref[lat:] * jnp.full((), 2.0, BF16)
    w_out_ref[...] = jnp.broadcast_to(w_out[...], (16, lat))


def tile_at(extra, side):
    return 8 * (3 * extra + 1 - side)


def sends_kernel(
    own_ref, first_ref, border_ref, cross_ref, last_ref, _, far_ref, near_ref, mid_ref, raw_ref
):
    even_n = lax.axis_index("inner") % 2 == 0
    odd = lax.axis_index("outer") % 2 == 1
    low_half, _ = row_kind()
    rows = lax.broadcasted_iota(jnp.int32, (8, LANES), 0)
    own, cross = own_ref[...], cross_ref[...]
    beside = jnp.where(low_half, first_ref[...], last_ref[...])
    raw_ref[0] = own
    raw_ref[1] = cross

    def tiles_of(raw, sides):
        halves = [raw[LISTS + 8 * i : LISTS + 8 * i + 8].astype(jnp.int32) for i in range(2)]
        names, ids = [], []
        for side in sides:
            if side == 0:
                picked = [half[3:5] for half in halves]
                names += [(0, -1), (0, 1)]
            else:
                upper = odd if side > 0 else jnp.logical_not(odd)
                picked = [jnp.where(upper, half[5:8], half[0:3]) for half in halves]
                names += [(side, dy) for dy in (-1, 0, 1)]
            for i in range(picked[0].shape[0]):
                ids += [picked[0][i : i + 1], picked[1][i : i + 1]]
        ids = jnp.concatenate(ids, 1)
        taken = gather(raw[TABLE : TABLE + 16], onehot_low(ids & 127), ids >> 7)
        tiles = {}
        for j, name in enumerate(names):
            at = 2 * j * LANES
            tiles[name] = jnp.where(
                rows < 4, taken[:, at : at + LANES], taken[:, at + LANES : at + 2 * LANES]
            )
        return tiles

    by_own = tiles_of(own, (1, 0))
    by_cross = tiles_of(cross, (0, -1))
    by_beside = tiles_of(beside, (1,))
    by_border = tiles_of(border_ref[...], (-1,))
    sources = ({1: by_beside, 0: by_own, -1: by_cross}, {1: by_own, 0: by_cross, -1: by_border})
    for extra in range(2):
        for side in (1, 0, -1):
            tiles = sources[extra][side]
            minus, plus = tiles[side, -1], tiles[side, 1]
            at = tile_at(extra, side)
            far_ref[at : at + 8] = jnp.where(even_n, minus, plus)
            near_ref[at : at + 8] = jnp.where(even_n, plus, minus)
            if side:
                m = 8 * (2 * extra + (1 - side) // 2)
                mid_ref[m : m + 8] = tiles[side, 0]


def silu_parts(pre):
    sig = 0.5 * jnp.tanh(0.5 * pre) + 0.5
    act = pre * sig
    return act, sig + act - act * sig


def half_turns(value):
    whole = jnp.floor(value + 0.5)
    rest = (value - whole) * math.pi
    sign = 1.0 - 2.0 * (whole - 2.0 * jnp.floor(whole * 0.5))
    r2 = rest * rest
    sine, cosine = -1.0 / 39916800, 1.0 / 479001600
    for term in (1.0 / 362880, -1.0 / 5040, 1.0 / 120, -1.0 / 6, 1.0):
        sine = term + r2 * sine
    for term in (-1.0 / 3628800, 1.0 / 40320, -1.0 / 720, 1.0 / 24, -0.5, 1.0):
        cosine = term + r2 * cosine
    return sign * rest * sine, sign * cosine


def neigh_place(tile):
    neigh = tile.astype(jnp.int32)
    ghost = neigh - 512
    listed = (ghost * 745) >> 17
    entry = ghost - 176 * listed
    is_local = neigh < 512
    low = jnp.where(is_local, neigh & 127, entry & 127)
    high = jnp.where(is_local, neigh >> 7, 4 + 2 * listed + (entry >> 7))
    return low, high


def columns_kernel(raw_ref, down_ref, hot_t_ref):
    lanes = lax.broadcasted_iota(jnp.int32, (1, LANES), 1).astype(F32).astype(BF16)
    for d in range(2):
        centers = raw_ref[d, CENTERS : CENTERS + 8]
        low, _ = neigh_place(raw_ref[d, NEIGH : NEIGH + 8])
        low = low.astype(F32)
        own_low = (centers.astype(jnp.int32) & 127).astype(F32)
        for i in range(down_ref.shape[1] // LANES):
            at = slice(i * LANES, (i + 1) * LANES)
            down_ref[d, at] = down_lanes(centers[i : i + 1] - 256.0)
            hot_t_ref[d, at] = hits(down_lanes(low[i : i + 1]), lanes)
            if d == 0:
                hot_t_ref[2, at] = hits(down_lanes(own_low[i : i + 1]), lanes)


def pair_kernel(feat, pair_len, *refs):
    _, two = row_kind()
    pl.when(two)(lambda: pair_body(2, feat, pair_len, *refs))
    pl.when(jnp.logical_not(two))(lambda: pair_body(1, feat, pair_len, *refs))


def pair_body(
    count,
    feat,
    pair_len,
    raw_ref,
    mid_ref,
    up_ref,
    low_ref,
    down_ref,
    hot_t_ref,
    front_ref,
    w_env_ref,
    w_lat_ref,
    w_out_ref,
    local_ref,
    edge_near_ref,
    edge_far_ref,
    back_far_ref,
    back_near_ref,
    same_ref,
    contrib_ref,
    gath_ref,
    back_ref,
):
    chunks = pair_len // LANES
    lat = w_lat_ref.shape[1]
    even_n = lax.axis_index("inner") % 2 == 0
    odd = lax.axis_index("outer") % 2 == 1
    front = front_ref[...]
    w1, w2 = front[0:8], front[8:16]
    w_env = w_env_ref[...]
    w_lat = w_lat_ref[...]
    w_out = w_out_ref[0:8].astype(F32).T[:, 0:1]

    def as_row(tile):
        return jnp.concatenate([tile[i : i + 1] for i in range(chunks)], 1)

    def feat_rows(k):
        return slice(k * feat, (k + 1) * feat)

    def of_order(value, k):
        return value[feat_rows(ORDER_OF[k])]

    def domain(d):
        return slice(d * pair_len, (d + 1) * pair_len)

    def build_same(d):
        shifted = raw_ref[d, CENTERS : CENTERS + 8] - 256.0
        across = shifted.astype(BF16)
        for i in range(chunks):
            down = down_ref[d, i * LANES : (i + 1) * LANES]
            for j in range(chunks):
                same_ref[d, i * LANES : (i + 1) * LANES, j * LANES : (j + 1) * LANES] = hits(
                    down, across[j : j + 1]
                )

    def place(d):
        raw = raw_ref.at[d]
        centers = raw[CENTERS : CENTERS + 8]
        table = [raw[TABLE : TABLE + 16]]

        def ghost_tile(side, dy):
            if dy == 0:
                m = 8 * (2 * d + (1 - side) // 2)
                return mid_ref[m : m + 8]
            t = tile_at(d, side)
            by_low, by_up = low_ref[t : t + 8], up_ref[t : t + 8]
            return jnp.where(even_n, by_low, by_up) if dy < 0 else jnp.where(even_n, by_up, by_low)

        for dx, dy in DIRS:
            if dx == 0:
                table.append(ghost_tile(0, dy))
            else:
                table.append(jnp.where(odd, ghost_tile(dx, dy), ghost_tile(-dx, dy)))
        table = jnp.concatenate(table, 0)
        neigh_low, neigh_high = neigh_place(raw[NEIGH : NEIGH + 8])
        neigh_high = as_row(neigh_high)
        center_ids = as_row(centers.astype(jnp.int32))
        center_high = center_ids >> 7
        at_neigh = gather(table, onehot_low(as_row(neigh_low)), neigh_high)
        at_center = gather(table[0:16], onehot_low(center_ids & 127), center_high)
        block = lax.broadcasted_iota(jnp.int32, (1, pair_len), 1) // 128
        mask = jnp.where(block.astype(F32) < raw[LIVE : LIVE + 1, 0:1], 1.0, 0.0)
        return at_neigh, at_center, mask, neigh_high, center_high

    placed = [place(d) for d in range(count)]
    at_neigh, at_center, mask = (jnp.concatenate([p[i] for p in placed], 1) for i in range(3))
    width = mask.shape[1]
    moved = at_neigh - at_center
    rx, ry, rz = moved[0:1], moved[1:2], moved[2:3]
    squared = rx * rx + ry * ry + rz * rz + 1.0
    inv = lax.rsqrt(squared)
    dist = squared * inv
    ux, uy, uz = rx * inv, ry * inv, rz * inv
    slack = 1.0 - squared * (1.0 / (CUTOFF * CUTOFF))
    env = slack * slack
    scaled = env * mask
    ns = (lax.broadcasted_iota(jnp.int32, (8, width), 0) + 1).astype(F32)
    sine, cosine = half_turns(ns * (dist * (1.0 / CUTOFF)))
    scale = inv * env
    kinds = lax.broadcasted_iota(jnp.int32, (8, width), 0).astype(F32)
    hot_center = jnp.where(at_center[3:4] == kinds, 1.0, 0.0).astype(BF16)
    hot_neigh = jnp.where(at_neigh[3:4] == kinds, 1.0, 0.0).astype(BF16)
    b1, b2, b3 = parts(sine * scale, 3)
    pre = dot_rows(front, jnp.concatenate([b1, b1, b2, b1, b2, b3, hot_center, hot_neigh], 0))
    for d in range(count):
        build_same(d)
    latent, slope = silu_parts(pre)
    half = latent.astype(BF16)
    raw = dot(w_env, half)
    weight = raw * scaled
    shape = [
        None,
        ROOT3 * ux,
        ROOT3 * uy,
        ROOT3 * uz,
        ROOT15 * ux * uy,
        ROOT15 * uy * uz,
        0.5 * ROOT5 * (2.0 * uz * uz - ux * ux - uy * uy),
        ROOT15 * ux * uz,
        0.5 * ROOT15 * (ux * ux - uy * uy),
    ]
    shape_half = [None] + [row.astype(BF16) for row in shape[1:]]

    def spread_same(d, value, out_ref):
        at = domain(d)
        value = value[:, at]
        for k in range(9):
            rows = of_order(value, k)
            contrib_ref[d, feat_rows(k)] = (rows if k == 0 else rows * shape[k][:, at]).astype(BF16)
        out_ref[d] = dot(contrib_ref[d], same_ref[d])

    def gathered_sums(d, in_ref):
        at = domain(d)
        sums = [None, None, None]
        for k in range(9):
            term = in_ref[d, feat_rows(k)]
            if k:
                term = term * shape[k][:, at]
            order = ORDER_OF[k]
            sums[order] = term if sums[order] is None else sums[order] + term
        return jnp.concatenate(sums, 0)

    for d in range(count):
        spread_same(d, weight, gath_ref)
    sums = jnp.concatenate([gathered_sums(d, gath_ref) for d in range(count)], 1)
    joined = jnp.concatenate([half, (weight * sums).astype(BF16)], 0)
    update, slope2 = silu_parts(dot_rows(w_lat, joined))
    refined = (latent + update).astype(BF16)
    raw_energy = dot(w_out_ref[...], refined)[0:1]
    d_refined = scaled * w_out
    d_joined = dot(w_lat, (d_refined * slope2).astype(BF16))
    d_latent = d_refined + d_joined[:lat]
    d_inv = d_joined[lat:]
    d_weight = d_inv * sums
    d_sums = d_inv * weight
    for d in range(count):
        spread_same(d, d_sums, back_ref)
    d_order, d_shape = [], []
    for d in range(count):
        at = domain(d)
        d_order.append(gathered_sums(d, back_ref))
        here = []
        for k in range(1, 9):
            both = (
                of_order(d_sums, k)[:, at] * gath_ref[d, feat_rows(k)]
                + of_order(weight, k)[:, at] * back_ref[d, feat_rows(k)]
            )
            here.append(jnp.sum(both, axis=0, keepdims=True))
        d_shape.append(here)
    d_weight = d_weight + jnp.concatenate(d_order, 1)
    d_shape = [None] + [jnp.concatenate([here[k] for here in d_shape], 1) for k in range(8)]
    d_scaled = raw_energy + jnp.sum(d_weight * raw, axis=0, keepdims=True)
    d_latent = d_latent + scaled * dot_rows(w_env, d_weight.astype(BF16))
    d_pre = (d_latent * slope).astype(BF16)
    d_basis = dot(jnp.concatenate([w1, w2], 0), d_pre)
    d_basis = d_basis[0:8] + d_basis[8:16]

    along = jnp.sum(d_basis * sine, axis=0, keepdims=True)
    turned = jnp.sum(d_basis * cosine * ns, axis=0, keepdims=True)
    d_env = along * inv + mask * d_scaled
    dx = (
        ROOT3 * d_shape[1]
        + ROOT15 * (uy * d_shape[4] + uz * d_shape[7] + ux * d_shape[8])
        - ROOT5 * ux * d_shape[6]
    )
    dy = (
        ROOT3 * d_shape[2]
        + ROOT15 * (ux * d_shape[4] + uz * d_shape[5] - uy * d_shape[8])
        - ROOT5 * uy * d_shape[6]
    )
    dz = (
        ROOT3 * d_shape[3]
        + ROOT15 * (uy * d_shape[5] + ux * d_shape[7])
        + 2.0 * ROOT5 * uz * d_shape[6]
    )
    d_inv = along * env + dx * rx + dy * ry + dz * rz
    d_dist = turned * (math.pi / CUTOFF) * scale - d_inv * inv * inv
    d_squared = 0.5 * inv * d_dist - (2.0 / (CUTOFF * CUTOFF)) * slack * d_env
    gx = dx * inv + 2.0 * rx * d_squared
    gy = dy * inv + 2.0 * ry * d_squared
    gz = dz * inv + 2.0 * rz * d_squared
    rows4 = [gx, gy, gz, 0.5 * scaled * raw_energy]
    values = jnp.concatenate(rows4 + rows4, 0)
    rows = lax.broadcasted_iota(jnp.int32, (8, width), 0)
    flipped = jnp.where((rows & 3) == 3, values, -values)
    first = jnp.where(odd, 5, 0)

    def groups_of(side):
        return [2 + (first if side > 0 else 5 - first) + i for i in range(3)]

    neigh_high, center_high = placed[0][3:]
    groups = [0, 1, 2 + 3, 2 + 4] + groups_of(1) + (groups_of(-1) if count == 1 else [])
    terms = scatter(flipped[:, domain(0)], hot_t_ref[0], neigh_high, groups)
    center_terms = scatter(values[:, domain(0)], hot_t_ref[2], center_high, (0, 1))
    local_ref[...] = terms[0:16] + center_terms
    tiles = [terms[8 * i : 8 * i + 8] for i in range(2, len(groups))]
    if count == 2:
        terms = scatter(flipped[:, domain(1)], hot_t_ref[1], placed[1][3], groups_of(1))
        tiles += [terms[8 * i : 8 * i + 8] for i in range(3)]
    edge_near_ref[...] = tiles[3]
    edge_far_ref[...] = tiles[6]
    for j, (minus, plus) in enumerate(
        (
            (tiles[0], tiles[1]),
            (tiles[2], tiles[4]),
            (tiles[5], tiles[7]),
        )
    ):
        at = slice(8 * j, 8 * j + 8)
        back_far_ref[at] = jnp.where(even_n, plus, minus)
        back_near_ref[at] = jnp.where(even_n, minus, plus)


def list_rows(raw_ref):
    odd = lax.axis_index("outer") % 2 == 1
    low = raw_ref[LISTS : LISTS + 8].astype(jnp.int32)
    high = raw_ref[LISTS + 8 : LISTS + 16].astype(jnp.int32)
    wide = jnp.concatenate([low, high], 1)
    below, above = wide[0:3], wide[5:8]
    return jnp.where(odd, below, above), jnp.where(odd, above, below), wide[3:5]


def flat(ids):
    return jnp.concatenate([ids[i : i + 1] for i in range(ids.shape[0])], 1)


def spread_tile(tile):
    rows = lax.broadcasted_iota(jnp.int32, (8, LANES), 0)
    turned = pltpu.roll(tile, 4, 0)
    return [jnp.where(rows < 4, tile, turned), jnp.where(rows < 4, turned, tile)]


def hot_rows(ids):
    lanes = lax.broadcasted_iota(jnp.int32, (1, LANES), 1).astype(F32).astype(BF16)
    low = (ids & 127).astype(F32)
    return jnp.concatenate(
        [
            hits(down_lanes(low[:, i : i + LANES]), lanes)
            for i in range(0, ids.shape[1], LANES)
        ],
        0,
    )


def begin_kernel(
    local_ref, raw_ref, up_ref, low_ref, total_ref, hot_ref
):
    even_n = lax.axis_index("inner") % 2 == 0
    away, toward, along = list_rows(raw_ref)
    plus = jnp.where(even_n, low_ref[0:8], up_ref[0:8])
    minus = jnp.where(even_n, up_ref[0:8], low_ref[0:8])
    ids = flat(along)
    values = jnp.concatenate(spread_tile(minus) + spread_tile(plus), 1)
    total_ref[...] = local_ref[...] + scatter(values, hot_rows(ids), ids >> 7, (0, 1))
    hot_ref[...] = hot_rows(jnp.concatenate([flat(away), flat(toward)], 1))


def collect_kernel(
    total_ref,
    hot_ref,
    raw_ref,
    up_ref,
    low_ref,
    edge_far_ref,
    beside_ref,
    inside_ref,
    forces_ref,
    energy_ref,
):
    even_n = lax.axis_index("inner") % 2 == 0
    _, at_border = row_kind()
    plus = jnp.where(even_n, low_ref[16:24], up_ref[16:24])
    minus = jnp.where(even_n, up_ref[16:24], low_ref[16:24])
    over = jnp.concatenate([minus, edge_far_ref[...], plus], 0)
    toward = jnp.where(at_border, over, inside_ref[...])
    away = beside_ref[...]
    ids = list_rows(raw_ref)
    ids = jnp.concatenate([flat(ids[0]), flat(ids[1])], 1)
    values = []
    for tiles in (away, toward):
        for j in range(3):
            values += spread_tile(tiles[8 * j : 8 * j + 8])
    values = jnp.concatenate(values, 1)
    total = total_ref[...] + scatter(values, hot_ref[...], ids >> 7, (0, 1))
    for j in range(4):
        forces_ref[:, j * LANES : (j + 1) * LANES] = total[4 * j : 4 * j + 3]
        energy_ref[:, j * LANES : (j + 1) * LANES] = total[4 * j + 3 : 4 * j + 4]


def on_device(
    positions,
    species,
    send_lists,
    centers,
    neighbours,
    live_blocks,
    w_rad,
    emb_center,
    emb_neigh,
    w_env,
    w_lat,
    w_out,
):
    pair_len = centers.shape[0]
    atom_count = positions.shape[1]
    feat = w_env.shape[1] // 3
    lat = w_env.shape[0]
    chunks = pair_len // LANES

    def rows(count):
        return jax.ShapeDtypeStruct((count, LANES), F32)

    packed = pl.pallas_call(
        pack_kernel,
        out_shape=rows(PACKED),
        in_specs=[pl.BlockSpec(memory_space=pltpu.HBM)] * 5
        + [pl.BlockSpec(memory_space=pltpu.SMEM)],
        scratch_shapes=[
            pltpu.VMEM(positions.shape, F32),
            pltpu.VMEM((1, atom_count), jnp.int32),
            pltpu.VMEM(send_lists.shape, jnp.int32),
            pltpu.VMEM((chunks, LANES), jnp.int32),
            pltpu.VMEM((chunks, LANES), jnp.int32),
            pltpu.SemaphoreType.DMA((5,)),
        ],
        compiler_params=SMALL,
        name="pack_domain",
    )(
        *(
            pltpu.with_memory_space_constraint(value, pltpu.HBM)
            for value in (
                positions,
                species.reshape(1, atom_count),
                send_lists,
                centers.reshape(chunks, LANES),
                neighbours.reshape(chunks, LANES),
            )
        ),
        live_blocks,
    )
    weights = pl.pallas_call(
        weights_kernel,
        out_shape=[
            jax.ShapeDtypeStruct((64, lat), BF16),
            jax.ShapeDtypeStruct((w_env.shape[1], lat), BF16),
            jax.ShapeDtypeStruct(w_lat.shape, BF16),
            jax.ShapeDtypeStruct((16, lat), BF16),
        ],
        in_specs=[pl.BlockSpec(memory_space=pltpu.HBM)] * 6,
        scratch_shapes=[
            pltpu.VMEM(w_rad.shape, F32),
            pltpu.VMEM(emb_center.shape, BF16),
            pltpu.VMEM(emb_neigh.shape, BF16),
            pltpu.VMEM((1, lat), BF16),
            pltpu.SemaphoreType.DMA((6,)),
        ],
        compiler_params=SMALL,
        cost_estimate=pl.CostEstimate(flops=0, bytes_accessed=4_000_000, transcendentals=0),
        name="place_weights",
    )(
        *(
            pltpu.with_memory_space_constraint(value, pltpu.HBM)
            for value in (w_rad, emb_center, emb_neigh, w_env.T, w_lat, w_out.reshape(1, -1))
        )
    )
    count = lax.axis_size("outer")
    half = count // 2
    low, high = half - 1, count - 1
    first = swap_outer(packed, 0, range(half))
    border = copy_rows(packed, {1: high, low - 1: half, half + 1: low, high - 1: 0})
    cross = swap_outer(packed, 1, range(count))
    last = swap_outer(packed, 0, range(half, count))
    far, near, mid, raw = pl.pallas_call(
        sends_kernel,
        out_shape=[
            rows(48),
            rows(48),
            rows(32),
            jax.ShapeDtypeStruct((2, PACKED, LANES), F32),
        ],
        compiler_params=SMALL,
        name="gather_sends",
    )(packed, first, border, cross, last, weights[3])
    up = swap_inner(far, 1)
    low = swap_inner(near, 0)
    down, hot_t = pl.pallas_call(
        columns_kernel,
        out_shape=[
            jax.ShapeDtypeStruct((2, pair_len, LANES), BF16),
            jax.ShapeDtypeStruct((3, pair_len, LANES), BF16),
        ],
        compiler_params=SMALL,
        cost_estimate=pl.CostEstimate(flops=0, bytes_accessed=4_000_000, transcendentals=0),
        name="pair_columns",
    )(raw)
    local, edge_near, edge_far, far, near = pl.pallas_call(
        lambda *refs: pair_kernel(feat, pair_len, *refs),
        out_shape=[rows(16), rows(8), rows(8), rows(24), rows(24)],
        scratch_shapes=[
            pltpu.VMEM((2, pair_len, pair_len), BF16),
            pltpu.VMEM((2, 9 * feat, pair_len), BF16),
            pltpu.VMEM((2, 9 * feat, pair_len), F32),
            pltpu.VMEM((2, 9 * feat, pair_len), F32),
        ],
        compiler_params=LARGE,
        name="pair_terms",
    )(raw, mid, up, low, down, hot_t, *weights)
    up = swap_inner(far, 1)
    low = swap_inner(near, 0)
    even_n = lax.axis_index("inner") % 2 == 0
    plus = jnp.where(even_n, low, up)
    minus = jnp.where(even_n, up, low)
    toward = jnp.concatenate([minus[16:24], edge_far, plus[16:24]], 0)
    away = jnp.concatenate([minus[8:16], edge_near, plus[8:16]], 0)
    inside = swap_outer(toward, 1, [o for o in range(count) if o % half not in (0, half - 1)])
    beside = swap_outer(away, 0, range(count))
    total, hot = pl.pallas_call(
        begin_kernel,
        out_shape=[rows(16), jax.ShapeDtypeStruct((6 * 2 * LANES, LANES), BF16)],
        compiler_params=SMALL,
        cost_estimate=pl.CostEstimate(flops=0, bytes_accessed=4_000_000, transcendentals=0),
        name="begin_terms",
    )(local, packed, up, low)
    forces, energy = pl.pallas_call(
        collect_kernel,
        out_shape=[
            jax.ShapeDtypeStruct((3, atom_count), F32),
            jax.ShapeDtypeStruct((1, atom_count), F32),
        ],
        compiler_params=SMALL,
        name="collect_terms",
    )(total, hot, packed, up, low, edge_far, beside, inside)
    return forces, energy.reshape(atom_count)


def solution(mesh):
    return jax.shard_map(
        on_device,
        mesh=mesh,
        in_specs=(
            P(None, AXES),
            P(AXES),
            P(None, AXES),
            P(AXES),
            P(AXES),
            P(AXES),
            P(),
            P(),
            P(),
            P(),
            P(),
            P(),
        ),
        out_specs=(P(None, AXES), P(AXES)),
        check_vma=False,
    )
```

```python
import math

import jax
import jax.numpy as jnp
from jax import lax
from jax.experimental import pallas as pl
from jax.experimental.pallas import tpu as pltpu
from jax.sharding import PartitionSpec as P

AXES = ("outer", "inner")
CUTOFF = 6.0
ROOT3 = math.sqrt(3.0)
ROOT5 = math.sqrt(5.0)
ROOT15 = math.sqrt(15.0)
LANES = 128
F32 = jnp.float32
BF16 = jnp.bfloat16
SMALL = pltpu.CompilerParams(vmem_limit_bytes=8 * 1024 * 1024)
LARGE = pltpu.CompilerParams(vmem_limit_bytes=32 * 1024 * 1024)
DIRS = ((-1, -1), (-1, 0), (-1, 1), (0, -1), (0, 1), (1, -1), (1, 0), (1, 1))
TABLE, LISTS, CENTERS, NEIGH, PACKED = 0, 16, 32, 40, 48
LIVE = 38
ORDER_OF = (0, 1, 1, 1, 2, 2, 2, 2, 2)


def permute(block, place):
    outer_len = lax.axis_size("outer")
    inner_len = lax.axis_size("inner")
    route = []
    for o in range(outer_len):
        for n in range(inner_len):
            there = place(o, n)
            if there is not None:
                to = there[0] % outer_len * inner_len + there[1] % inner_len
                route.append((o * inner_len + n, to))
    return lax.ppermute(block, AXES, route)


def swap_inner(block, parity):
    return permute(block, lambda o, n: (o, n + 1 if n % 2 == parity else n - 1))


def swap_outer(block, parity, rows):
    def place(o, n):
        return (o + 1 if o % 2 == parity else o - 1, n) if o in rows else None

    return permute(block, place)


def copy_rows(block, rows):
    return permute(block, lambda o, n: (rows[o], n) if o in rows else None)


def row_kind():
    half = lax.axis_size("outer") // 2
    row = lax.axis_index("outer")
    place = lax.rem(row, half)
    return row < half, (place == 0) | (place == half - 1)


def dot(lhs, rhs):
    return jnp.dot(lhs, rhs, preferred_element_type=F32)


def dot_rows(lhs, rhs):
    return lax.dot_general(lhs, rhs, (((0,), (0,)), ((), ())), preferred_element_type=F32)


def parts(value, count):
    out = []
    for _ in range(count):
        piece = value.astype(BF16)
        out.append(piece)
        value = value - piece.astype(F32)
    return out


def hits(left, right):
    return jnp.where(left == right, jnp.ones((), BF16), jnp.zeros((), BF16))


def down_lanes(row):
    return jnp.broadcast_to(row, (LANES, LANES)).T.astype(BF16)


def onehot_low(low_row):
    rows = lax.broadcasted_iota(jnp.int32, (LANES, low_row.shape[1]), 0).astype(F32).astype(BF16)
    return hits(rows, low_row.astype(F32).astype(BF16))


def high_mask(high_row, group):
    rows = lax.broadcasted_iota(jnp.int32, (8, high_row.shape[1]), 0)
    return high_row == 2 * group + jnp.where(rows >= 4, 1, 0)


def gather(table, low_hot, high_row):
    size = table.shape[0]
    found = dot(jnp.concatenate(parts(table, 3), 0), low_hot)
    found = found[0:size] + found[size : 2 * size] + found[2 * size :]
    total = None
    for group in range(size // 8):
        term = jnp.where(high_mask(high_row, group), found[8 * group : 8 * group + 8], 0.0)
        total = term if total is None else total + term
    return total + pltpu.roll(total, 4, 0)


def scatter(values, low_hot_t, high_row, groups):
    spread = [jnp.where(high_mask(high_row, group), values, 0.0) for group in groups]
    spread = jnp.concatenate(spread, 0)
    size = 8 * len(groups)
    summed = dot(jnp.concatenate(parts(spread, 2), 0), low_hot_t)
    return summed[0:size] + summed[size:]


def pack_kernel(
    pos_hbm,
    spec_hbm,
    lists_hbm,
    centers_hbm,
    neigh_hbm,
    live_ref,
    out_ref,
    pos,
    spec,
    lists,
    centers,
    neigh,
    sems,
):
    fetched = []
    for j, (src, dst) in enumerate(
        (
            (pos_hbm, pos),
            (spec_hbm, spec),
            (lists_hbm, lists),
            (centers_hbm, centers),
            (neigh_hbm, neigh),
        )
    ):
        copy = pltpu.make_async_copy(src, dst, sems.at[j])
        copy.start()
        fetched.append(copy)
    for copy in fetched:
        copy.wait()
    rows = []
    for j in range(4):
        at = slice(j * LANES, (j + 1) * LANES)
        rows.append(pos[:, at])
        rows.append(spec[:, at].astype(F32))
    ids = lists[...].astype(F32)
    rest = ids.shape[1] - LANES
    rows.append(ids[:, 0:LANES])
    rows.append(jnp.concatenate([ids[:, LANES:], jnp.zeros((8, LANES - rest), F32)], 1))
    rows.append(centers[...].astype(F32))
    rows.append(jnp.full((1, LANES), live_ref[0].astype(F32)))
    rows.append(jnp.zeros((1, LANES), F32))
    rows.append(neigh[...].astype(F32))
    rows.append(jnp.zeros((2, LANES), F32))
    out_ref[...] = jnp.concatenate(rows, 0)


def weights_kernel(
    w_rad_hbm,
    w_env_hbm,
    w_lat_hbm,
    emb_center_ref,
    emb_neigh_ref,
    w_out_in_ref,
    front_ref,
    w_env_ref,
    w_lat_ref,
    w_out_ref,
    w_rad,
    sems,
):
    fetched = []
    for j, (src, dst) in enumerate(
        ((w_rad_hbm, w_rad), (w_env_hbm, w_env_ref), (w_lat_hbm, w_lat_ref))
    ):
        copy = pltpu.make_async_copy(src, dst, sems.at[j])
        copy.start()
        fetched.append(copy)
    for copy in fetched:
        copy.wait()
    lat = w_lat_ref.shape[1]
    w1, w2, w3 = parts(w_rad[...], 3)
    none = jnp.zeros((1, lat), BF16)
    front_ref[...] = jnp.concatenate(
        [w1, w2, w1, w3, w2, w1, emb_center_ref[...], none, emb_neigh_ref[...], none], 0
    )
    w_lat_ref[lat:] = w_lat_ref[lat:] * jnp.full((), 2.0, BF16)
    w_out_ref[...] = jnp.broadcast_to(w_out_in_ref[...], (16, lat))


def tile_at(extra, side):
    return 8 * (3 * extra + 1 - side)


def sends_kernel(
    own_ref, first_ref, border_ref, cross_ref, last_ref, _, far_ref, near_ref, mid_ref, raw_ref
):
    even_n = lax.axis_index("inner") % 2 == 0
    odd = lax.axis_index("outer") % 2 == 1
    low_half, _ = row_kind()
    rows = lax.broadcasted_iota(jnp.int32, (8, LANES), 0)
    own, cross = own_ref[...], cross_ref[...]
    beside = jnp.where(low_half, first_ref[...], last_ref[...])
    raw_ref[0] = own
    raw_ref[1] = cross

    def tiles_of(raw, sides):
        halves = [raw[LISTS + 8 * i : LISTS + 8 * i + 8].astype(jnp.int32) for i in range(2)]
        names, ids = [], []
        for side in sides:
            if side == 0:
                picked = [half[3:5] for half in halves]
                names += [(0, -1), (0, 1)]
            else:
                upper = odd if side > 0 else jnp.logical_not(odd)
                picked = [jnp.where(upper, half[5:8], half[0:3]) for half in halves]
                names += [(side, dy) for dy in (-1, 0, 1)]
            for i in range(picked[0].shape[0]):
                ids += [picked[0][i : i + 1], picked[1][i : i + 1]]
        ids = jnp.concatenate(ids, 1)
        taken = gather(raw[TABLE : TABLE + 16], onehot_low(ids & 127), ids >> 7)
        tiles = {}
        for j, name in enumerate(names):
            at = 2 * j * LANES
            tiles[name] = jnp.where(
                rows < 4, taken[:, at : at + LANES], taken[:, at + LANES : at + 2 * LANES]
            )
        return tiles

    by_own = tiles_of(own, (1, 0))
    by_cross = tiles_of(cross, (0, -1))
    by_beside = tiles_of(beside, (1,))
    by_border = tiles_of(border_ref[...], (-1,))
    sources = ({1: by_beside, 0: by_own, -1: by_cross}, {1: by_own, 0: by_cross, -1: by_border})
    for extra in range(2):
        for side in (1, 0, -1):
            tiles = sources[extra][side]
            minus, plus = tiles[side, -1], tiles[side, 1]
            at = tile_at(extra, side)
            far_ref[at : at + 8] = jnp.where(even_n, minus, plus)
            near_ref[at : at + 8] = jnp.where(even_n, plus, minus)
            if side:
                m = 8 * (2 * extra + (1 - side) // 2)
                mid_ref[m : m + 8] = tiles[side, 0]


def silu_parts(pre):
    sig = 0.5 * jnp.tanh(0.5 * pre) + 0.5
    act = pre * sig
    return act, sig + act - act * sig


def half_turns(value):
    whole = jnp.floor(value + 0.5)
    rest = (value - whole) * math.pi
    sign = 1.0 - 2.0 * (whole - 2.0 * jnp.floor(whole * 0.5))
    r2 = rest * rest
    sine, cosine = -1.0 / 39916800, 1.0 / 479001600
    for term in (1.0 / 362880, -1.0 / 5040, 1.0 / 120, -1.0 / 6, 1.0):
        sine = term + r2 * sine
    for term in (-1.0 / 3628800, 1.0 / 40320, -1.0 / 720, 1.0 / 24, -0.5, 1.0):
        cosine = term + r2 * cosine
    return sign * rest * sine, sign * cosine


def neigh_place(tile):
    neigh = tile.astype(jnp.int32)
    ghost = neigh - 512
    listed = (ghost * 745) >> 17
    entry = ghost - 176 * listed
    is_local = neigh < 512
    low = jnp.where(is_local, neigh & 127, entry & 127)
    high = jnp.where(is_local, neigh >> 7, 4 + 2 * listed + (entry >> 7))
    return low, high


def columns_kernel(raw_ref, down_ref, hot_t_ref):
    lanes = lax.broadcasted_iota(jnp.int32, (1, LANES), 1).astype(F32).astype(BF16)
    for d in range(2):
        centers = raw_ref[d, CENTERS : CENTERS + 8]
        low, _ = neigh_place(raw_ref[d, NEIGH : NEIGH + 8])
        low = low.astype(F32)
        own_low = (centers.astype(jnp.int32) & 127).astype(F32)
        for i in range(down_ref.shape[1] // LANES):
            at = slice(i * LANES, (i + 1) * LANES)
            down_ref[d, at] = down_lanes(centers[i : i + 1] - 256.0)
            hot_t_ref[d, at] = hits(down_lanes(low[i : i + 1]), lanes)
            if d == 0:
                hot_t_ref[2, at] = hits(down_lanes(own_low[i : i + 1]), lanes)


def pair_kernel(feat, pair_len, *refs):
    _, two = row_kind()
    pl.when(two)(lambda: pair_body(2, feat, pair_len, *refs))
    pl.when(jnp.logical_not(two))(lambda: pair_body(1, feat, pair_len, *refs))


def pair_body(
    count,
    feat,
    pair_len,
    raw_ref,
    mid_ref,
    up_ref,
    low_ref,
    down_ref,
    hot_t_ref,
    front_ref,
    w_env_ref,
    w_lat_ref,
    w_out_ref,
    local_ref,
    edge_near_ref,
    edge_far_ref,
    back_far_ref,
    back_near_ref,
    same_ref,
    contrib_ref,
    gath_ref,
    back_ref,
):
    chunks = pair_len // LANES
    lat = w_lat_ref.shape[1]
    even_n = lax.axis_index("inner") % 2 == 0
    odd = lax.axis_index("outer") % 2 == 1
    front = front_ref[...]
    w_env = w_env_ref[...]
    w_lat = w_lat_ref[...]
    w_out = w_out_ref[...].astype(F32).T[:, 0:1]

    def as_row(tile):
        return jnp.concatenate([tile[i : i + 1] for i in range(chunks)], 1)

    def feat_rows(k):
        return slice(k * feat, (k + 1) * feat)

    def of_order(value, k):
        return value[feat_rows(ORDER_OF[k])]

    def domain(d):
        return slice(d * pair_len, (d + 1) * pair_len)

    def build_same(d):
        shifted = raw_ref[d, CENTERS : CENTERS + 8] - 256.0
        across = shifted.astype(BF16)
        for i in range(chunks):
            down = down_ref[d, i * LANES : (i + 1) * LANES]
            for j in range(chunks):
                same_ref[d, i * LANES : (i + 1) * LANES, j * LANES : (j + 1) * LANES] = hits(
                    down, across[j : j + 1]
                )

    def place(d):
        raw = raw_ref.at[d]
        centers = raw[CENTERS : CENTERS + 8]
        table = [raw[TABLE : TABLE + 16]]

        def ghost_tile(side, dy):
            if dy == 0:
                m = 8 * (2 * d + (1 - side) // 2)
                return mid_ref[m : m + 8]
            t = tile_at(d, side)
            by_low, by_up = low_ref[t : t + 8], up_ref[t : t + 8]
            return jnp.where(even_n, by_low, by_up) if dy < 0 else jnp.where(even_n, by_up, by_low)

        for dx, dy in DIRS:
            if dx == 0:
                table.append(ghost_tile(0, dy))
            else:
                table.append(jnp.where(odd, ghost_tile(dx, dy), ghost_tile(-dx, dy)))
        table = jnp.concatenate(table, 0)
        neigh_low, neigh_high = neigh_place(raw[NEIGH : NEIGH + 8])
        neigh_high = as_row(neigh_high)
        center_ids = as_row(centers.astype(jnp.int32))
        center_high = center_ids >> 7
        at_neigh = gather(table, onehot_low(as_row(neigh_low)), neigh_high)
        at_center = gather(table[0:16], onehot_low(center_ids & 127), center_high)
        block = lax.broadcasted_iota(jnp.int32, (1, pair_len), 1) // 128
        mask = jnp.where(block.astype(F32) < raw[LIVE : LIVE + 1, 0:1], 1.0, 0.0)
        return at_neigh, at_center, mask, neigh_high, center_high

    placed = [place(d) for d in range(count)]
    at_neigh, at_center, mask = (jnp.concatenate([p[i] for p in placed], 1) for i in range(3))
    width = mask.shape[1]
    moved = at_neigh - at_center
    rx, ry, rz = moved[0:1], moved[1:2], moved[2:3]
    squared = rx * rx + ry * ry + rz * rz + 1.0
    inv = lax.rsqrt(squared)
    dist = squared * inv
    ux, uy, uz = rx * inv, ry * inv, rz * inv
    slack = 1.0 - squared * (1.0 / (CUTOFF * CUTOFF))
    env = slack * slack
    scaled = env * mask
    ns = (lax.broadcasted_iota(jnp.int32, (8, width), 0) + 1).astype(F32)
    sine, cosine = half_turns(ns * (dist * (1.0 / CUTOFF)))
    scale = inv * env
    kinds = lax.broadcasted_iota(jnp.int32, (8, width), 0).astype(F32)
    hot_center = jnp.where(at_center[3:4] == kinds, 1.0, 0.0).astype(BF16)
    hot_neigh = jnp.where(at_neigh[3:4] == kinds, 1.0, 0.0).astype(BF16)
    b1, b2, b3 = parts(sine * scale, 3)
    pre = dot_rows(front, jnp.concatenate([b1, b1, b2, b1, b2, b3, hot_center, hot_neigh], 0))
    for d in range(count):
        build_same(d)
    latent, slope = silu_parts(pre)
    half = latent.astype(BF16)
    raw = dot(w_env, half)
    weight = raw * scaled
    shape = [
        None,
        ROOT3 * ux,
        ROOT3 * uy,
        ROOT3 * uz,
        ROOT15 * ux * uy,
        ROOT15 * uy * uz,
        0.5 * ROOT5 * (2.0 * uz * uz - ux * ux - uy * uy),
        ROOT15 * ux * uz,
        0.5 * ROOT15 * (ux * ux - uy * uy),
    ]
    shape_half = [None] + [row.astype(BF16) for row in shape[1:]]

    def spread_same(d, value, out_ref):
        at = domain(d)
        value = value[:, at]
        for k in range(9):
            rows = of_order(value, k)
            contrib_ref[d, feat_rows(k)] = (rows if k == 0 else rows * shape[k][:, at]).astype(BF16)
        out_ref[d] = dot(contrib_ref[d], same_ref[d])

    def gathered_sums(d, in_ref):
        at = domain(d)
        sums = [None, None, None]
        for k in range(9):
            term = in_ref[d, feat_rows(k)]
            if k:
                term = term * shape[k][:, at]
            order = ORDER_OF[k]
            sums[order] = term if sums[order] is None else sums[order] + term
        return jnp.concatenate(sums, 0)

    for d in range(count):
        spread_same(d, weight, gath_ref)
    sums = jnp.concatenate([gathered_sums(d, gath_ref) for d in range(count)], 1)
    joined = jnp.concatenate([half, (weight * sums).astype(BF16)], 0)
    update, slope2 = silu_parts(dot_rows(w_lat, joined))
    refined = (latent + update).astype(BF16)
    raw_energy = dot(w_out_ref[...], refined)[0:1]
    d_refined = scaled * w_out
    d_joined = dot(w_lat, (d_refined * slope2).astype(BF16))
    d_latent = d_refined + d_joined[:lat]
    d_inv = d_joined[lat:]
    d_weight = d_inv * sums
    d_sums = d_inv * weight
    for d in range(count):
        spread_same(d, d_sums, back_ref)
    d_order, d_shape = [], []
    for d in range(count):
        at = domain(d)
        d_order.append(gathered_sums(d, back_ref))
        here = []
        for k in range(1, 9):
            both = (
                of_order(d_sums, k)[:, at] * gath_ref[d, feat_rows(k)]
                + of_order(weight, k)[:, at] * back_ref[d, feat_rows(k)]
            )
            here.append(jnp.sum(both, axis=0, keepdims=True))
        d_shape.append(here)
    d_weight = d_weight + jnp.concatenate(d_order, 1)
    d_shape = [None] + [jnp.concatenate([here[k] for here in d_shape], 1) for k in range(8)]
    d_scaled = raw_energy + jnp.sum(d_weight * raw, axis=0, keepdims=True)
    d_latent = d_latent + scaled * dot_rows(w_env, d_weight.astype(BF16))
    d_pre = (d_latent * slope).astype(BF16)
    d_basis = dot(front_ref[0:16], d_pre)
    d_basis = d_basis[0:8] + d_basis[8:16]

    along = jnp.sum(d_basis * sine, axis=0, keepdims=True)
    turned = jnp.sum(d_basis * cosine * ns, axis=0, keepdims=True)
    d_env = along * inv + mask * d_scaled
    dx = (
        ROOT3 * d_shape[1]
        + ROOT15 * (uy * d_shape[4] + uz * d_shape[7] + ux * d_shape[8])
        - ROOT5 * ux * d_shape[6]
    )
    dy = (
        ROOT3 * d_shape[2]
        + ROOT15 * (ux * d_shape[4] + uz * d_shape[5] - uy * d_shape[8])
        - ROOT5 * uy * d_shape[6]
    )
    dz = (
        ROOT3 * d_shape[3]
        + ROOT15 * (uy * d_shape[5] + ux * d_shape[7])
        + 2.0 * ROOT5 * uz * d_shape[6]
    )
    d_inv = along * env + dx * rx + dy * ry + dz * rz
    d_dist = turned * (math.pi / CUTOFF) * scale - d_inv * inv * inv
    d_squared = 0.5 * inv * d_dist - (2.0 / (CUTOFF * CUTOFF)) * slack * d_env
    gx = dx * inv + 2.0 * rx * d_squared
    gy = dy * inv + 2.0 * ry * d_squared
    gz = dz * inv + 2.0 * rz * d_squared
    rows4 = [gx, gy, gz, 0.5 * scaled * raw_energy]
    values = jnp.concatenate(rows4 + rows4, 0)
    rows = lax.broadcasted_iota(jnp.int32, (8, width), 0)
    flipped = jnp.where((rows & 3) == 3, values, -values)
    first = jnp.where(odd, 5, 0)

    def groups_of(side):
        return [2 + (first if side > 0 else 5 - first) + i for i in range(3)]

    neigh_high, center_high = placed[0][3:]
    groups = [0, 1, 2 + 3, 2 + 4] + groups_of(1) + (groups_of(-1) if count == 1 else [])
    terms = scatter(flipped[:, domain(0)], hot_t_ref[0], neigh_high, groups)
    center_terms = scatter(values[:, domain(0)], hot_t_ref[2], center_high, (0, 1))
    local_ref[...] = terms[0:16] + center_terms
    tiles = [terms[8 * i : 8 * i + 8] for i in range(2, len(groups))]
    if count == 2:
        terms = scatter(flipped[:, domain(1)], hot_t_ref[1], placed[1][3], groups_of(1))
        tiles += [terms[8 * i : 8 * i + 8] for i in range(3)]
    edge_near_ref[...] = tiles[3]
    edge_far_ref[...] = tiles[6]
    for j, (minus, plus) in enumerate(
        (
            (tiles[0], tiles[1]),
            (tiles[2], tiles[4]),
            (tiles[5], tiles[7]),
        )
    ):
        at = slice(8 * j, 8 * j + 8)
        back_far_ref[at] = jnp.where(even_n, plus, minus)
        back_near_ref[at] = jnp.where(even_n, minus, plus)


def list_rows(raw_ref):
    odd = lax.axis_index("outer") % 2 == 1
    low = raw_ref[LISTS : LISTS + 8].astype(jnp.int32)
    high = raw_ref[LISTS + 8 : LISTS + 16].astype(jnp.int32)
    wide = jnp.concatenate([low, high], 1)
    below, above = wide[0:3], wide[5:8]
    return jnp.where(odd, below, above), jnp.where(odd, above, below), wide[3:5]


def flat(ids):
    return jnp.concatenate([ids[i : i + 1] for i in range(ids.shape[0])], 1)


def spread_tile(tile):
    rows = lax.broadcasted_iota(jnp.int32, (8, LANES), 0)
    turned = pltpu.roll(tile, 4, 0)
    return [jnp.where(rows < 4, tile, turned), jnp.where(rows < 4, turned, tile)]


def hot_rows(ids):
    lanes = lax.broadcasted_iota(jnp.int32, (1, LANES), 1).astype(F32).astype(BF16)
    low = (ids & 127).astype(F32)
    return jnp.concatenate(
        [
            hits(down_lanes(low[:, i : i + LANES]), lanes)
            for i in range(0, ids.shape[1], LANES)
        ],
        0,
    )


def begin_kernel(
    local_ref, raw_ref, up_ref, low_ref, total_ref, hot_ref
):
    even_n = lax.axis_index("inner") % 2 == 0
    away, toward, along = list_rows(raw_ref)
    plus = jnp.where(even_n, low_ref[0:8], up_ref[0:8])
    minus = jnp.where(even_n, up_ref[0:8], low_ref[0:8])
    ids = flat(along)
    values = jnp.concatenate(spread_tile(minus) + spread_tile(plus), 1)
    total_ref[...] = local_ref[...] + scatter(values, hot_rows(ids), ids >> 7, (0, 1))
    hot_ref[...] = hot_rows(jnp.concatenate([flat(away), flat(toward)], 1))


def collect_kernel(
    total_ref,
    hot_ref,
    raw_ref,
    up_ref,
    low_ref,
    edge_far_ref,
    beside_ref,
    inside_ref,
    forces_ref,
    energy_ref,
):
    even_n = lax.axis_index("inner") % 2 == 0
    _, at_border = row_kind()
    plus = jnp.where(even_n, low_ref[16:24], up_ref[16:24])
    minus = jnp.where(even_n, up_ref[16:24], low_ref[16:24])
    over = jnp.concatenate([minus, edge_far_ref[...], plus], 0)
    toward = jnp.where(at_border, over, inside_ref[...])
    away = beside_ref[...]
    ids = list_rows(raw_ref)
    ids = jnp.concatenate([flat(ids[0]), flat(ids[1])], 1)
    values = []
    for tiles in (away, toward):
        for j in range(3):
            values += spread_tile(tiles[8 * j : 8 * j + 8])
    values = jnp.concatenate(values, 1)
    total = total_ref[...] + scatter(values, hot_ref[...], ids >> 7, (0, 1))
    for j in range(4):
        forces_ref[:, j * LANES : (j + 1) * LANES] = total[4 * j : 4 * j + 3]
        energy_ref[:, j * LANES : (j + 1) * LANES] = total[4 * j + 3 : 4 * j + 4]


def on_device(
    positions,
    species,
    send_lists,
    centers,
    neighbours,
    live_blocks,
    w_rad,
    emb_center,
    emb_neigh,
    w_env,
    w_lat,
    w_out,
):
    pair_len = centers.shape[0]
    atom_count = positions.shape[1]
    feat = w_env.shape[1] // 3
    lat = w_env.shape[0]
    chunks = pair_len // LANES

    def rows(count):
        return jax.ShapeDtypeStruct((count, LANES), F32)

    packed = pl.pallas_call(
        pack_kernel,
        out_shape=rows(PACKED),
        in_specs=[pl.BlockSpec(memory_space=pltpu.HBM)] * 5
        + [pl.BlockSpec(memory_space=pltpu.SMEM)],
        scratch_shapes=[
            pltpu.VMEM(positions.shape, F32),
            pltpu.VMEM((1, atom_count), jnp.int32),
            pltpu.VMEM(send_lists.shape, jnp.int32),
            pltpu.VMEM((chunks, LANES), jnp.int32),
            pltpu.VMEM((chunks, LANES), jnp.int32),
            pltpu.SemaphoreType.DMA((5,)),
        ],
        compiler_params=SMALL,
        name="pack_domain",
    )(
        *(
            pltpu.with_memory_space_constraint(value, pltpu.HBM)
            for value in (
                positions,
                species.reshape(1, atom_count),
                send_lists,
                centers.reshape(chunks, LANES),
                neighbours.reshape(chunks, LANES),
            )
        ),
        live_blocks,
    )
    weights = pl.pallas_call(
        weights_kernel,
        out_shape=[
            jax.ShapeDtypeStruct((64, lat), BF16),
            jax.ShapeDtypeStruct((w_env.shape[1], lat), BF16),
            jax.ShapeDtypeStruct(w_lat.shape, BF16),
            jax.ShapeDtypeStruct((16, lat), BF16),
        ],
        in_specs=[pl.BlockSpec(memory_space=pltpu.HBM)] * 3
        + [pl.BlockSpec(memory_space=pltpu.VMEM)] * 3,
        scratch_shapes=[pltpu.VMEM(w_rad.shape, F32), pltpu.SemaphoreType.DMA((3,))],
        compiler_params=SMALL,
        cost_estimate=pl.CostEstimate(flops=0, bytes_accessed=4_000_000, transcendentals=0),
        name="place_weights",
    )(
        *(
            pltpu.with_memory_space_constraint(value, pltpu.HBM)
            for value in (w_rad, w_env.T, w_lat)
        ),
        emb_center,
        emb_neigh,
        w_out.reshape(1, -1),
    )
    count = lax.axis_size("outer")
    half = count // 2
    low, high = half - 1, count - 1
    first = swap_outer(packed, 0, range(half))
    border = copy_rows(packed, {1: high, low - 1: half, half + 1: low, high - 1: 0})
    cross = swap_outer(packed, 1, range(count))
    last = swap_outer(packed, 0, range(half, count))
    far, near, mid, raw = pl.pallas_call(
        sends_kernel,
        out_shape=[
            rows(48),
            rows(48),
            rows(32),
            jax.ShapeDtypeStruct((2, PACKED, LANES), F32),
        ],
        compiler_params=SMALL,
        name="gather_sends",
    )(packed, first, border, cross, last, weights[3])
    up = swap_inner(far, 1)
    low = swap_inner(near, 0)
    down, hot_t = pl.pallas_call(
        columns_kernel,
        out_shape=[
            jax.ShapeDtypeStruct((2, pair_len, LANES), BF16),
            jax.ShapeDtypeStruct((3, pair_len, LANES), BF16),
        ],
        compiler_params=SMALL,
        cost_estimate=pl.CostEstimate(flops=0, bytes_accessed=4_000_000, transcendentals=0),
        name="pair_columns",
    )(raw)
    local, edge_near, edge_far, far, near = pl.pallas_call(
        lambda *refs: pair_kernel(feat, pair_len, *refs),
        out_shape=[rows(16), rows(8), rows(8), rows(24), rows(24)],
        scratch_shapes=[
            pltpu.VMEM((2, pair_len, pair_len), BF16),
            pltpu.VMEM((2, 9 * feat, pair_len), BF16),
            pltpu.VMEM((2, 9 * feat, pair_len), F32),
            pltpu.VMEM((2, 9 * feat, pair_len), F32),
        ],
        compiler_params=LARGE,
        name="pair_terms",
    )(raw, mid, up, low, down, hot_t, *weights)
    up = swap_inner(far, 1)
    low = swap_inner(near, 0)
    even_n = lax.axis_index("inner") % 2 == 0
    plus = jnp.where(even_n, low, up)
    minus = jnp.where(even_n, up, low)
    toward = jnp.concatenate([minus[16:24], edge_far, plus[16:24]], 0)
    away = jnp.concatenate([minus[8:16], edge_near, plus[8:16]], 0)
    inside = swap_outer(toward, 1, [o for o in range(count) if o % half not in (0, half - 1)])
    beside = swap_outer(away, 0, range(count))
    total, hot = pl.pallas_call(
        begin_kernel,
        out_shape=[rows(16), jax.ShapeDtypeStruct((6 * 2 * LANES, LANES), BF16)],
        compiler_params=SMALL,
        cost_estimate=pl.CostEstimate(flops=0, bytes_accessed=4_000_000, transcendentals=0),
        name="begin_terms",
    )(local, packed, up, low)
    forces, energy = pl.pallas_call(
        collect_kernel,
        out_shape=[
            jax.ShapeDtypeStruct((3, atom_count), F32),
            jax.ShapeDtypeStruct((1, atom_count), F32),
        ],
        compiler_params=SMALL,
        name="collect_terms",
    )(total, hot, packed, up, low, edge_far, beside, inside)
    return forces, energy.reshape(atom_count)


def solution(mesh):
    return jax.shard_map(
        on_device,
        mesh=mesh,
        in_specs=(
            P(None, AXES),
            P(AXES),
            P(None, AXES),
            P(AXES),
            P(AXES),
            P(AXES),
            P(),
            P(),
            P(),
            P(),
            P(),
            P(),
        ),
        out_specs=(P(None, AXES), P(AXES)),
        check_vma=False,
    )
```

```python
import math

import jax
import jax.numpy as jnp
from jax import lax
from jax.experimental import pallas as pl
from jax.experimental.pallas import tpu as pltpu
from jax.sharding import PartitionSpec as P

AXES = ("outer", "inner")
CUTOFF = 6.0
ROOT3 = math.sqrt(3.0)
ROOT5 = math.sqrt(5.0)
ROOT15 = math.sqrt(15.0)
LANES = 128
F32 = jnp.float32
BF16 = jnp.bfloat16
SMALL = pltpu.CompilerParams(vmem_limit_bytes=8 * 1024 * 1024)
LARGE = pltpu.CompilerParams(vmem_limit_bytes=32 * 1024 * 1024)
DIRS = ((-1, -1), (-1, 0), (-1, 1), (0, -1), (0, 1), (1, -1), (1, 0), (1, 1))
TABLE, LISTS, CENTERS, NEIGH, PACKED = 0, 16, 32, 40, 48
LIVE = 38
ORDER_OF = (0, 1, 1, 1, 2, 2, 2, 2, 2)


def permute(block, place):
    outer_len = lax.axis_size("outer")
    inner_len = lax.axis_size("inner")
    route = []
    for o in range(outer_len):
        for n in range(inner_len):
            there = place(o, n)
            if there is not None:
                to = there[0] % outer_len * inner_len + there[1] % inner_len
                route.append((o * inner_len + n, to))
    return lax.ppermute(block, AXES, route)


def swap_inner(block, parity):
    return permute(block, lambda o, n: (o, n + 1 if n % 2 == parity else n - 1))


def swap_outer(block, parity, rows):
    def place(o, n):
        return (o + 1 if o % 2 == parity else o - 1, n) if o in rows else None

    return permute(block, place)


def copy_rows(block, rows):
    return permute(block, lambda o, n: (rows[o], n) if o in rows else None)


def row_kind():
    half = lax.axis_size("outer") // 2
    row = lax.axis_index("outer")
    place = lax.rem(row, half)
    return row < half, (place == 0) | (place == half - 1)


def dot(lhs, rhs):
    return jnp.dot(lhs, rhs, preferred_element_type=F32)


def dot_rows(lhs, rhs):
    return lax.dot_general(lhs, rhs, (((0,), (0,)), ((), ())), preferred_element_type=F32)


def parts(value, count):
    out = []
    for _ in range(count):
        piece = value.astype(BF16)
        out.append(piece)
        value = value - piece.astype(F32)
    return out


def hits(left, right):
    return jnp.where(left == right, jnp.ones((), BF16), jnp.zeros((), BF16))


def down_lanes(row):
    return jnp.broadcast_to(row, (LANES, LANES)).T.astype(BF16)


def onehot_low(low_row):
    rows = lax.broadcasted_iota(jnp.int32, (LANES, low_row.shape[1]), 0).astype(F32).astype(BF16)
    return hits(rows, low_row.astype(F32).astype(BF16))


def high_mask(high_row, group):
    rows = lax.broadcasted_iota(jnp.int32, (8, high_row.shape[1]), 0)
    return high_row == 2 * group + jnp.where(rows >= 4, 1, 0)


def gather(table, low_hot, high_row):
    size = table.shape[0]
    found = dot(jnp.concatenate(parts(table, 3), 0), low_hot)
    found = found[0:size] + found[size : 2 * size] + found[2 * size :]
    total = None
    for group in range(size // 8):
        term = jnp.where(high_mask(high_row, group), found[8 * group : 8 * group + 8], 0.0)
        total = term if total is None else total + term
    return total + pltpu.roll(total, 4, 0)


def scatter(values, low_hot_t, high_row, groups):
    spread = [jnp.where(high_mask(high_row, group), values, 0.0) for group in groups]
    spread = jnp.concatenate(spread, 0)
    size = 8 * len(groups)
    summed = dot(jnp.concatenate(parts(spread, 2), 0), low_hot_t)
    return summed[0:size] + summed[size:]


def pack_kernel(
    pos_hbm,
    spec_hbm,
    lists_hbm,
    centers_hbm,
    neigh_hbm,
    live_ref,
    out_ref,
    pos,
    spec,
    lists,
    centers,
    neigh,
    sems,
):
    fetched = []
    for j, (src, dst) in enumerate(
        (
            (pos_hbm, pos),
            (spec_hbm, spec),
            (lists_hbm, lists),
            (centers_hbm, centers),
            (neigh_hbm, neigh),
        )
    ):
        copy = pltpu.make_async_copy(src, dst, sems.at[j])
        copy.start()
        fetched.append(copy)
    for copy in fetched:
        copy.wait()
    rows = []
    for j in range(4):
        at = slice(j * LANES, (j + 1) * LANES)
        rows.append(pos[:, at])
        rows.append(spec[:, at].astype(F32))
    ids = lists[...].astype(F32)
    rest = ids.shape[1] - LANES
    rows.append(ids[:, 0:LANES])
    rows.append(jnp.concatenate([ids[:, LANES:], jnp.zeros((8, LANES - rest), F32)], 1))
    rows.append(centers[...].astype(F32))
    rows.append(jnp.full((1, LANES), live_ref[0].astype(F32)))
    rows.append(jnp.zeros((1, LANES), F32))
    rows.append(neigh[...].astype(F32))
    rows.append(jnp.zeros((2, LANES), F32))
    out_ref[...] = jnp.concatenate(rows, 0)


def weights_kernel(
    w_rad_hbm,
    w_env_hbm,
    w_lat_hbm,
    emb_center_ref,
    emb_neigh_ref,
    w_out_in_ref,
    front_ref,
    w_env_ref,
    w_lat_ref,
    w_out_ref,
    w_rad,
    sems,
):
    fetched = []
    for j, (src, dst) in enumerate(
        ((w_rad_hbm, w_rad), (w_env_hbm, w_env_ref), (w_lat_hbm, w_lat_ref))
    ):
        copy = pltpu.make_async_copy(src, dst, sems.at[j])
        copy.start()
        fetched.append(copy)
    for copy in fetched:
        copy.wait()
    lat = w_lat_ref.shape[1]
    w1, w2, w3 = parts(w_rad[...], 3)
    none = jnp.zeros((1, lat), BF16)
    front_ref[...] = jnp.concatenate(
        [w1, w2, w1, w3, w2, w1, emb_center_ref[...], none, emb_neigh_ref[...], none], 0
    )
    w_lat_ref[lat:] = w_lat_ref[lat:] * jnp.full((), 2.0, BF16)
    w_out_ref[...] = jnp.broadcast_to(w_out_in_ref[...], (16, lat))


def tile_at(extra, side):
    return 8 * (3 * extra + 1 - side)


def tiles_of(raw, sides):
    odd = lax.axis_index("outer") % 2 == 1
    rows = lax.broadcasted_iota(jnp.int32, (8, LANES), 0)
    halves = [raw[LISTS + 8 * i : LISTS + 8 * i + 8].astype(jnp.int32) for i in range(2)]
    names, ids = [], []
    for side in sides:
        if side == 0:
            picked = [half[3:5] for half in halves]
            names += [(0, -1), (0, 1)]
        else:
            upper = odd if side > 0 else jnp.logical_not(odd)
            picked = [jnp.where(upper, half[5:8], half[0:3]) for half in halves]
            names += [(side, dy) for dy in (-1, 0, 1)]
        for i in range(picked[0].shape[0]):
            ids += [picked[0][i : i + 1], picked[1][i : i + 1]]
    ids = jnp.concatenate(ids, 1)
    taken = gather(raw[TABLE : TABLE + 16], onehot_low(ids & 127), ids >> 7)
    tiles = {}
    for j, name in enumerate(names):
        at = 2 * j * LANES
        tiles[name] = jnp.where(
            rows < 4, taken[:, at : at + LANES], taken[:, at + LANES : at + 2 * LANES]
        )
    return tiles


def names_of(sides):
    return [(side, dy) for side in sides for dy in ((-1, 1) if side == 0 else (-1, 0, 1))]


def early_kernel(own_ref, first_ref, border_ref, _, early_ref):
    at = 0
    for raw, sides in ((own_ref[...], (1, 0)), (first_ref[...], (1,)), (border_ref[...], (-1,))):
        tiles = tiles_of(raw, sides)
        for name in names_of(sides):
            early_ref[at : at + 8] = tiles[name]
            at += 8


def sends_kernel(
    early_ref, own_ref, cross_ref, last_ref, far_ref, near_ref, mid_ref, raw_ref
):
    even_n = lax.axis_index("inner") % 2 == 0
    cross = cross_ref[...]
    raw_ref[0] = own_ref[...]
    raw_ref[1] = cross
    made = []
    at = 0
    for sides in ((1, 0), (1,), (-1,)):
        tiles = {}
        for name in names_of(sides):
            tiles[name] = early_ref[at : at + 8]
            at += 8
        made.append(tiles)
    by_own, by_beside, by_border = made
    by_cross = tiles_of(cross, (0, -1))
    by_last = tiles_of(last_ref[...], (1,))
    low_half, _ = row_kind()
    by_beside = {n: jnp.where(low_half, by_beside[n], by_last[n]) for n in by_last}
    sources = ({1: by_beside, 0: by_own, -1: by_cross}, {1: by_own, 0: by_cross, -1: by_border})
    for extra in range(2):
        for side in (1, 0, -1):
            tiles = sources[extra][side]
            minus, plus = tiles[side, -1], tiles[side, 1]
            at = tile_at(extra, side)
            far_ref[at : at + 8] = jnp.where(even_n, minus, plus)
            near_ref[at : at + 8] = jnp.where(even_n, plus, minus)
            if side:
                m = 8 * (2 * extra + (1 - side) // 2)
                mid_ref[m : m + 8] = tiles[side, 0]


def silu_parts(pre):
    sig = 0.5 * jnp.tanh(0.5 * pre) + 0.5
    act = pre * sig
    return act, sig + act - act * sig


def half_turns(value):
    whole = jnp.floor(value + 0.5)
    rest = (value - whole) * math.pi
    sign = 1.0 - 2.0 * (whole - 2.0 * jnp.floor(whole * 0.5))
    r2 = rest * rest
    sine, cosine = -1.0 / 39916800, 1.0 / 479001600
    for term in (1.0 / 362880, -1.0 / 5040, 1.0 / 120, -1.0 / 6, 1.0):
        sine = term + r2 * sine
    for term in (-1.0 / 3628800, 1.0 / 40320, -1.0 / 720, 1.0 / 24, -0.5, 1.0):
        cosine = term + r2 * cosine
    return sign * rest * sine, sign * cosine


def neigh_place(tile):
    neigh = tile.astype(jnp.int32)
    ghost = neigh - 512
    listed = (ghost * 745) >> 17
    entry = ghost - 176 * listed
    is_local = neigh < 512
    low = jnp.where(is_local, neigh & 127, entry & 127)
    high = jnp.where(is_local, neigh >> 7, 4 + 2 * listed + (entry >> 7))
    return low, high


def columns_kernel(raw_ref, down_ref, hot_t_ref):
    lanes = lax.broadcasted_iota(jnp.int32, (1, LANES), 1).astype(F32).astype(BF16)
    for d in range(2):
        centers = raw_ref[d, CENTERS : CENTERS + 8]
        low, _ = neigh_place(raw_ref[d, NEIGH : NEIGH + 8])
        low = low.astype(F32)
        own_low = (centers.astype(jnp.int32) & 127).astype(F32)
        for i in range(down_ref.shape[1] // LANES):
            at = slice(i * LANES, (i + 1) * LANES)
            down_ref[d, at] = down_lanes(centers[i : i + 1] - 256.0)
            hot_t_ref[d, at] = hits(down_lanes(low[i : i + 1]), lanes)
            if d == 0:
                hot_t_ref[2, at] = hits(down_lanes(own_low[i : i + 1]), lanes)


def pair_kernel(feat, pair_len, *refs):
    _, two = row_kind()
    pl.when(two)(lambda: pair_body(2, feat, pair_len, *refs))
    pl.when(jnp.logical_not(two))(lambda: pair_body(1, feat, pair_len, *refs))


def pair_body(
    count,
    feat,
    pair_len,
    raw_ref,
    mid_ref,
    up_ref,
    low_ref,
    down_ref,
    hot_t_ref,
    front_ref,
    w_env_ref,
    w_lat_ref,
    w_out_ref,
    local_ref,
    edge_near_ref,
    edge_far_ref,
    back_far_ref,
    back_near_ref,
    same_ref,
    contrib_ref,
    gath_ref,
    back_ref,
):
    chunks = pair_len // LANES
    lat = w_lat_ref.shape[1]
    even_n = lax.axis_index("inner") % 2 == 0
    odd = lax.axis_index("outer") % 2 == 1
    front = front_ref[...]
    w_env = w_env_ref[...]
    w_lat = w_lat_ref[...]
    w_out = w_out_ref[...].astype(F32).T[:, 0:1]

    def as_row(tile):
        return jnp.concatenate([tile[i : i + 1] for i in range(chunks)], 1)

    def feat_rows(k):
        return slice(k * feat, (k + 1) * feat)

    def of_order(value, k):
        return value[feat_rows(ORDER_OF[k])]

    def domain(d):
        return slice(d * pair_len, (d + 1) * pair_len)

    def build_same(d):
        shifted = raw_ref[d, CENTERS : CENTERS + 8] - 256.0
        across = shifted.astype(BF16)
        for i in range(chunks):
            down = down_ref[d, i * LANES : (i + 1) * LANES]
            for j in range(chunks):
                same_ref[d, i * LANES : (i + 1) * LANES, j * LANES : (j + 1) * LANES] = hits(
                    down, across[j : j + 1]
                )

    def place(d):
        raw = raw_ref.at[d]
        centers = raw[CENTERS : CENTERS + 8]
        table = [raw[TABLE : TABLE + 16]]

        def ghost_tile(side, dy):
            if dy == 0:
                m = 8 * (2 * d + (1 - side) // 2)
                return mid_ref[m : m + 8]
            t = tile_at(d, side)
            by_low, by_up = low_ref[t : t + 8], up_ref[t : t + 8]
            return jnp.where(even_n, by_low, by_up) if dy < 0 else jnp.where(even_n, by_up, by_low)

        for dx, dy in DIRS:
            if dx == 0:
                table.append(ghost_tile(0, dy))
            else:
                table.append(jnp.where(odd, ghost_tile(dx, dy), ghost_tile(-dx, dy)))
        table = jnp.concatenate(table, 0)
        neigh_low, neigh_high = neigh_place(raw[NEIGH : NEIGH + 8])
        neigh_high = as_row(neigh_high)
        center_ids = as_row(centers.astype(jnp.int32))
        center_high = center_ids >> 7
        at_neigh = gather(table, onehot_low(as_row(neigh_low)), neigh_high)
        at_center = gather(table[0:16], onehot_low(center_ids & 127), center_high)
        block = lax.broadcasted_iota(jnp.int32, (1, pair_len), 1) // 128
        mask = jnp.where(block.astype(F32) < raw[LIVE : LIVE + 1, 0:1], 1.0, 0.0)
        return at_neigh, at_center, mask, neigh_high, center_high

    placed = [place(d) for d in range(count)]
    at_neigh, at_center, mask = (jnp.concatenate([p[i] for p in placed], 1) for i in range(3))
    width = mask.shape[1]
    moved = at_neigh - at_center
    rx, ry, rz = moved[0:1], moved[1:2], moved[2:3]
    squared = rx * rx + ry * ry + rz * rz + 1.0
    inv = lax.rsqrt(squared)
    dist = squared * inv
    ux, uy, uz = rx * inv, ry * inv, rz * inv
    slack = 1.0 - squared * (1.0 / (CUTOFF * CUTOFF))
    env = slack * slack
    scaled = env * mask
    ns = (lax.broadcasted_iota(jnp.int32, (8, width), 0) + 1).astype(F32)
    sine, cosine = half_turns(ns * (dist * (1.0 / CUTOFF)))
    scale = inv * env
    kinds = lax.broadcasted_iota(jnp.int32, (8, width), 0).astype(F32)
    hot_center = jnp.where(at_center[3:4] == kinds, 1.0, 0.0).astype(BF16)
    hot_neigh = jnp.where(at_neigh[3:4] == kinds, 1.0, 0.0).astype(BF16)
    b1, b2, b3 = parts(sine * scale, 3)
    pre = dot_rows(front, jnp.concatenate([b1, b1, b2, b1, b2, b3, hot_center, hot_neigh], 0))
    for d in range(count):
        build_same(d)
    latent, slope = silu_parts(pre)
    half = latent.astype(BF16)
    raw = dot(w_env, half)
    weight = raw * scaled
    shape = [
        None,
        ROOT3 * ux,
        ROOT3 * uy,
        ROOT3 * uz,
        ROOT15 * ux * uy,
        ROOT15 * uy * uz,
        0.5 * ROOT5 * (2.0 * uz * uz - ux * ux - uy * uy),
        ROOT15 * ux * uz,
        0.5 * ROOT15 * (ux * ux - uy * uy),
    ]
    shape_half = [None] + [row.astype(BF16) for row in shape[1:]]

    def spread_same(d, value, out_ref):
        at = domain(d)
        value = value[:, at]
        for k in range(9):
            rows = of_order(value, k)
            contrib_ref[d, feat_rows(k)] = (rows if k == 0 else rows * shape[k][:, at]).astype(BF16)
        out_ref[d] = dot(contrib_ref[d], same_ref[d])

    def gathered_sums(d, in_ref):
        at = domain(d)
        sums = [None, None, None]
        for k in range(9):
            term = in_ref[d, feat_rows(k)]
            if k:
                term = term * shape[k][:, at]
            order = ORDER_OF[k]
            sums[order] = term if sums[order] is None else sums[order] + term
        return jnp.concatenate(sums, 0)

    for d in range(count):
        spread_same(d, weight, gath_ref)
    sums = jnp.concatenate([gathered_sums(d, gath_ref) for d in range(count)], 1)
    joined = jnp.concatenate([half, (weight * sums).astype(BF16)], 0)
    update, slope2 = silu_parts(dot_rows(w_lat, joined))
    refined = (latent + update).astype(BF16)
    raw_energy = dot(w_out_ref[...], refined)[0:1]
    d_refined = scaled * w_out
    d_joined = dot(w_lat, (d_refined * slope2).astype(BF16))
    d_latent = d_refined + d_joined[:lat]
    d_inv = d_joined[lat:]
    d_weight = d_inv * sums
    d_sums = d_inv * weight
    for d in range(count):
        spread_same(d, d_sums, back_ref)
    d_order, d_shape = [], []
    for d in range(count):
        at = domain(d)
        d_order.append(gathered_sums(d, back_ref))
        here = []
        for k in range(1, 9):
            both = (
                of_order(d_sums, k)[:, at] * gath_ref[d, feat_rows(k)]
                + of_order(weight, k)[:, at] * back_ref[d, feat_rows(k)]
            )
            here.append(jnp.sum(both, axis=0, keepdims=True))
        d_shape.append(here)
    d_weight = d_weight + jnp.concatenate(d_order, 1)
    d_shape = [None] + [jnp.concatenate([here[k] for here in d_shape], 1) for k in range(8)]
    d_scaled = raw_energy + jnp.sum(d_weight * raw, axis=0, keepdims=True)
    d_latent = d_latent + scaled * dot_rows(w_env, d_weight.astype(BF16))
    d_pre = (d_latent * slope).astype(BF16)
    d_basis = dot(front_ref[0:16], d_pre)
    d_basis = d_basis[0:8] + d_basis[8:16]

    along = jnp.sum(d_basis * sine, axis=0, keepdims=True)
    turned = jnp.sum(d_basis * cosine * ns, axis=0, keepdims=True)
    d_env = along * inv + mask * d_scaled
    dx = (
        ROOT3 * d_shape[1]
        + ROOT15 * (uy * d_shape[4] + uz * d_shape[7] + ux * d_shape[8])
        - ROOT5 * ux * d_shape[6]
    )
    dy = (
        ROOT3 * d_shape[2]
        + ROOT15 * (ux * d_shape[4] + uz * d_shape[5] - uy * d_shape[8])
        - ROOT5 * uy * d_shape[6]
    )
    dz = (
        ROOT3 * d_shape[3]
        + ROOT15 * (uy * d_shape[5] + ux * d_shape[7])
        + 2.0 * ROOT5 * uz * d_shape[6]
    )
    d_inv = along * env + dx * rx + dy * ry + dz * rz
    d_dist = turned * (math.pi / CUTOFF) * scale - d_inv * inv * inv
    d_squared = 0.5 * inv * d_dist - (2.0 / (CUTOFF * CUTOFF)) * slack * d_env
    gx = dx * inv + 2.0 * rx * d_squared
    gy = dy * inv + 2.0 * ry * d_squared
    gz = dz * inv + 2.0 * rz * d_squared
    rows4 = [gx, gy, gz, 0.5 * scaled * raw_energy]
    values = jnp.concatenate(rows4 + rows4, 0)
    rows = lax.broadcasted_iota(jnp.int32, (8, width), 0)
    flipped = jnp.where((rows & 3) == 3, values, -values)
    first = jnp.where(odd, 5, 0)

    def groups_of(side):
        return [2 + (first if side > 0 else 5 - first) + i for i in range(3)]

    neigh_high, center_high = placed[0][3:]
    groups = [0, 1, 2 + 3, 2 + 4] + groups_of(1) + (groups_of(-1) if count == 1 else [])
    terms = scatter(flipped[:, domain(0)], hot_t_ref[0], neigh_high, groups)
    center_terms = scatter(values[:, domain(0)], hot_t_ref[2], center_high, (0, 1))
    local_ref[...] = terms[0:16] + center_terms
    tiles = [terms[8 * i : 8 * i + 8] for i in range(2, len(groups))]
    if count == 2:
        terms = scatter(flipped[:, domain(1)], hot_t_ref[1], placed[1][3], groups_of(1))
        tiles += [terms[8 * i : 8 * i + 8] for i in range(3)]
    edge_near_ref[...] = tiles[3]
    edge_far_ref[...] = tiles[6]
    for j, (minus, plus) in enumerate(
        (
            (tiles[0], tiles[1]),
            (tiles[2], tiles[4]),
            (tiles[5], tiles[7]),
        )
    ):
        at = slice(8 * j, 8 * j + 8)
        back_far_ref[at] = jnp.where(even_n, plus, minus)
        back_near_ref[at] = jnp.where(even_n, minus, plus)


def list_rows(raw_ref):
    odd = lax.axis_index("outer") % 2 == 1
    low = raw_ref[LISTS : LISTS + 8].astype(jnp.int32)
    high = raw_ref[LISTS + 8 : LISTS + 16].astype(jnp.int32)
    wide = jnp.concatenate([low, high], 1)
    below, above = wide[0:3], wide[5:8]
    return jnp.where(odd, below, above), jnp.where(odd, above, below), wide[3:5]


def flat(ids):
    return jnp.concatenate([ids[i : i + 1] for i in range(ids.shape[0])], 1)


def spread_tile(tile):
    rows = lax.broadcasted_iota(jnp.int32, (8, LANES), 0)
    turned = pltpu.roll(tile, 4, 0)
    return [jnp.where(rows < 4, tile, turned), jnp.where(rows < 4, turned, tile)]


def hot_rows(ids):
    lanes = lax.broadcasted_iota(jnp.int32, (1, LANES), 1).astype(F32).astype(BF16)
    low = (ids & 127).astype(F32)
    return jnp.concatenate(
        [
            hits(down_lanes(low[:, i : i + LANES]), lanes)
            for i in range(0, ids.shape[1], LANES)
        ],
        0,
    )


def begin_kernel(
    local_ref, raw_ref, up_ref, low_ref, total_ref, hot_ref
):
    even_n = lax.axis_index("inner") % 2 == 0
    away, toward, along = list_rows(raw_ref)
    plus = jnp.where(even_n, low_ref[0:8], up_ref[0:8])
    minus = jnp.where(even_n, up_ref[0:8], low_ref[0:8])
    ids = flat(along)
    values = jnp.concatenate(spread_tile(minus) + spread_tile(plus), 1)
    total_ref[...] = local_ref[...] + scatter(values, hot_rows(ids), ids >> 7, (0, 1))
    hot_ref[...] = hot_rows(jnp.concatenate([flat(away), flat(toward)], 1))


def collect_kernel(
    total_ref,
    hot_ref,
    raw_ref,
    up_ref,
    low_ref,
    edge_far_ref,
    beside_ref,
    inside_ref,
    forces_ref,
    energy_ref,
):
    even_n = lax.axis_index("inner") % 2 == 0
    _, at_border = row_kind()
    plus = jnp.where(even_n, low_ref[16:24], up_ref[16:24])
    minus = jnp.where(even_n, up_ref[16:24], low_ref[16:24])
    over = jnp.concatenate([minus, edge_far_ref[...], plus], 0)
    toward = jnp.where(at_border, over, inside_ref[...])
    away = beside_ref[...]
    ids = list_rows(raw_ref)
    ids = jnp.concatenate([flat(ids[0]), flat(ids[1])], 1)
    values = []
    for tiles in (away, toward):
        for j in range(3):
            values += spread_tile(tiles[8 * j : 8 * j + 8])
    values = jnp.concatenate(values, 1)
    total = total_ref[...] + scatter(values, hot_ref[...], ids >> 7, (0, 1))
    for j in range(4):
        forces_ref[:, j * LANES : (j + 1) * LANES] = total[4 * j : 4 * j + 3]
        energy_ref[:, j * LANES : (j + 1) * LANES] = total[4 * j + 3 : 4 * j + 4]


def on_device(
    positions,
    species,
    send_lists,
    centers,
    neighbours,
    live_blocks,
    w_rad,
    emb_center,
    emb_neigh,
    w_env,
    w_lat,
    w_out,
):
    pair_len = centers.shape[0]
    atom_count = positions.shape[1]
    feat = w_env.shape[1] // 3
    lat = w_env.shape[0]
    chunks = pair_len // LANES

    def rows(count):
        return jax.ShapeDtypeStruct((count, LANES), F32)

    packed = pl.pallas_call(
        pack_kernel,
        out_shape=rows(PACKED),
        in_specs=[pl.BlockSpec(memory_space=pltpu.HBM)] * 5
        + [pl.BlockSpec(memory_space=pltpu.SMEM)],
        scratch_shapes=[
            pltpu.VMEM(positions.shape, F32),
            pltpu.VMEM((1, atom_count), jnp.int32),
            pltpu.VMEM(send_lists.shape, jnp.int32),
            pltpu.VMEM((chunks, LANES), jnp.int32),
            pltpu.VMEM((chunks, LANES), jnp.int32),
            pltpu.SemaphoreType.DMA((5,)),
        ],
        compiler_params=SMALL,
        name="pack_domain",
    )(
        *(
            pltpu.with_memory_space_constraint(value, pltpu.HBM)
            for value in (
                positions,
                species.reshape(1, atom_count),
                send_lists,
                centers.reshape(chunks, LANES),
                neighbours.reshape(chunks, LANES),
            )
        ),
        live_blocks,
    )
    weights = pl.pallas_call(
        weights_kernel,
        out_shape=[
            jax.ShapeDtypeStruct((64, lat), BF16),
            jax.ShapeDtypeStruct((w_env.shape[1], lat), BF16),
            jax.ShapeDtypeStruct(w_lat.shape, BF16),
            jax.ShapeDtypeStruct((16, lat), BF16),
        ],
        in_specs=[pl.BlockSpec(memory_space=pltpu.HBM)] * 3
        + [pl.BlockSpec(memory_space=pltpu.VMEM)] * 3,
        scratch_shapes=[pltpu.VMEM(w_rad.shape, F32), pltpu.SemaphoreType.DMA((3,))],
        compiler_params=SMALL,
        cost_estimate=pl.CostEstimate(flops=0, bytes_accessed=4_000_000, transcendentals=0),
        name="place_weights",
    )(
        *(
            pltpu.with_memory_space_constraint(value, pltpu.HBM)
            for value in (w_rad, w_env.T, w_lat)
        ),
        emb_center,
        emb_neigh,
        w_out.reshape(1, -1),
    )
    count = lax.axis_size("outer")
    half = count // 2
    low, high = half - 1, count - 1
    first = swap_outer(packed, 0, range(half))
    border = copy_rows(packed, {1: high, low - 1: half, half + 1: low, high - 1: 0})
    cross = swap_outer(packed, 1, range(count))
    last = swap_outer(packed, 0, range(half, count))
    early = pl.pallas_call(
        early_kernel,
        out_shape=rows(88),
        compiler_params=SMALL,
        name="gather_early",
    )(packed, first, border, weights[3])
    far, near, mid, raw = pl.pallas_call(
        sends_kernel,
        out_shape=[
            rows(48),
            rows(48),
            rows(32),
            jax.ShapeDtypeStruct((2, PACKED, LANES), F32),
        ],
        compiler_params=SMALL,
        name="gather_sends",
    )(early, packed, cross, last)
    up = swap_inner(far, 1)
    low = swap_inner(near, 0)
    down, hot_t = pl.pallas_call(
        columns_kernel,
        out_shape=[
            jax.ShapeDtypeStruct((2, pair_len, LANES), BF16),
            jax.ShapeDtypeStruct((3, pair_len, LANES), BF16),
        ],
        compiler_params=SMALL,
        cost_estimate=pl.CostEstimate(flops=0, bytes_accessed=4_000_000, transcendentals=0),
        name="pair_columns",
    )(raw)
    local, edge_near, edge_far, far, near = pl.pallas_call(
        lambda *refs: pair_kernel(feat, pair_len, *refs),
        out_shape=[rows(16), rows(8), rows(8), rows(24), rows(24)],
        scratch_shapes=[
            pltpu.VMEM((2, pair_len, pair_len), BF16),
            pltpu.VMEM((2, 9 * feat, pair_len), BF16),
            pltpu.VMEM((2, 9 * feat, pair_len), F32),
            pltpu.VMEM((2, 9 * feat, pair_len), F32),
        ],
        compiler_params=LARGE,
        name="pair_terms",
    )(raw, mid, up, low, down, hot_t, *weights)
    up = swap_inner(far, 1)
    low = swap_inner(near, 0)
    even_n = lax.axis_index("inner") % 2 == 0
    plus = jnp.where(even_n, low, up)
    minus = jnp.where(even_n, up, low)
    toward = jnp.concatenate([minus[16:24], edge_far, plus[16:24]], 0)
    away = jnp.concatenate([minus[8:16], edge_near, plus[8:16]], 0)
    inside = swap_outer(toward, 1, [o for o in range(count) if o % half not in (0, half - 1)])
    beside = swap_outer(away, 0, range(count))
    total, hot = pl.pallas_call(
        begin_kernel,
        out_shape=[rows(16), jax.ShapeDtypeStruct((6 * 2 * LANES, LANES), BF16)],
        compiler_params=SMALL,
        cost_estimate=pl.CostEstimate(flops=0, bytes_accessed=4_000_000, transcendentals=0),
        name="begin_terms",
    )(local, packed, up, low)
    forces, energy = pl.pallas_call(
        collect_kernel,
        out_shape=[
            jax.ShapeDtypeStruct((3, atom_count), F32),
            jax.ShapeDtypeStruct((1, atom_count), F32),
        ],
        compiler_params=SMALL,
        name="collect_terms",
    )(total, hot, packed, up, low, edge_far, beside, inside)
    return forces, energy.reshape(atom_count)


def solution(mesh):
    return jax.shard_map(
        on_device,
        mesh=mesh,
        in_specs=(
            P(None, AXES),
            P(AXES),
            P(None, AXES),
            P(AXES),
            P(AXES),
            P(AXES),
            P(),
            P(),
            P(),
            P(),
            P(),
            P(),
        ),
        out_specs=(P(None, AXES), P(AXES)),
        check_vma=False,
    )
```

```python
import math

import jax
import jax.numpy as jnp
from jax import lax
from jax.experimental import pallas as pl
from jax.experimental.pallas import tpu as pltpu
from jax.sharding import PartitionSpec as P

AXES = ("outer", "inner")
CUTOFF = 6.0
ROOT3 = math.sqrt(3.0)
ROOT5 = math.sqrt(5.0)
ROOT15 = math.sqrt(15.0)
LANES = 128
F32 = jnp.float32
BF16 = jnp.bfloat16
SMALL = pltpu.CompilerParams(vmem_limit_bytes=8 * 1024 * 1024)
LARGE = pltpu.CompilerParams(vmem_limit_bytes=32 * 1024 * 1024)
DIRS = ((-1, -1), (-1, 0), (-1, 1), (0, -1), (0, 1), (1, -1), (1, 0), (1, 1))
TABLE, LISTS, CENTERS, NEIGH, PACKED = 0, 16, 32, 40, 48
LIVE = 38
ORDER_OF = (0, 1, 1, 1, 2, 2, 2, 2, 2)


def permute(block, place):
    outer_len = lax.axis_size("outer")
    inner_len = lax.axis_size("inner")
    route = []
    for o in range(outer_len):
        for n in range(inner_len):
            there = place(o, n)
            if there is not None:
                to = there[0] % outer_len * inner_len + there[1] % inner_len
                route.append((o * inner_len + n, to))
    return lax.ppermute(block, AXES, route)


def swap_inner(block, parity):
    return permute(block, lambda o, n: (o, n + 1 if n % 2 == parity else n - 1))


def swap_outer(block, parity, rows):
    def place(o, n):
        return (o + 1 if o % 2 == parity else o - 1, n) if o in rows else None

    return permute(block, place)


def copy_rows(block, rows):
    return permute(block, lambda o, n: (rows[o], n) if o in rows else None)


def row_kind():
    half = lax.axis_size("outer") // 2
    row = lax.axis_index("outer")
    place = lax.rem(row, half)
    return row < half, (place == 0) | (place == half - 1)


def dot(lhs, rhs):
    return jnp.dot(lhs, rhs, preferred_element_type=F32)


def dot_rows(lhs, rhs):
    return lax.dot_general(lhs, rhs, (((0,), (0,)), ((), ())), preferred_element_type=F32)


def parts(value, count):
    out = []
    for _ in range(count):
        piece = value.astype(BF16)
        out.append(piece)
        value = value - piece.astype(F32)
    return out


def hits(left, right):
    return jnp.where(left == right, jnp.ones((), BF16), jnp.zeros((), BF16))


def down_lanes(row):
    return jnp.broadcast_to(row, (LANES, LANES)).T.astype(BF16)


def onehot_low(low_row):
    rows = lax.broadcasted_iota(jnp.int32, (LANES, low_row.shape[1]), 0).astype(F32).astype(BF16)
    return hits(rows, low_row.astype(F32).astype(BF16))


def high_mask(high_row, group):
    rows = lax.broadcasted_iota(jnp.int32, (8, high_row.shape[1]), 0)
    return high_row == 2 * group + jnp.where(rows >= 4, 1, 0)


def gather(table, low_hot, high_row):
    size = table.shape[0]
    found = dot(jnp.concatenate(parts(table, 3), 0), low_hot)
    found = found[0:size] + found[size : 2 * size] + found[2 * size :]
    total = None
    for group in range(size // 8):
        term = jnp.where(high_mask(high_row, group), found[8 * group : 8 * group + 8], 0.0)
        total = term if total is None else total + term
    return total + pltpu.roll(total, 4, 0)


def scatter(values, low_hot_t, high_row, groups):
    spread = [jnp.where(high_mask(high_row, group), values, 0.0) for group in groups]
    spread = jnp.concatenate(spread, 0)
    size = 8 * len(groups)
    summed = dot(jnp.concatenate(parts(spread, 2), 0), low_hot_t)
    return summed[0:size] + summed[size:]


def pack_kernel(
    pos_hbm,
    spec_hbm,
    lists_hbm,
    centers_hbm,
    neigh_hbm,
    live_ref,
    out_ref,
    pos,
    spec,
    lists,
    centers,
    neigh,
    sems,
):
    fetched = []
    for j, (src, dst) in enumerate(
        (
            (pos_hbm, pos),
            (spec_hbm, spec),
            (lists_hbm, lists),
            (centers_hbm, centers),
            (neigh_hbm, neigh),
        )
    ):
        copy = pltpu.make_async_copy(src, dst, sems.at[j])
        copy.start()
        fetched.append(copy)
    for copy in fetched:
        copy.wait()
    rows = []
    for j in range(4):
        at = slice(j * LANES, (j + 1) * LANES)
        rows.append(pos[:, at])
        rows.append(spec[:, at].astype(F32))
    ids = lists[...].astype(F32)
    rest = ids.shape[1] - LANES
    rows.append(ids[:, 0:LANES])
    rows.append(jnp.concatenate([ids[:, LANES:], jnp.zeros((8, LANES - rest), F32)], 1))
    rows.append(centers[...].astype(F32))
    rows.append(jnp.full((1, LANES), live_ref[0].astype(F32)))
    rows.append(jnp.zeros((1, LANES), F32))
    rows.append(neigh[...].astype(F32))
    rows.append(jnp.zeros((2, LANES), F32))
    out_ref[...] = jnp.concatenate(rows, 0)


def weights_kernel(
    w_rad_hbm,
    w_env_hbm,
    w_lat_hbm,
    emb_center_ref,
    emb_neigh_ref,
    w_out_in_ref,
    front_ref,
    w_env_ref,
    w_lat_ref,
    w_out_ref,
    w_rad,
    sems,
):
    fetched = []
    for j, (src, dst) in enumerate(
        ((w_rad_hbm, w_rad), (w_env_hbm, w_env_ref), (w_lat_hbm, w_lat_ref))
    ):
        copy = pltpu.make_async_copy(src, dst, sems.at[j])
        copy.start()
        fetched.append(copy)
    for copy in fetched:
        copy.wait()
    lat = w_lat_ref.shape[1]
    w1, w2, w3 = parts(w_rad[...], 3)
    none = jnp.zeros((1, lat), BF16)
    front_ref[...] = jnp.concatenate(
        [w1, w2, w1, w3, w2, w1, emb_center_ref[...], none, emb_neigh_ref[...], none], 0
    )
    w_lat_ref[lat:] = w_lat_ref[lat:] * jnp.full((), 2.0, BF16)
    w_out_ref[...] = jnp.broadcast_to(w_out_in_ref[...], (16, lat))


def tile_at(extra, side):
    return 8 * (3 * extra + 1 - side)


def sends_kernel(
    own_ref, first_ref, border_ref, cross_ref, last_ref, _, far_ref, near_ref, mid_ref, raw_ref
):
    even_n = lax.axis_index("inner") % 2 == 0
    odd = lax.axis_index("outer") % 2 == 1
    low_half, _ = row_kind()
    rows = lax.broadcasted_iota(jnp.int32, (8, LANES), 0)
    own, cross = own_ref[...], cross_ref[...]
    beside = jnp.where(low_half, first_ref[...], last_ref[...])
    raw_ref[0] = own
    raw_ref[1] = cross

    def tiles_of(raw, sides):
        halves = [raw[LISTS + 8 * i : LISTS + 8 * i + 8].astype(jnp.int32) for i in range(2)]
        names, ids = [], []
        for side in sides:
            if side == 0:
                picked = [half[3:5] for half in halves]
                names += [(0, -1), (0, 1)]
            else:
                upper = odd if side > 0 else jnp.logical_not(odd)
                picked = [jnp.where(upper, half[5:8], half[0:3]) for half in halves]
                names += [(side, dy) for dy in (-1, 0, 1)]
            for i in range(picked[0].shape[0]):
                ids += [picked[0][i : i + 1], picked[1][i : i + 1]]
        ids = jnp.concatenate(ids, 1)
        taken = gather(raw[TABLE : TABLE + 16], onehot_low(ids & 127), ids >> 7)
        tiles = {}
        for j, name in enumerate(names):
            at = 2 * j * LANES
            tiles[name] = jnp.where(
                rows < 4, taken[:, at : at + LANES], taken[:, at + LANES : at + 2 * LANES]
            )
        return tiles

    by_own = tiles_of(own, (1, 0))
    by_cross = tiles_of(cross, (0, -1))
    by_beside = tiles_of(beside, (1,))
    by_border = tiles_of(border_ref[...], (-1,))
    sources = ({1: by_beside, 0: by_own, -1: by_cross}, {1: by_own, 0: by_cross, -1: by_border})
    for extra in range(2):
        for side in (1, 0, -1):
            tiles = sources[extra][side]
            minus, plus = tiles[side, -1], tiles[side, 1]
            at = tile_at(extra, side)
            far_ref[at : at + 8] = jnp.where(even_n, minus, plus)
            near_ref[at : at + 8] = jnp.where(even_n, plus, minus)
            if side:
                m = 8 * (2 * extra + (1 - side) // 2)
                mid_ref[m : m + 8] = tiles[side, 0]


def silu_parts(pre):
    sig = 0.5 * jnp.tanh(0.5 * pre) + 0.5
    act = pre * sig
    return act, sig + act - act * sig


def half_turns(value):
    whole = jnp.floor(value + 0.5)
    rest = (value - whole) * math.pi
    sign = 1.0 - 2.0 * (whole - 2.0 * jnp.floor(whole * 0.5))
    r2 = rest * rest
    sine, cosine = -1.0 / 39916800, 1.0 / 479001600
    for term in (1.0 / 362880, -1.0 / 5040, 1.0 / 120, -1.0 / 6, 1.0):
        sine = term + r2 * sine
    for term in (-1.0 / 3628800, 1.0 / 40320, -1.0 / 720, 1.0 / 24, -0.5, 1.0):
        cosine = term + r2 * cosine
    return sign * rest * sine, sign * cosine


def neigh_place(tile):
    neigh = tile.astype(jnp.int32)
    ghost = neigh - 512
    listed = (ghost * 745) >> 17
    entry = ghost - 176 * listed
    is_local = neigh < 512
    low = jnp.where(is_local, neigh & 127, entry & 127)
    high = jnp.where(is_local, neigh >> 7, 4 + 2 * listed + (entry >> 7))
    return low, high


def columns_kernel(raw_ref, down_ref, hot_t_ref):
    lanes = lax.broadcasted_iota(jnp.int32, (1, LANES), 1).astype(F32).astype(BF16)
    for d in range(2):
        centers = raw_ref[d, CENTERS : CENTERS + 8]
        low, _ = neigh_place(raw_ref[d, NEIGH : NEIGH + 8])
        low = low.astype(F32)
        own_low = (centers.astype(jnp.int32) & 127).astype(F32)
        for i in range(down_ref.shape[1] // LANES):
            at = slice(i * LANES, (i + 1) * LANES)
            down_ref[d, at] = down_lanes(centers[i : i + 1] - 256.0)
            hot_t_ref[d, at] = hits(down_lanes(low[i : i + 1]), lanes)
            if d == 0:
                hot_t_ref[2, at] = hits(down_lanes(own_low[i : i + 1]), lanes)


def pair_kernel(feat, pair_len, *refs):
    _, two = row_kind()
    pl.when(two)(lambda: pair_body(2, feat, pair_len, *refs))
    pl.when(jnp.logical_not(two))(lambda: pair_body(1, feat, pair_len, *refs))


def pair_body(
    count,
    feat,
    pair_len,
    raw_ref,
    mid_ref,
    up_ref,
    low_ref,
    down_ref,
    hot_t_ref,
    front_ref,
    w_env_ref,
    w_lat_ref,
    w_out_ref,
    local_ref,
    edge_near_ref,
    edge_far_ref,
    back_far_ref,
    back_near_ref,
    same_ref,
    contrib_ref,
    gath_ref,
    back_ref,
):
    chunks = pair_len // LANES
    lat = w_lat_ref.shape[1]
    even_n = lax.axis_index("inner") % 2 == 0
    odd = lax.axis_index("outer") % 2 == 1
    front = front_ref[...]
    w_env = w_env_ref[...]
    w_lat = w_lat_ref[...]
    w_out = w_out_ref[...].astype(F32).T[:, 0:1]

    def as_row(tile):
        return jnp.concatenate([tile[i : i + 1] for i in range(chunks)], 1)

    def feat_rows(k):
        return slice(k * feat, (k + 1) * feat)

    def of_order(value, k):
        return value[feat_rows(ORDER_OF[k])]

    def domain(d):
        return slice(d * pair_len, (d + 1) * pair_len)

    def build_same(d):
        shifted = raw_ref[d, CENTERS : CENTERS + 8] - 256.0
        across = shifted.astype(BF16)
        for i in range(chunks):
            down = down_ref[d, i * LANES : (i + 1) * LANES]
            for j in range(chunks):
                same_ref[d, i * LANES : (i + 1) * LANES, j * LANES : (j + 1) * LANES] = hits(
                    down, across[j : j + 1]
                )

    def place(d):
        raw = raw_ref.at[d]
        centers = raw[CENTERS : CENTERS + 8]
        table = [raw[TABLE : TABLE + 16]]

        def ghost_tile(side, dy):
            if dy == 0:
                m = 8 * (2 * d + (1 - side) // 2)
                return mid_ref[m : m + 8]
            t = tile_at(d, side)
            by_low, by_up = low_ref[t : t + 8], up_ref[t : t + 8]
            return jnp.where(even_n, by_low, by_up) if dy < 0 else jnp.where(even_n, by_up, by_low)

        for dx, dy in DIRS:
            if dx == 0:
                table.append(ghost_tile(0, dy))
            else:
                table.append(jnp.where(odd, ghost_tile(dx, dy), ghost_tile(-dx, dy)))
        table = jnp.concatenate(table, 0)
        neigh_low, neigh_high = neigh_place(raw[NEIGH : NEIGH + 8])
        neigh_high = as_row(neigh_high)
        center_ids = as_row(centers.astype(jnp.int32))
        center_high = center_ids >> 7
        at_neigh = gather(table, onehot_low(as_row(neigh_low)), neigh_high)
        at_center = gather(table[0:16], onehot_low(center_ids & 127), center_high)
        block = lax.broadcasted_iota(jnp.int32, (1, pair_len), 1) // 128
        mask = jnp.where(block.astype(F32) < raw[LIVE : LIVE + 1, 0:1], 1.0, 0.0)
        return at_neigh, at_center, mask, neigh_high, center_high

    placed = [place(d) for d in range(count)]
    at_neigh, at_center, mask = (jnp.concatenate([p[i] for p in placed], 1) for i in range(3))
    width = mask.shape[1]
    moved = at_neigh - at_center
    rx, ry, rz = moved[0:1], moved[1:2], moved[2:3]
    squared = rx * rx + ry * ry + rz * rz + 1.0
    inv = lax.rsqrt(squared)
    dist = squared * inv
    ux, uy, uz = rx * inv, ry * inv, rz * inv
    slack = 1.0 - squared * (1.0 / (CUTOFF * CUTOFF))
    env = slack * slack
    scaled = env * mask
    ns = (lax.broadcasted_iota(jnp.int32, (8, width), 0) + 1).astype(F32)
    sine, cosine = half_turns(ns * (dist * (1.0 / CUTOFF)))
    scale = inv * env
    kinds = lax.broadcasted_iota(jnp.int32, (8, width), 0).astype(F32)
    hot_center = jnp.where(at_center[3:4] == kinds, 1.0, 0.0).astype(BF16)
    hot_neigh = jnp.where(at_neigh[3:4] == kinds, 1.0, 0.0).astype(BF16)
    b1, b2, b3 = parts(sine * scale, 3)
    pre = dot_rows(front, jnp.concatenate([b1, b1, b2, b1, b2, b3, hot_center, hot_neigh], 0))
    for d in range(count):
        build_same(d)
    latent, slope = silu_parts(pre)
    half = latent.astype(BF16)
    raw = dot(w_env, half)
    weight = raw * scaled
    shape = [
        None,
        ROOT3 * ux,
        ROOT3 * uy,
        ROOT3 * uz,
        ROOT15 * ux * uy,
        ROOT15 * uy * uz,
        0.5 * ROOT5 * (2.0 * uz * uz - ux * ux - uy * uy),
        ROOT15 * ux * uz,
        0.5 * ROOT15 * (ux * ux - uy * uy),
    ]
    shape_half = [None] + [row.astype(BF16) for row in shape[1:]]

    def spread_same(d, value, out_ref):
        at = domain(d)
        value = value[:, at].astype(BF16)
        for k in range(9):
            rows = of_order(value, k)
            contrib_ref[d, feat_rows(k)] = rows if k == 0 else rows * shape_half[k][:, at]
        out_ref[d] = dot(contrib_ref[d], same_ref[d])

    def gathered_sums(d, in_ref):
        at = domain(d)
        sums = [None, None, None]
        for k in range(9):
            term = in_ref[d, feat_rows(k)]
            if k:
                term = term * shape[k][:, at]
            order = ORDER_OF[k]
            sums[order] = term if sums[order] is None else sums[order] + term
        return jnp.concatenate(sums, 0)

    for d in range(count):
        spread_same(d, weight, gath_ref)
    sums = jnp.concatenate([gathered_sums(d, gath_ref) for d in range(count)], 1)
    joined = jnp.concatenate([half, (weight * sums).astype(BF16)], 0)
    update, slope2 = silu_parts(dot_rows(w_lat, joined))
    refined = (latent + update).astype(BF16)
    raw_energy = dot(w_out_ref[...], refined)[0:1]
    d_refined = scaled * w_out
    d_joined = dot(w_lat, (d_refined * slope2).astype(BF16))
    d_latent = d_refined + d_joined[:lat]
    d_inv = d_joined[lat:]
    d_weight = d_inv * sums
    d_sums = d_inv * weight
    for d in range(count):
        spread_same(d, d_sums, back_ref)
    d_order, d_shape = [], []
    for d in range(count):
        at = domain(d)
        d_order.append(gathered_sums(d, back_ref))
        here = []
        for k in range(1, 9):
            both = (
                of_order(d_sums, k)[:, at] * gath_ref[d, feat_rows(k)]
                + of_order(weight, k)[:, at] * back_ref[d, feat_rows(k)]
            )
            here.append(jnp.sum(both, axis=0, keepdims=True))
        d_shape.append(here)
    d_weight = d_weight + jnp.concatenate(d_order, 1)
    d_shape = [None] + [jnp.concatenate([here[k] for here in d_shape], 1) for k in range(8)]
    d_scaled = raw_energy + jnp.sum(d_weight * raw, axis=0, keepdims=True)
    d_latent = d_latent + scaled * dot_rows(w_env, d_weight.astype(BF16))
    d_pre = (d_latent * slope).astype(BF16)
    d_basis = dot(front_ref[0:16], d_pre)
    d_basis = d_basis[0:8] + d_basis[8:16]

    along = jnp.sum(d_basis * sine, axis=0, keepdims=True)
    turned = jnp.sum(d_basis * cosine * ns, axis=0, keepdims=True)
    d_env = along * inv + mask * d_scaled
    dx = (
        ROOT3 * d_shape[1]
        + ROOT15 * (uy * d_shape[4] + uz * d_shape[7] + ux * d_shape[8])
        - ROOT5 * ux * d_shape[6]
    )
    dy = (
        ROOT3 * d_shape[2]
        + ROOT15 * (ux * d_shape[4] + uz * d_shape[5] - uy * d_shape[8])
        - ROOT5 * uy * d_shape[6]
    )
    dz = (
        ROOT3 * d_shape[3]
        + ROOT15 * (uy * d_shape[5] + ux * d_shape[7])
        + 2.0 * ROOT5 * uz * d_shape[6]
    )
    d_inv = along * env + dx * rx + dy * ry + dz * rz
    d_dist = turned * (math.pi / CUTOFF) * scale - d_inv * inv * inv
    d_squared = 0.5 * inv * d_dist - (2.0 / (CUTOFF * CUTOFF)) * slack * d_env
    gx = dx * inv + 2.0 * rx * d_squared
    gy = dy * inv + 2.0 * ry * d_squared
    gz = dz * inv + 2.0 * rz * d_squared
    rows4 = [gx, gy, gz, 0.5 * scaled * raw_energy]
    values = jnp.concatenate(rows4 + rows4, 0)
    rows = lax.broadcasted_iota(jnp.int32, (8, width), 0)
    flipped = jnp.where((rows & 3) == 3, values, -values)
    first = jnp.where(odd, 5, 0)

    def groups_of(side):
        return [2 + (first if side > 0 else 5 - first) + i for i in range(3)]

    neigh_high, center_high = placed[0][3:]
    groups = [0, 1, 2 + 3, 2 + 4] + groups_of(1) + (groups_of(-1) if count == 1 else [])
    terms = scatter(flipped[:, domain(0)], hot_t_ref[0], neigh_high, groups)
    center_terms = scatter(values[:, domain(0)], hot_t_ref[2], center_high, (0, 1))
    local_ref[...] = terms[0:16] + center_terms
    tiles = [terms[8 * i : 8 * i + 8] for i in range(2, len(groups))]
    if count == 2:
        terms = scatter(flipped[:, domain(1)], hot_t_ref[1], placed[1][3], groups_of(1))
        tiles += [terms[8 * i : 8 * i + 8] for i in range(3)]
    edge_near_ref[...] = tiles[3]
    edge_far_ref[...] = tiles[6]
    for j, (minus, plus) in enumerate(
        (
            (tiles[0], tiles[1]),
            (tiles[2], tiles[4]),
            (tiles[5], tiles[7]),
        )
    ):
        at = slice(8 * j, 8 * j + 8)
        back_far_ref[at] = jnp.where(even_n, plus, minus)
        back_near_ref[at] = jnp.where(even_n, minus, plus)


def list_rows(raw_ref):
    odd = lax.axis_index("outer") % 2 == 1
    low = raw_ref[LISTS : LISTS + 8].astype(jnp.int32)
    high = raw_ref[LISTS + 8 : LISTS + 16].astype(jnp.int32)
    wide = jnp.concatenate([low, high], 1)
    below, above = wide[0:3], wide[5:8]
    return jnp.where(odd, below, above), jnp.where(odd, above, below), wide[3:5]


def flat(ids):
    return jnp.concatenate([ids[i : i + 1] for i in range(ids.shape[0])], 1)


def spread_tile(tile):
    rows = lax.broadcasted_iota(jnp.int32, (8, LANES), 0)
    turned = pltpu.roll(tile, 4, 0)
    return [jnp.where(rows < 4, tile, turned), jnp.where(rows < 4, turned, tile)]


def hot_rows(ids):
    lanes = lax.broadcasted_iota(jnp.int32, (1, LANES), 1).astype(F32).astype(BF16)
    low = (ids & 127).astype(F32)
    return jnp.concatenate(
        [
            hits(down_lanes(low[:, i : i + LANES]), lanes)
            for i in range(0, ids.shape[1], LANES)
        ],
        0,
    )


def begin_kernel(
    local_ref, raw_ref, up_ref, low_ref, total_ref, hot_ref
):
    even_n = lax.axis_index("inner") % 2 == 0
    away, toward, along = list_rows(raw_ref)
    plus = jnp.where(even_n, low_ref[0:8], up_ref[0:8])
    minus = jnp.where(even_n, up_ref[0:8], low_ref[0:8])
    ids = flat(along)
    values = jnp.concatenate(spread_tile(minus) + spread_tile(plus), 1)
    total_ref[...] = local_ref[...] + scatter(values, hot_rows(ids), ids >> 7, (0, 1))
    hot_ref[...] = hot_rows(jnp.concatenate([flat(away), flat(toward)], 1))


def collect_kernel(
    total_ref,
    hot_ref,
    raw_ref,
    up_ref,
    low_ref,
    edge_far_ref,
    beside_ref,
    inside_ref,
    forces_ref,
    energy_ref,
):
    even_n = lax.axis_index("inner") % 2 == 0
    _, at_border = row_kind()
    plus = jnp.where(even_n, low_ref[16:24], up_ref[16:24])
    minus = jnp.where(even_n, up_ref[16:24], low_ref[16:24])
    over = jnp.concatenate([minus, edge_far_ref[...], plus], 0)
    toward = jnp.where(at_border, over, inside_ref[...])
    away = beside_ref[...]
    ids = list_rows(raw_ref)
    ids = jnp.concatenate([flat(ids[0]), flat(ids[1])], 1)
    values = []
    for tiles in (away, toward):
        for j in range(3):
            values += spread_tile(tiles[8 * j : 8 * j + 8])
    values = jnp.concatenate(values, 1)
    total = total_ref[...] + scatter(values, hot_ref[...], ids >> 7, (0, 1))
    for j in range(4):
        forces_ref[:, j * LANES : (j + 1) * LANES] = total[4 * j : 4 * j + 3]
        energy_ref[:, j * LANES : (j + 1) * LANES] = total[4 * j + 3 : 4 * j + 4]


def on_device(
    positions,
    species,
    send_lists,
    centers,
    neighbours,
    live_blocks,
    w_rad,
    emb_center,
    emb_neigh,
    w_env,
    w_lat,
    w_out,
):
    pair_len = centers.shape[0]
    atom_count = positions.shape[1]
    feat = w_env.shape[1] // 3
    lat = w_env.shape[0]
    chunks = pair_len // LANES

    def rows(count):
        return jax.ShapeDtypeStruct((count, LANES), F32)

    packed = pl.pallas_call(
        pack_kernel,
        out_shape=rows(PACKED),
        in_specs=[pl.BlockSpec(memory_space=pltpu.HBM)] * 5
        + [pl.BlockSpec(memory_space=pltpu.SMEM)],
        scratch_shapes=[
            pltpu.VMEM(positions.shape, F32),
            pltpu.VMEM((1, atom_count), jnp.int32),
            pltpu.VMEM(send_lists.shape, jnp.int32),
            pltpu.VMEM((chunks, LANES), jnp.int32),
            pltpu.VMEM((chunks, LANES), jnp.int32),
            pltpu.SemaphoreType.DMA((5,)),
        ],
        compiler_params=SMALL,
        name="pack_domain",
    )(
        *(
            pltpu.with_memory_space_constraint(value, pltpu.HBM)
            for value in (
                positions,
                species.reshape(1, atom_count),
                send_lists,
                centers.reshape(chunks, LANES),
                neighbours.reshape(chunks, LANES),
            )
        ),
        live_blocks,
    )
    weights = pl.pallas_call(
        weights_kernel,
        out_shape=[
            jax.ShapeDtypeStruct((64, lat), BF16),
            jax.ShapeDtypeStruct((w_env.shape[1], lat), BF16),
            jax.ShapeDtypeStruct(w_lat.shape, BF16),
            jax.ShapeDtypeStruct((16, lat), BF16),
        ],
        in_specs=[pl.BlockSpec(memory_space=pltpu.HBM)] * 3
        + [pl.BlockSpec(memory_space=pltpu.VMEM)] * 3,
        scratch_shapes=[pltpu.VMEM(w_rad.shape, F32), pltpu.SemaphoreType.DMA((3,))],
        compiler_params=SMALL,
        cost_estimate=pl.CostEstimate(flops=0, bytes_accessed=4_000_000, transcendentals=0),
        name="place_weights",
    )(
        *(
            pltpu.with_memory_space_constraint(value, pltpu.HBM)
            for value in (w_rad, w_env.T, w_lat)
        ),
        emb_center,
        emb_neigh,
        w_out.reshape(1, -1),
    )
    count = lax.axis_size("outer")
    half = count // 2
    low, high = half - 1, count - 1
    first = swap_outer(packed, 0, range(half))
    border = copy_rows(packed, {1: high, low - 1: half, half + 1: low, high - 1: 0})
    cross = swap_outer(packed, 1, range(count))
    last = swap_outer(packed, 0, range(half, count))
    far, near, mid, raw = pl.pallas_call(
        sends_kernel,
        out_shape=[
            rows(48),
            rows(48),
            rows(32),
            jax.ShapeDtypeStruct((2, PACKED, LANES), F32),
        ],
        compiler_params=SMALL,
        name="gather_sends",
    )(packed, first, border, cross, last, weights[3])
    up = swap_inner(far, 1)
    low = swap_inner(near, 0)
    down, hot_t = pl.pallas_call(
        columns_kernel,
        out_shape=[
            jax.ShapeDtypeStruct((2, pair_len, LANES), BF16),
            jax.ShapeDtypeStruct((3, pair_len, LANES), BF16),
        ],
        compiler_params=SMALL,
        cost_estimate=pl.CostEstimate(flops=0, bytes_accessed=4_000_000, transcendentals=0),
        name="pair_columns",
    )(raw)
    local, edge_near, edge_far, far, near = pl.pallas_call(
        lambda *refs: pair_kernel(feat, pair_len, *refs),
        out_shape=[rows(16), rows(8), rows(8), rows(24), rows(24)],
        scratch_shapes=[
            pltpu.VMEM((2, pair_len, pair_len), BF16),
            pltpu.VMEM((2, 9 * feat, pair_len), BF16),
            pltpu.VMEM((2, 9 * feat, pair_len), F32),
            pltpu.VMEM((2, 9 * feat, pair_len), F32),
        ],
        compiler_params=LARGE,
        name="pair_terms",
    )(raw, mid, up, low, down, hot_t, *weights)
    up = swap_inner(far, 1)
    low = swap_inner(near, 0)
    even_n = lax.axis_index("inner") % 2 == 0
    plus = jnp.where(even_n, low, up)
    minus = jnp.where(even_n, up, low)
    toward = jnp.concatenate([minus[16:24], edge_far, plus[16:24]], 0)
    away = jnp.concatenate([minus[8:16], edge_near, plus[8:16]], 0)
    inside = swap_outer(toward, 1, [o for o in range(count) if o % half not in (0, half - 1)])
    beside = swap_outer(away, 0, range(count))
    total, hot = pl.pallas_call(
        begin_kernel,
        out_shape=[rows(16), jax.ShapeDtypeStruct((6 * 2 * LANES, LANES), BF16)],
        compiler_params=SMALL,
        cost_estimate=pl.CostEstimate(flops=0, bytes_accessed=4_000_000, transcendentals=0),
        name="begin_terms",
    )(local, packed, up, low)
    forces, energy = pl.pallas_call(
        collect_kernel,
        out_shape=[
            jax.ShapeDtypeStruct((3, atom_count), F32),
            jax.ShapeDtypeStruct((1, atom_count), F32),
        ],
        compiler_params=SMALL,
        name="collect_terms",
    )(total, hot, packed, up, low, edge_far, beside, inside)
    return forces, energy.reshape(atom_count)


def solution(mesh):
    return jax.shard_map(
        on_device,
        mesh=mesh,
        in_specs=(
            P(None, AXES),
            P(AXES),
            P(None, AXES),
            P(AXES),
            P(AXES),
            P(AXES),
            P(),
            P(),
            P(),
            P(),
            P(),
            P(),
        ),
        out_specs=(P(None, AXES), P(AXES)),
        check_vma=False,
    )
```
